32 devices in a mesh: groups: 2 (over y), seq: 8 (over z, core), head: 2 (over x).
Axes of the slice: x: 2, y: 2, z: 4, core: 2. Of those that a mesh axis runs over, the one named last changes fastest.
Arguments:
- history: bfloat16 [16384, 1024], P(('groups', 'seq')), parts along dimension 0, may hold values from -32 to 32
- qkv_weight: bfloat16 [3, 1024, 1024], P(None, None, 'head'), may hold values from -0.1875 to 0.1875
- out_weight: bfloat16 [1024, 1024], P('head'), may hold values from -0.1875 to 0.1875
- rand_blocks: int32 [16, 256, 3], P('head', ('groups', 'seq')), parts along dimension 1, may hold values from 0 to 127, as said below
Outputs:
- attended: bfloat16 [16384, 1024], P(('groups', 'seq', 'head')), parts along dimension 0
The draws below stay inside these ranges and needn't reach their ends.
There are 2 independent parts, one for each index of `groups`. The reference program is written for one: setup_inputs(seed, part) draws one part's arguments, and reference() takes and returns one part's arrays. A program takes and returns all parts, laid end to end along the dimension named above; an argument that names none is the same for every part. Nothing has to cross between parts.
Inputs may be any that keep to these rules, and one draw needn't show every extreme that they name: `rand_blocks`: entry [h, j, r] is a block of the history. For each head and each aligned run of 16 query blocks, the 48 named blocks take at most 7 from any one aligned run of 16 key blocks, and exactly 7 from at least one such run. Entries of global query blocks are not read.
All inputs are finite; a program needn't handle non-finite values.
Results may differ from the reference program's by a relative error of at most 0.028.
The reference program's roundings to bfloat16 on the way count: a program that leaves them out, or rounds other values in their place, can miss the bound.
Values may be sent and summed in bfloat16 or wider, within the bound.
No kernel may reach another device: no remote copies, remote signals or barrier semaphores. Data moves between devices by JAX's collectives and lax.ppermute only.
A program may use at most 128 MiB of HBM per device.

```python
import math
import jax
import jax.numpy as jnp
from jax import lax

D = 1024
H = 16
B = 64
R = 3
G = 1024
TOK_DEV = 1024
HD = 64
TOKENS = 8192
BLOCKS = 128
BLOCKS_DEV = 16
GBLOCKS = 16
CAP = 7
N_SEQ = 8


def draw_history(key, part):
    key = jax.random.fold_in(key, 3)
    values = jnp.clip(jax.random.normal(key, (TOKENS, D), jnp.float32), -4.0, 4.0)
    return values.astype(jnp.bfloat16)


def draw_rand_blocks(key, part):
    key = jax.random.fold_in(key, 11)
    devices = BLOCKS // BLOCKS_DEV
    request_count = BLOCKS_DEV * R
    slot_count = devices * CAP
    keys_all = jax.random.split(key, H * devices)

    def one_list(sub_key):
        star_key, perm_key, shuffle_key, local_key = jax.random.split(sub_key, 4)
        star_dev = jax.random.randint(star_key, (), 0, devices)
        base_slots = jax.random.permutation(perm_key, slot_count)
        positions = jnp.arange(slot_count, dtype=jnp.int32)
        scores = jnp.where(base_slots // CAP == star_dev, positions - slot_count, positions)
        chosen = base_slots[jnp.argsort(scores)][:request_count]
        chosen = jax.random.permutation(shuffle_key, chosen)
        local_blocks = jax.random.randint(local_key, (request_count,), 0, BLOCKS_DEV)
        return (chosen // CAP * BLOCKS_DEV + local_blocks).astype(jnp.int32).reshape(BLOCKS_DEV, R)
    lists = jax.vmap(one_list)(keys_all)
    return lists.reshape(H, devices * BLOCKS_DEV, R)


def steps_of(rng, dims, cuts, smallest, largest):
    def one(axis_at, parts):
        heights = jax.random.uniform(jax.random.fold_in(jax.random.fold_in(rng, 6), axis_at), (parts,), jnp.float32, smallest / len(cuts), largest / len(cuts))
        return jnp.repeat(jnp.exp(heights), dims[axis_at] // parts).reshape((-1,) + (1,) * (len(dims) - axis_at - 1))

    gain = one(*cuts[0])
    for cut in cuts[1:]:
        gain = gain * one(*cut)
    return gain


def normal_values(own_key, extent, spread, bound, pieces=(), kind=jnp.bfloat16):
    factor_of = steps_of(own_key, extent, pieces, -0.22, 0.18) if pieces else 1.0
    drawn = jax.random.normal(own_key, extent, jnp.float32) * spread * factor_of
    return jnp.minimum(jnp.maximum(drawn, -bound), bound).astype(kind)


def setup_inputs(seed: int = 0, part: int = 0) -> dict:
    arg_keys = jax.random.split(jax.random.key(seed), 5)
    own_keys = jax.random.split(jax.random.fold_in(arg_keys[4], part), 5)
    return {
        "history": draw_history(jax.random.fold_in(jax.random.fold_in(arg_keys[4], part), 71), part),
        "qkv_weight": normal_values(arg_keys[1], (3, D, H * HD), D ** -0.5, 0.1875, ((2, 2),)),
        "out_weight": normal_values(arg_keys[2], (H * HD, D), (H * HD) ** -0.5, 0.1875, ((0, 2),)),
        "rand_blocks": draw_rand_blocks(jax.random.fold_in(jax.random.fold_in(arg_keys[4], part), 71), part),
    }


masked_score = -1e+30

def attend_blocks(queries, glob_keys, glob_values, near_keys, near_values, block_ids):
    score_scale = 1.0 / math.sqrt(HD)
    highest = lax.Precision.HIGHEST
    query_f32 = queries.astype(jnp.float32)
    score_glob = jnp.einsum('nqd,kd->nqk', query_f32, glob_keys.astype(jnp.float32), precision=highest) * score_scale
    score_near = jnp.einsum('nqd,nkd->nqk', query_f32, near_keys.astype(jnp.float32), precision=highest) * score_scale
    window_ids = block_ids[:, None] + jnp.arange(3, dtype=jnp.int32)[None, :] - 1
    window_ok = (window_ids >= GBLOCKS) & (window_ids < BLOCKS)
    keep_cols = jnp.concatenate([jnp.repeat(window_ok, B, axis=1), jnp.ones((block_ids.shape[0], R * B), dtype=bool)], axis=1)
    score_near = jnp.where(keep_cols[:, None, :], score_near, masked_score)
    top_score = jnp.maximum(lax.optimization_barrier(jnp.max(score_glob, -1, keepdims=True)), lax.optimization_barrier(jnp.max(score_near, -1, keepdims=True)))
    weight_glob = jnp.exp(score_glob - top_score)
    weight_near = jnp.exp(score_near - top_score)
    mass_sum = lax.optimization_barrier(jnp.sum(weight_glob, -1, keepdims=True)) + lax.optimization_barrier(jnp.sum(weight_near, -1, keepdims=True))
    glob_bf = (weight_glob / mass_sum).astype(jnp.bfloat16)
    near_bf = (weight_near / mass_sum).astype(jnp.bfloat16)
    result = jnp.einsum('nqk,kd->nqd', glob_bf.astype(jnp.float32), glob_values.astype(jnp.float32), precision=highest)
    result = result + jnp.einsum('nqk,nkd->nqd', near_bf.astype(jnp.float32), near_values.astype(jnp.float32), precision=highest)
    return result.astype(jnp.bfloat16)

def reference(history, qkv_weight, out_weight, rand_blocks):
    highest = lax.Precision.HIGHEST
    score_scale = 1.0 / math.sqrt(HD)
    projected = [jnp.dot(history, qkv_weight[index], preferred_element_type=jnp.float32).astype(jnp.bfloat16).reshape(TOKENS, H, HD).transpose(1, 0, 2) for index in range(3)]
    query_all, key_all, value_all = projected
    span_ids = jnp.arange(N_SEQ, dtype=jnp.int32)

    def one_head(packed):
        head_query, head_keys, head_values, head_rand = packed
        key_f32 = head_keys.astype(jnp.float32)
        glob_scores = jnp.dot(head_query[:G].astype(jnp.float32), key_f32.T, precision=highest) * score_scale
        glob_weights = jnp.exp(glob_scores - lax.optimization_barrier(jnp.max(glob_scores, -1, keepdims=True)))
        glob_out = jnp.dot(glob_weights, head_values.astype(jnp.float32), precision=highest) / lax.optimization_barrier(jnp.sum(glob_weights, -1, keepdims=True))
        zero_block = jnp.zeros((B, HD), jnp.bfloat16)
        key_pad = jnp.concatenate([zero_block, head_keys, zero_block]).reshape(BLOCKS + 2, B, HD)
        value_pad = jnp.concatenate([zero_block, head_values, zero_block]).reshape(BLOCKS + 2, B, HD)
        key_blocks = head_keys.reshape(BLOCKS, B, HD)
        value_blocks = head_values.reshape(BLOCKS, B, HD)

        def one_span(span):
            block_ids = span * BLOCKS_DEV + jnp.arange(BLOCKS_DEV, dtype=jnp.int32)
            queries = lax.dynamic_slice_in_dim(head_query, span * TOK_DEV, TOK_DEV, 0).reshape(BLOCKS_DEV, B, HD)
            window_idx = block_ids[:, None] + jnp.arange(3, dtype=jnp.int32)[None, :]
            rand_idx = lax.dynamic_slice_in_dim(head_rand, span * BLOCKS_DEV, BLOCKS_DEV, 0)
            near_keys = jnp.concatenate([key_pad[window_idx].reshape(BLOCKS_DEV, 3 * B, HD), key_blocks[rand_idx].reshape(BLOCKS_DEV, R * B, HD)], axis=1)
            near_values = jnp.concatenate([value_pad[window_idx].reshape(BLOCKS_DEV, 3 * B, HD), value_blocks[rand_idx].reshape(BLOCKS_DEV, R * B, HD)], axis=1)
            return attend_blocks(queries, head_keys[:G], head_values[:G], near_keys, near_values, block_ids)
        sparse_all = lax.map(one_span, span_ids).reshape(TOKENS, HD)
        return jnp.concatenate([glob_out.astype(jnp.bfloat16), sparse_all[G:]], axis=0)
    head_outs = lax.map(one_head, (query_all, key_all, value_all, rand_blocks))
    attn = head_outs.transpose(1, 0, 2).reshape(TOKENS, H * HD)
    return jnp.dot(attn, out_weight, preferred_element_type=jnp.float32).astype(jnp.bfloat16)
```

```python
import functools
import math

import jax
import jax.numpy as jnp
from jax import lax
from jax.experimental import pallas as pl
from jax.experimental.pallas import tpu as pltpu
from jax.sharding import PartitionSpec as P

B = 64
R = 3
G = 1024
HD = 64
GBLOCKS = 16
LANES = 2 * HD
KEY_TILE = 1024
VMEM_LIMIT = 56 * 1024 * 1024

masked_score = -1e30


def dot_nt(a, b):
    return lax.dot_general(a, b, (((1,), (1,)), ((), ())), preferred_element_type=jnp.float32)


def dot_nn(a, b):
    return jnp.dot(a, b, preferred_element_type=jnp.float32)


def left_half(rows):
    return lax.broadcasted_iota(jnp.int32, (rows, LANES), 1) < HD


def swap_halves(value):
    return jnp.concatenate([value[:, HD:], value[:, :HD]], axis=1)


def project_kv(history_ref, key_ref, value_ref, out_ref):
    weight = jnp.concatenate([key_ref[0], value_ref[0]], axis=1)
    both = dot_nn(history_ref[...], weight).astype(jnp.bfloat16)
    keys, values = both[:, :LANES], both[:, LANES:]
    left = left_half(keys.shape[0])
    out_ref[0] = jnp.where(left, keys, swap_halves(values))
    out_ref[1] = jnp.where(left, swap_halves(keys), values)


def project_q(group_count, history_ref, weight_ref, out_ref):
    query = dot_nn(history_ref[...], weight_ref[0]).astype(jnp.bfloat16)
    query = query * jnp.bfloat16(1.0 / math.sqrt(HD))
    rows = query.shape[0] // group_count
    half = rows // 2
    left = left_half(half)
    for pair in range(query.shape[1] // LANES):
        for group in range(group_count):
            top = query[group * rows : group * rows + half, pair * LANES : (pair + 1) * LANES]
            low = query[group * rows + half : (group + 1) * rows, pair * LANES : (pair + 1) * LANES]
            out_ref[2 * pair * group_count + group] = jnp.where(left, top, swap_halves(low))
            out_ref[(2 * pair + 1) * group_count + group] = jnp.where(left, swap_halves(top), low)


def project(history, qkv_weight, group_count):
    rows, width = history.shape
    heads = qkv_weight.shape[2] // HD
    whole = pl.BlockSpec((rows, width), lambda i: (0, 0))
    params = pltpu.CompilerParams(vmem_limit_bytes=VMEM_LIMIT)
    key_value = pl.pallas_call(
        project_kv,
        grid=(heads // 2,),
        in_specs=[
            whole,
            pl.BlockSpec((1, width, LANES), lambda i: (1, 0, i)),
            pl.BlockSpec((1, width, LANES), lambda i: (2, 0, i)),
        ],
        out_specs=pl.BlockSpec((2, rows, LANES), lambda i: (i, 0, 0)),
        out_shape=jax.ShapeDtypeStruct((heads, rows, LANES), jnp.bfloat16),
        compiler_params=params,
        cost_estimate=pl.CostEstimate(
            flops=4 * rows * width * heads * HD, bytes_accessed=6 << 20, transcendentals=0
        ),
        name="project_kv",
    )(history, qkv_weight, qkv_weight)
    step = min(4, heads)
    half = rows // group_count // 2
    query = pl.pallas_call(
        functools.partial(project_q, group_count),
        grid=(heads // step,),
        in_specs=[whole, pl.BlockSpec((1, width, step * HD), lambda i: (0, 0, i))],
        out_specs=pl.BlockSpec((step * group_count, half, LANES), lambda i: (i, 0, 0)),
        out_shape=jax.ShapeDtypeStruct((heads * group_count, half, LANES), jnp.bfloat16),
        compiler_params=params,
        cost_estimate=pl.CostEstimate(
            flops=2 * rows * width * heads * HD, bytes_accessed=4 << 20, transcendentals=0
        ),
        name="project_q",
    )(history, qkv_weight)
    return key_value, query


def pack_rows(value):
    half = value.shape[0] // 2
    value = value.astype(jnp.bfloat16)
    return jnp.where(left_half(half), value[:half], swap_halves(value[half:]))


def attend(sizes, where_ref, rand_ref, query_ref, kv_ref, out_ref, values_ref):
    total_blocks, blocks_dev, group_blocks, chunk = sizes
    source = pl.program_id(0)
    half = query_ref.shape[1]
    rows = 2 * half
    tile = min(rows, 256)
    total = kv_ref.shape[0]

    @pl.when(source == 0)
    def _():
        def build(i, _):
            at = pl.ds(pl.multiple_of(i * KEY_TILE, KEY_TILE), KEY_TILE)
            lane = lax.broadcasted_iota(jnp.int32, (KEY_TILE, LANES), 1)
            ones = jnp.where(lane == HD, 1.0, 0.0).astype(jnp.bfloat16)
            values_ref[at] = jnp.where(lane < HD, swap_halves(kv_ref[at]), ones)
            return 0

        lax.fori_loop(0, total // KEY_TILE, build, 0)

    packed = query_ref[0]
    left = left_half(half)
    zero = jnp.zeros((), jnp.bfloat16)
    query = jnp.concatenate(
        [jnp.where(left, packed, zero), jnp.where(left, swap_halves(packed), zero)], axis=0
    )

    def finish(acc):
        return acc / acc[:, HD : HD + 1]

    def write(done):
        value = jnp.concatenate(done, axis=0)
        if half >= B:
            out_ref[0] = pack_rows(value[:half])
            out_ref[1] = pack_rows(value[half:])
        else:
            out_ref[0] = pack_rows(value)

    @pl.when(source == 0)
    def _():
        done = []
        for first in range(0, rows, tile):
            part = query[first : first + tile]

            def step(i, carry):
                top, acc = carry
                at = pl.ds(pl.multiple_of(i * KEY_TILE, KEY_TILE), KEY_TILE)
                scores = dot_nt(part, kv_ref[at])
                new_top = jnp.maximum(top, jnp.max(scores, -1, keepdims=True))
                weights = jnp.exp(scores - new_top).astype(jnp.bfloat16)
                acc = acc * jnp.exp(top - new_top) + dot_nn(weights, values_ref[at])
                return new_top, acc

            start = (
                jnp.full((tile, 1), -jnp.inf, jnp.float32),
                jnp.zeros((tile, LANES), jnp.float32),
            )
            _, acc = lax.fori_loop(0, total // KEY_TILE, step, start)
            done.append(finish(acc))
        write(done)

    @pl.when(source > 0)
    def _():
        done = []
        lane = lax.broadcasted_iota(jnp.int32, (1, 2 * R * B), 1)
        for first in range(0, rows, tile):
            part = query[first : first + tile]
            glob_scores = dot_nt(part, kv_ref[:G])
            glob_top = jnp.max(glob_scores, -1, keepdims=True)
            near = []
            tops = []
            for n in range(tile // B):
                at = first // B + n
                if half >= B:
                    per = half // B
                    local = (at // per) * (group_blocks // 2) + chunk * per + at % per
                else:
                    local = 0
                block = source * blocks_dev + where_ref[0] * group_blocks + local
                ids = [
                    block - 1,
                    block,
                    jnp.minimum(block + 1, total_blocks - 1),
                ] + [rand_ref[(source * group_blocks + local) * R + r] for r in range(R)]
                slices = [pl.ds(pl.multiple_of(k * B, B), B) for k in ids]
                near_keys = jnp.concatenate([kv_ref[s] for s in slices], axis=0)
                near_values = jnp.concatenate([values_ref[s] for s in slices], axis=0)
                dead_low = block - 1 < GBLOCKS
                dead_high = block + 1 >= total_blocks
                dead = ((lane < B) & dead_low) | ((lane >= 2 * B) & (lane < 3 * B) & dead_high)
                scores = dot_nt(part[n * B : (n + 1) * B], near_keys)
                scores = jnp.where(dead, masked_score, scores)
                top = jnp.maximum(
                    glob_top[n * B : (n + 1) * B], jnp.max(scores, -1, keepdims=True)
                )
                near.append(
                    dot_nn(jnp.exp(scores - top).astype(jnp.bfloat16), near_values)
                )
                tops.append(top)
            top = jnp.concatenate(tops, axis=0)
            weights = jnp.exp(glob_scores - top).astype(jnp.bfloat16)
            acc = dot_nn(weights, values_ref[:G]) + jnp.concatenate(near, axis=0)
            done.append(finish(acc))
        write(done)


def attention(query, key_value, rand, group, sizes):
    sources, half, _ = query.shape
    total = key_value.shape[0]
    rows = 2 * half
    outs = 2 if half >= B else 1
    pairs = rows * (G * (sources - 1) + total)
    return pl.pallas_call(
        functools.partial(attend, sizes),
        grid_spec=pltpu.PrefetchScalarGridSpec(
            num_scalar_prefetch=2,
            grid=(sources,),
            in_specs=[
                pl.BlockSpec((1, half, LANES), lambda i, *_: (i, 0, 0)),
                pl.BlockSpec((total, LANES), lambda i, *_: (0, 0)),
            ],
            out_specs=pl.BlockSpec((outs, rows // outs // 2, LANES), lambda i, *_: (i, 0, 0)),
            scratch_shapes=[pltpu.VMEM((total, LANES), jnp.bfloat16)],
        ),
        out_shape=jax.ShapeDtypeStruct((sources * outs, rows // outs // 2, LANES), jnp.bfloat16),
        compiler_params=pltpu.CompilerParams(vmem_limit_bytes=VMEM_LIMIT),
        cost_estimate=pl.CostEstimate(
            flops=16 * HD * pairs, bytes_accessed=4 << 20, transcendentals=pairs
        ),
        name="attend",
    )(group, rand, query, key_value)


def project_out(head_count, *refs):
    weight_ref, out_ref = refs[-2:]
    parts = []
    for ref in refs[:-2]:
        half = ref.shape[1]
        left = left_half(half)
        tops, lows = [], []
        axis = ref.shape[0] // head_count
        for head in range(0, ref.shape[0], 2):
            one = ref[(head % head_count) * axis + head // head_count]
            two = ref[((head + 1) % head_count) * axis + (head + 1) // head_count]
            tops.append(jnp.where(left, one, swap_halves(two)))
            lows.append(jnp.where(left, swap_halves(one), two))
        parts.append(jnp.concatenate(tops, axis=1))
        parts.append(jnp.concatenate(lows, axis=1))
    attn = jnp.concatenate(parts, axis=0)
    out_ref[...] = dot_nn(attn, weight_ref[...]).astype(jnp.bfloat16)


def shards(history, qkv_weight, out_weight, rand_blocks):
    tok_rows, width = history.shape
    head_count = qkv_weight.shape[2] // HD
    seq_count = lax.axis_size("seq")
    blocks_dev = tok_rows // B
    total_blocks = blocks_dev * seq_count
    group_count = seq_count // head_count
    group_blocks = blocks_dev // group_count
    chunks = 2 if group_count == 1 else 1
    key_value, query = project(history, qkv_weight, group_count)
    rand = lax.all_to_all(
        rand_blocks.reshape(seq_count, group_blocks * R), "seq", 0, 0, tiled=True
    ).reshape(-1)
    seq_at = lax.axis_index("seq")
    group = (seq_at % group_count).reshape(1)
    if group_count == 1:
        key_value = lax.all_to_all(key_value, "seq", 0, 0, tiled=True)
        weight = lax.all_gather(out_weight, "head", tiled=True)
    else:
        key_value = lax.all_gather(key_value, "seq")
        key_value = lax.dynamic_index_in_dim(key_value, seq_at // group_count, 1, False)
    key_value = key_value.reshape(seq_count * tok_rows, LANES)
    half = query.shape[1] // chunks
    outs = []
    for chunk in range(chunks):
        part = lax.slice_in_dim(query, chunk * half, (chunk + 1) * half, axis=1)
        part = lax.all_to_all(part, "seq", 0, 0, tiled=True)
        sizes = (total_blocks, blocks_dev, group_blocks, chunk)
        outs.append(attention(part, key_value, rand, group, sizes))
    if group_count == 1:
        outs = [lax.all_to_all(part, ("seq", "head"), 0, 0, tiled=True) for part in outs]
        rows = tok_rows // lax.axis_size("head")
        return pl.pallas_call(
            functools.partial(project_out, head_count),
            out_shape=jax.ShapeDtypeStruct((rows, width), jnp.bfloat16),
            compiler_params=pltpu.CompilerParams(vmem_limit_bytes=VMEM_LIMIT),
            cost_estimate=pl.CostEstimate(
                flops=2 * rows * width * weight.shape[0], bytes_accessed=4 << 20, transcendentals=0
            ),
            name="project_out",
        )(*outs, weight)
    attn = lax.all_to_all(outs[0], "seq", 0, 0, tiled=True)
    attn = attn.reshape(head_count, group_count, -1, 2, HD).transpose(1, 3, 2, 0, 4)
    attn = attn.reshape(tok_rows, head_count * HD)
    return lax.psum_scatter(
        jnp.dot(attn, out_weight, preferred_element_type=jnp.float32).astype(jnp.bfloat16),
        "head",
        scatter_dimension=0,
        tiled=True,
    )


def solution(mesh):
    placed = (
        P(("groups", "seq"), None),
        P(None, None, "head"),
        P("head", None),
        P("head", ("groups", "seq"), None),
    )
    return jax.shard_map(
        shards,
        mesh=mesh,
        in_specs=placed,
        out_specs=P(("groups", "seq", "head"), None),
        check_vma=False,
    )
```

```python
import functools
import math

import jax
import jax.numpy as jnp
from jax import lax
from jax.experimental import pallas as pl
from jax.experimental.pallas import tpu as pltpu
from jax.sharding import PartitionSpec as P

B = 64
R = 3
G = 1024
HD = 64
GBLOCKS = 16
LANES = 2 * HD
QUAD = 4
NEAR = 3 + R
KEY_TILE = 1024
SUM_ROWS = 16
VMEM_LIMIT = 56 * 1024 * 1024

masked_score = -1e30


def dot_nt(a, b):
    return lax.dot_general(a, b, (((1,), (1,)), ((), ())), preferred_element_type=jnp.float32)


def dot_nn(a, b):
    return jnp.dot(a, b, preferred_element_type=jnp.float32)


def left_half(rows):
    return lax.broadcasted_iota(jnp.int32, (rows, LANES), 1) < HD


def swap_halves(value):
    return jnp.concatenate([value[:, HD:], value[:, :HD]], axis=1)


def pair_rows(value):
    half = value.shape[0] // 2
    left = left_half(half)
    top, low = value[:half], value[half:]
    return jnp.where(left, top, swap_halves(low)), jnp.where(left, swap_halves(top), low)


def project_kv(history_ref, key_ref, value_ref, out_ref):
    weight = jnp.concatenate([key_ref[0], value_ref[0]], axis=1)
    both = dot_nn(history_ref[...], weight)
    rows = both.shape[0]
    first, second = pair_rows(both[:, :LANES].astype(jnp.bfloat16))
    out_ref[0, : rows // 2] = first
    out_ref[1, : rows // 2] = second
    turned = both[:, LANES:].T.astype(jnp.bfloat16)
    for i in range(rows // LANES):
        at = pl.ds(rows // 2 + i * HD, HD)
        out_ref[0, at] = turned[:HD, i * LANES : (i + 1) * LANES]
        out_ref[1, at] = turned[HD:, i * LANES : (i + 1) * LANES]


def project_q(history_ref, weight_ref, out_ref):
    query = dot_nn(history_ref[...], weight_ref[0]).astype(jnp.bfloat16)
    query = query * jnp.bfloat16(1.0 / math.sqrt(HD))
    for pair in range(query.shape[1] // LANES):
        first, second = pair_rows(query[:, pair * LANES : (pair + 1) * LANES])
        out_ref[2 * pair] = first
        out_ref[2 * pair + 1] = second


def project(history, qkv_weight):
    rows, width = history.shape
    heads = qkv_weight.shape[2] // HD
    whole = pl.BlockSpec((rows, width), lambda i: (0, 0))
    params = pltpu.CompilerParams(vmem_limit_bytes=VMEM_LIMIT)
    key_value = pl.pallas_call(
        project_kv,
        grid=(heads // 2,),
        in_specs=[
            whole,
            pl.BlockSpec((1, width, LANES), lambda i: (1, 0, i)),
            pl.BlockSpec((1, width, LANES), lambda i: (2, 0, i)),
        ],
        out_specs=pl.BlockSpec((2, rows, LANES), lambda i: (i, 0, 0)),
        out_shape=jax.ShapeDtypeStruct((heads, rows, LANES), jnp.bfloat16),
        compiler_params=params,
        cost_estimate=pl.CostEstimate(
            flops=4 * rows * width * heads * HD, bytes_accessed=6 << 20, transcendentals=0
        ),
        name="project_kv",
    )(history, qkv_weight, qkv_weight)
    history, key_value = lax.optimization_barrier((history, key_value))
    step = min(4, heads)
    query = pl.pallas_call(
        project_q,
        grid=(heads // step,),
        in_specs=[whole, pl.BlockSpec((1, width, step * HD), lambda i: (0, 0, i))],
        out_specs=pl.BlockSpec((step, rows // 2, LANES), lambda i: (i, 0, 0)),
        out_shape=jax.ShapeDtypeStruct((heads, rows // 2, LANES), jnp.bfloat16),
        compiler_params=params,
        cost_estimate=pl.CostEstimate(
            flops=2 * rows * width * heads * HD, bytes_accessed=4 << 20, transcendentals=0
        ),
        name="project_q",
    )(history, qkv_weight)
    return key_value, query


def attend(sizes, ids_ref, query_ref, kv_ref, out_ref, keys_ref, values_ref):
    total_blocks, global_steps, mixed = sizes
    step = pl.program_id(0)
    sources, rows, _ = kv_ref.shape
    half = rows // 2
    quads = query_ref.shape[1] // (2 * B)
    pairs = rows // LANES
    left = left_half(B)
    zero = jnp.zeros((B, LANES), jnp.bfloat16)

    @pl.when(step == 0)
    def _():
        def build(source, _):
            packed = kv_ref[source, :half]
            wide = left_half(half)
            other = swap_halves(packed)
            keys_ref[pl.ds(pl.multiple_of(source * rows, rows), half)] = jnp.where(
                wide, packed, other
            )
            keys_ref[pl.ds(pl.multiple_of(source * rows + half, half), half)] = jnp.where(
                wide, other, packed
            )
            for i in range(pairs):
                tile = kv_ref[source, half + i * HD : half + (i + 1) * HD]
                turned = swap_halves(tile)
                values_ref[source * 2 * pairs + 2 * i] = jnp.where(left, tile, turned)
                values_ref[source * 2 * pairs + 2 * i + 1] = jnp.where(left, turned, tile)
            return 0

        lax.fori_loop(0, sources, build, 0)

    def turned_values(source):
        tiles = [kv_ref[source, half + i * HD : half + (i + 1) * HD] for i in range(pairs)]
        ones = jnp.ones((SUM_ROWS, rows), jnp.bfloat16)
        return jnp.concatenate([jnp.concatenate(tiles, axis=1), ones], axis=0)

    def queries_of(quad):
        parts = []
        for i in range(2):
            at = (2 * quad + i) * B
            packed = query_ref[0, at : at + B]
            parts.append(jnp.where(left, packed, zero))
            parts.append(jnp.where(left, zero, packed))
        return parts

    def write(quad, acc):
        value = acc[:HD] / acc[HD : HD + 1]
        first, second = value[:, :LANES], value[:, LANES:]
        at = slice(quad * LANES, (quad + 1) * LANES)
        out_ref[0, 0, :, at] = jnp.where(left, first, swap_halves(second)).astype(jnp.bfloat16)
        out_ref[0, 1, :, at] = jnp.where(left, swap_halves(first), second).astype(jnp.bfloat16)

    def full_rows():
        query = jnp.concatenate([p for quad in range(quads) for p in queries_of(quad)], axis=0)

        def body(source, carry):
            top, acc = carry
            at = pl.ds(pl.multiple_of(source * rows, rows), rows)
            scores = dot_nt(keys_ref[at], query)
            new_top = jnp.maximum(top, jnp.max(scores, 0, keepdims=True))
            weights = jnp.exp(scores - new_top).astype(jnp.bfloat16)
            acc = acc * jnp.exp(top - new_top) + dot_nn(turned_values(source), weights)
            return new_top, acc

        start = (
            jnp.full((1, query.shape[0]), -jnp.inf, jnp.float32),
            jnp.zeros((HD + SUM_ROWS, query.shape[0]), jnp.float32),
        )
        acc = lax.fori_loop(0, sources, body, start, unroll=min(sources, 8))[1]
        width = QUAD * B
        return [acc[:, quad * width : (quad + 1) * width] for quad in range(quads)]

    def block_of(quad, b):
        return ids_ref[((step * quads + quad) * QUAD + b) * (1 + R)]

    def near_rows(quad):
        parts = queries_of(quad)
        glob_scores = dot_nt(keys_ref[:G], jnp.concatenate(parts, axis=0))
        lists = []
        dead = []
        for b in range(QUAD):
            at = ((step * quads + quad) * QUAD + b) * (1 + R)
            block = ids_ref[at]
            lists.append(
                [jnp.maximum(block - 1, 0), block, jnp.minimum(block + 1, total_blocks - 1)]
                + [ids_ref[at + 1 + r] for r in range(R)]
            )
            dead.append((block - 1 < GBLOCKS, block + 1 >= total_blocks))
        near_keys = []
        for b in range(0, QUAD, 2):
            tiles = []
            for k in range(NEAR):
                one, two = [
                    keys_ref[pl.ds(pl.multiple_of(lists[b + j][k] * B, B), B)] for j in range(2)
                ]
                tiles.append(jnp.where(left, one, two))
            near_keys.append(jnp.concatenate(tiles, axis=0))
        blank = jnp.zeros((2 * B, LANES), jnp.bfloat16)
        diagonal = jnp.concatenate(
            [
                jnp.concatenate(parts[:2] + [blank], axis=0),
                jnp.concatenate([blank] + parts[2:], axis=0),
            ],
            axis=1,
        )
        scores = dot_nt(jnp.concatenate(near_keys, axis=1), diagonal)
        column = lax.broadcasted_iota(jnp.int32, (1, QUAD * B), 1) // B
        low = functools.reduce(
            jnp.logical_or, [(column == b) & dead[b][0] for b in range(QUAD)]
        )
        high = functools.reduce(
            jnp.logical_or, [(column == b) & dead[b][1] for b in range(QUAD)]
        )
        scores = jnp.concatenate(
            [
                jnp.where(low, masked_score, scores[:B]),
                scores[B : 2 * B],
                jnp.where(high, masked_score, scores[2 * B : 3 * B]),
                scores[3 * B :],
            ],
            axis=0,
        )
        top = jnp.maximum(
            jnp.max(glob_scores, 0, keepdims=True), jnp.max(scores, 0, keepdims=True)
        )
        glob_weights = jnp.exp(glob_scores - top).astype(jnp.bfloat16)
        weights = jnp.exp(scores - top).astype(jnp.bfloat16)
        near_values = [
            jnp.concatenate(
                [
                    jnp.where(left, values_ref[lists[b][k]], values_ref[lists[b][k + 1]])
                    for k in range(0, NEAR, 2)
                ],
                axis=1,
            )
            for b in range(QUAD)
        ]
        near_values.append(jnp.ones((SUM_ROWS, NEAR * B), jnp.bfloat16))
        near = dot_nn(jnp.concatenate(near_values, axis=0), weights)
        own = jnp.concatenate(
            [
                jnp.where(left, near[:HD, :LANES], near[HD : 2 * HD, :LANES]),
                jnp.where(left, near[2 * HD : 3 * HD, LANES:], near[3 * HD : 4 * HD, LANES:]),
            ],
            axis=1,
        )
        return dot_nn(turned_values(0), glob_weights) + jnp.concatenate(
            [own, near[QUAD * HD :]], axis=0
        )

    @pl.when(step < global_steps)
    def _():
        for quad, acc in enumerate(full_rows()):
            if mixed:
                column = lax.broadcasted_iota(jnp.int32, (1, QUAD * B), 1) // B
                glob = functools.reduce(
                    jnp.logical_or,
                    [(column == b) & (block_of(quad, b) < GBLOCKS) for b in range(QUAD)],
                )
                acc = jnp.where(glob, acc, near_rows(quad))
            write(quad, acc)

    @pl.when(step >= global_steps)
    def _():
        for quad in range(quads):
            write(quad, near_rows(quad))


def attention(query, key_value, ids, sizes):
    steps, half, _ = query.shape
    sources, rows, _ = key_value.shape
    total = sources * rows
    pairs = 2 * half * (G * steps + total)
    return pl.pallas_call(
        functools.partial(attend, sizes),
        grid_spec=pltpu.PrefetchScalarGridSpec(
            num_scalar_prefetch=1,
            grid=(steps,),
            in_specs=[
                pl.BlockSpec((1, half, LANES), lambda i, *_: (i, 0, 0)),
                pl.BlockSpec((sources, rows, LANES), lambda i, *_: (0, 0, 0)),
            ],
            out_specs=pl.BlockSpec((1, 2, HD, half), lambda i, *_: (i, 0, 0, 0)),
            scratch_shapes=[
                pltpu.VMEM((total, LANES), jnp.bfloat16),
                pltpu.VMEM((total // B, HD, LANES), jnp.bfloat16),
            ],
        ),
        out_shape=jax.ShapeDtypeStruct((steps, 2, HD, half), jnp.bfloat16),
        compiler_params=pltpu.CompilerParams(vmem_limit_bytes=VMEM_LIMIT),
        cost_estimate=pl.CostEstimate(
            flops=16 * HD * pairs, bytes_accessed=4 << 20, transcendentals=pairs
        ),
        name="attend",
    )(ids, query, key_value)


def project_out(head_count, *refs):
    weight_ref, out_ref = refs[-2:]
    at = 0
    for ref in refs[:-2]:
        axis = ref.shape[0] // head_count
        heads = [ref[(h % head_count) * axis + h // head_count] for h in range(ref.shape[0])]
        turned = jnp.concatenate(heads, axis=0)
        value = lax.dot_general(
            turned,
            weight_ref[...],
            (((0,), (0,)), ((), ())),
            preferred_element_type=jnp.float32,
        )
        out_ref[at : at + value.shape[0]] = value.astype(jnp.bfloat16)
        at += value.shape[0]


def shards(history, qkv_weight, out_weight, rand_blocks):
    tok_rows, width = history.shape
    head_count = qkv_weight.shape[2] // HD
    seq_count = lax.axis_size("seq")
    blocks_dev = tok_rows // B
    total_blocks = blocks_dev * seq_count
    group_count = seq_count // head_count
    seq_at = lax.axis_index("seq")
    key_value, query = project(history, qkv_weight)
    own_ids = seq_at * blocks_dev + jnp.arange(blocks_dev, dtype=jnp.int32)
    own_ids = jnp.broadcast_to(own_ids[None, :, None], (head_count, blocks_dev, 1))
    ids = jnp.concatenate([own_ids, rand_blocks], axis=2)

    if group_count == 1:
        chunks = 2
        key_value, query, ids = lax.optimization_barrier((key_value, query, ids))
        key_value = lax.all_to_all(key_value, "seq", 0, 0, tiled=True)
        ids = lax.all_to_all(ids, "seq", 0, 0, tiled=True)
        weight = lax.all_gather(out_weight, "head", tiled=True)
        half = tok_rows // 2 // chunks
        per = half // B
        ids = ids.reshape(seq_count, 2, chunks, per, 1 + R).transpose(2, 0, 3, 1, 4)
        outs = []
        for chunk in range(chunks):
            part = lax.slice_in_dim(query, chunk * half, (chunk + 1) * half, axis=1)
            part = lax.all_to_all(part, "seq", 0, 0, tiled=True)
            out = attention(part, key_value, ids[chunk].reshape(-1), (total_blocks, 1, False))
            out = out.reshape(2 * seq_count, HD, half)
            outs.append(lax.all_to_all(out, ("seq", "head"), 0, 0, tiled=True))
        rows = tok_rows // lax.axis_size("head")
        return pl.pallas_call(
            functools.partial(project_out, head_count),
            out_shape=jax.ShapeDtypeStruct((rows, width), jnp.bfloat16),
            compiler_params=pltpu.CompilerParams(vmem_limit_bytes=VMEM_LIMIT),
            cost_estimate=pl.CostEstimate(
                flops=2 * rows * width * weight.shape[0], bytes_accessed=4 << 20, transcendentals=0
            ),
            name="project_out",
        )(*outs, weight)

    key_value = lax.all_gather(key_value, "seq")
    key_value = lax.dynamic_index_in_dim(key_value, seq_at // group_count, 1, False)
    blocks = seq_count * blocks_dev // group_count
    query = query.reshape(head_count, tok_rows // 2, 2, HD).transpose(0, 2, 1, 3)
    query = query.reshape(seq_count, -1, HD)
    query = lax.all_to_all(query, "seq", 0, 0, tiled=True)
    query = query.reshape(blocks // QUAD, 2, 2, B, HD).transpose(0, 1, 3, 2, 4)
    query = query.reshape(blocks // QUAD, 2 * B, LANES)
    ids = ids.reshape(seq_count, -1, 1 + R)
    ids = lax.all_to_all(ids, "seq", 0, 0, tiled=True).reshape(-1)
    global_steps = -(-GBLOCKS // group_count // QUAD)
    out = attention(query, key_value, ids, (total_blocks, global_steps, True))
    out = out.reshape(blocks // QUAD, 2, HD, 2, B).transpose(0, 3, 1, 4, 2)
    out = lax.all_to_all(out.reshape(seq_count, -1, HD), "seq", 0, 0, tiled=True)
    attn = out.reshape(head_count, tok_rows, HD).transpose(1, 0, 2)
    return lax.psum_scatter(
        jnp.dot(
            attn.reshape(tok_rows, head_count * HD),
            out_weight,
            preferred_element_type=jnp.float32,
        ).astype(jnp.bfloat16),
        "head",
        scatter_dimension=0,
        tiled=True,
    )


def solution(mesh):
    placed = (
        P(("groups", "seq"), None),
        P(None, None, "head"),
        P("head", None),
        P("head", ("groups", "seq"), None),
    )
    return jax.shard_map(
        shards,
        mesh=mesh,
        in_specs=placed,
        out_specs=P(("groups", "seq", "head"), None),
        check_vma=False,
    )
```

```python
import functools
import math

import jax
import jax.numpy as jnp
from jax import lax
from jax.experimental import pallas as pl
from jax.experimental.pallas import tpu as pltpu
from jax.sharding import PartitionSpec as P

B = 64
R = 3
G = 1024
HD = 64
GBLOCKS = 16
LANES = 2 * HD
QUAD = 4
NEAR = 3 + R
SUM_ROWS = 16
ID_ROWS = 16
ID_BASE = 256
VMEM_LIMIT = 56 * 1024 * 1024

AHEAD = 8

masked_score = -1e30


def dot_nt(a, b):
    return lax.dot_general(a, b, (((1,), (1,)), ((), ())), preferred_element_type=jnp.float32)


def dot_nn(a, b):
    return jnp.dot(a, b, preferred_element_type=jnp.float32)


def left_half(rows):
    return lax.broadcasted_iota(jnp.int32, (rows, LANES), 1) < HD


def swap_halves(value):
    return jnp.concatenate([value[:, HD:], value[:, :HD]], axis=1)


def pair_rows(value):
    half = value.shape[0] // 2
    left = left_half(half)
    top, low = value[:half], value[half:]
    return jnp.where(left, top, swap_halves(low)), jnp.where(left, swap_halves(top), low)


def project_first(half, history_ref, query_ref, key_ref, value_ref, ids_ref, out_ref):
    rows = history_ref.shape[0]
    weight = jnp.concatenate([key_ref[0], value_ref[0]], axis=1)
    both = dot_nn(history_ref[...], weight)
    pairs = pair_rows(both[:, :LANES].astype(jnp.bfloat16))
    turned = both[:, LANES:].T.astype(jnp.bfloat16)
    queries = project_half(history_ref, query_ref[0], 0, half)
    for j in range(2):
        out_ref[j, : rows // 2] = pairs[j]
        for i in range(rows // LANES):
            tile = turned[j * HD : (j + 1) * HD, i * LANES : (i + 1) * LANES]
            out_ref[j, rows // 2 + i * HD : rows // 2 + (i + 1) * HD] = tile
        out_ref[j, rows : rows + half] = queries[j]
        out_ref[j, rows + half :] = ids_ref[j]


def project_half(history_ref, weight, first, half):
    middle = history_ref.shape[0] // 2
    chosen = jnp.concatenate(
        [
            history_ref[first : first + half],
            history_ref[middle + first : middle + first + half],
        ],
        axis=0,
    )
    query = dot_nn(chosen, weight).astype(jnp.bfloat16)
    query = query * jnp.bfloat16(1.0 / math.sqrt(HD))
    found = []
    for pair in range(query.shape[1] // LANES):
        found.extend(pair_rows(query[:, pair * LANES : (pair + 1) * LANES]))
    return found


def project_later(first, history_ref, weight_ref, out_ref):
    found = project_half(history_ref, weight_ref[0], first, out_ref.shape[1])
    for j, value in enumerate(found):
        out_ref[j] = value


def project(history, qkv_weight, ids, chunks):
    rows, width = history.shape
    heads = qkv_weight.shape[2] // HD
    half = rows // 2 // chunks
    total = rows + half + ID_ROWS
    whole = pl.BlockSpec((rows, width), lambda i: (0, 0))
    params = pltpu.CompilerParams(vmem_limit_bytes=VMEM_LIMIT)
    first = pl.pallas_call(
        functools.partial(project_first, half),
        grid=(heads // 2,),
        in_specs=[
            whole,
            pl.BlockSpec((1, width, LANES), lambda i: (0, 0, i)),
            pl.BlockSpec((1, width, LANES), lambda i: (1, 0, i)),
            pl.BlockSpec((1, width, LANES), lambda i: (2, 0, i)),
            pl.BlockSpec((2, ID_ROWS, LANES), lambda i: (i, 0, 0)),
        ],
        out_specs=pl.BlockSpec((2, total, LANES), lambda i: (i, 0, 0)),
        out_shape=jax.ShapeDtypeStruct((heads, total, LANES), jnp.bfloat16),
        compiler_params=params,
        cost_estimate=pl.CostEstimate(
            flops=5 * rows * width * heads * HD, bytes_accessed=6 << 20, transcendentals=0
        ),
        name="project_first",
    )(history, qkv_weight, qkv_weight, qkv_weight, ids)
    later = []
    step = min(4, heads)
    for chunk in range(1, chunks):
        history, first = lax.optimization_barrier((history, first))
        later.append(
            pl.pallas_call(
                functools.partial(project_later, chunk * half),
                grid=(heads // step,),
                in_specs=[whole, pl.BlockSpec((1, width, step * HD), lambda i: (0, 0, i))],
                out_specs=pl.BlockSpec((step, half, LANES), lambda i: (i, 0, 0)),
                out_shape=jax.ShapeDtypeStruct((heads, half, LANES), jnp.bfloat16),
                compiler_params=params,
                cost_estimate=pl.CostEstimate(
                    flops=4 * half * width * heads * HD, bytes_accessed=4 << 20, transcendentals=0
                ),
                name="project_later",
            )(history, qkv_weight)
        )
    return first, later


def attend(plan, query_ref, kv_ref, ids_in_ref, out_ref, keys_ref, values_ref, ids_vmem, ids_ref, sem):
    rows, blocks_dev, total_blocks, places, global_quads, mixed, carried = plan
    sources = kv_ref.shape[0]
    half = rows // 2
    quads = len(places)
    per = out_ref.shape[3] // LANES
    pairs = rows // LANES
    left = left_half(B)
    zero = jnp.zeros((B, LANES), jnp.bfloat16)

    if carried:
        found = []
        for source in range(sources):
            pair = kv_ref[source, -ID_ROWS:].astype(jnp.float32)
            found.append(pair[:1] + pair[1:2] * ID_BASE)
        ids_vmem[...] = jnp.concatenate(found, axis=0).astype(jnp.int32)
        copy = pltpu.make_async_copy(ids_vmem, ids_ref, sem)
    else:
        copy = pltpu.make_async_copy(ids_in_ref, ids_ref, sem)
    copy.start()

    def build(source):
        packed = kv_ref[source, :half]
        wide = left_half(half)
        other = swap_halves(packed)
        keys_ref[source, :half] = jnp.where(wide, packed, other)
        keys_ref[source, half:] = jnp.where(wide, other, packed)
        for i in range(pairs):
            tile = kv_ref[source, half + i * HD : half + (i + 1) * HD]
            turned = swap_halves(tile)
            values_ref[source * 2 * pairs + 2 * i] = jnp.where(left, tile, turned)
            values_ref[source * 2 * pairs + 2 * i + 1] = jnp.where(left, turned, tile)

    def turned_values(source):
        tiles = [kv_ref[source, half + i * HD : half + (i + 1) * HD] for i in range(pairs)]
        ones = jnp.ones((SUM_ROWS, rows), jnp.bfloat16)
        return jnp.concatenate([jnp.concatenate(tiles, axis=1), ones], axis=0)

    def queries_of(quad):
        parts = []
        for i in range(2):
            packed = query_ref[quad, i * B : (i + 1) * B]
            parts.append(jnp.where(left, packed, zero))
            parts.append(jnp.where(left, zero, packed))
        return parts

    def write(quad, acc):
        value = acc[:HD] / acc[HD : HD + 1]
        first, second = value[:, :LANES], value[:, LANES:]
        at = slice(quad % per * LANES, (quad % per + 1) * LANES)
        out_ref[quad // per, 0, :, at] = jnp.where(left, first, swap_halves(second)).astype(
            jnp.bfloat16
        )
        out_ref[quad // per, 1, :, at] = jnp.where(left, swap_halves(first), second).astype(
            jnp.bfloat16
        )

    def full_rows():
        query = jnp.concatenate([p for n in range(global_quads) for p in queries_of(n)], axis=0)

        def score(source):
            return dot_nt(keys_ref[source], query)

        def fold(source, scores, carry):
            top, acc = carry
            new_top = jnp.maximum(top, jnp.max(scores, 0, keepdims=True))
            weights = jnp.exp(scores - new_top).astype(jnp.bfloat16)
            acc = acc * jnp.exp(top - new_top) + dot_nn(turned_values(source), weights)
            return new_top, acc

        carry = (
            jnp.full((1, query.shape[0]), -jnp.inf, jnp.float32),
            jnp.zeros((HD + SUM_ROWS, query.shape[0]), jnp.float32),
        )
        if sources <= 8:
            build(0)
            scores = score(0)
            for source in range(sources):
                later = None
                if source + 1 < sources:
                    build(source + 1)
                    later = score(source + 1)
                carry = fold(source, scores, carry)
                scores = later
        else:
            lax.fori_loop(0, sources, lambda i, _: (build(i), 0)[1], 0)
            carry = lax.fori_loop(0, sources, lambda i, c: fold(i, score(i), c), carry)
        width = QUAD * B
        return [carry[1][:, n * width : (n + 1) * width] for n in range(global_quads)]

    def block_of(place):
        source, local = place
        if carried:
            return source * blocks_dev + local
        return source * blocks_dev + ids_ref[source, LANES - 1] + local

    def key_block(block):
        at = block % blocks_dev if isinstance(block, int) else lax.rem(block, blocks_dev)
        source = block // blocks_dev if isinstance(block, int) else lax.div(block, blocks_dev)
        return keys_ref[source, pl.ds(at * B if isinstance(at, int) else pl.multiple_of(at * B, B), B)]

    def near_scores(quad):
        parts = queries_of(quad)
        glob_scores = dot_nt(keys_ref[0], jnp.concatenate(parts, axis=0))
        lists = []
        column = lax.broadcasted_iota(jnp.int32, (1, QUAD * B), 1) // B
        low = high = None
        for b, (source, local) in enumerate(places[quad]):
            block = block_of((source, local))
            if carried:
                window = [max(block - 1, 0), block, min(block + 1, total_blocks - 1)]
                dead_low, dead_high = block - 1 < GBLOCKS, block + 1 >= total_blocks
                if dead_low:
                    low = column == b if low is None else low | (column == b)
                if dead_high:
                    high = column == b if high is None else high | (column == b)
            else:
                window = [
                    jnp.maximum(block - 1, 0),
                    block,
                    jnp.minimum(block + 1, total_blocks - 1),
                ]
                one = (column == b) & (block - 1 < GBLOCKS)
                two = (column == b) & (block + 1 >= total_blocks)
                low = one if low is None else low | one
                high = two if high is None else high | two
            lists.append(window + [ids_ref[source, local * R + r] for r in range(R)])
        near_keys = []
        for b in range(0, QUAD, 2):
            tiles = [
                jnp.where(left, key_block(lists[b][k]), key_block(lists[b + 1][k]))
                for k in range(NEAR)
            ]
            near_keys.append(jnp.concatenate(tiles, axis=0))
        blank = jnp.zeros((2 * B, LANES), jnp.bfloat16)
        diagonal = jnp.concatenate(
            [
                jnp.concatenate(parts[:2] + [blank], axis=0),
                jnp.concatenate([blank] + parts[2:], axis=0),
            ],
            axis=1,
        )
        scores = dot_nt(jnp.concatenate(near_keys, axis=1), diagonal)
        if low is not None or high is not None:
            before, after = scores[:B], scores[2 * B : 3 * B]
            if low is not None:
                before = jnp.where(low, masked_score, before)
            if high is not None:
                after = jnp.where(high, masked_score, after)
            scores = jnp.concatenate([before, scores[B : 2 * B], after, scores[3 * B :]], axis=0)
        return glob_scores, scores, lists

    def near_finish(glob_scores, scores, lists):
        top = jnp.maximum(
            jnp.max(glob_scores, 0, keepdims=True), jnp.max(scores, 0, keepdims=True)
        )
        glob_weights = jnp.exp(glob_scores - top).astype(jnp.bfloat16)
        weights = jnp.exp(scores - top).astype(jnp.bfloat16)
        near_values = [
            jnp.concatenate(
                [
                    jnp.where(left, values_ref[lists[b][k]], values_ref[lists[b][k + 1]])
                    for k in range(0, NEAR, 2)
                ],
                axis=1,
            )
            for b in range(QUAD)
        ]
        near_values.append(jnp.ones((SUM_ROWS, NEAR * B), jnp.bfloat16))
        near = dot_nn(jnp.concatenate(near_values, axis=0), weights)
        own = jnp.concatenate(
            [
                jnp.where(left, near[:HD, :LANES], near[HD : 2 * HD, :LANES]),
                jnp.where(left, near[2 * HD : 3 * HD, LANES:], near[3 * HD : 4 * HD, LANES:]),
            ],
            axis=1,
        )
        return dot_nn(turned_values(0), glob_weights) + jnp.concatenate(
            [own, near[QUAD * HD :]], axis=0
        )

    glob = full_rows()
    copy.wait()
    if not mixed:
        for quad in range(global_quads):
            write(quad, glob[quad])
    first = 0 if mixed else global_quads
    ready = [near_scores(quad) for quad in range(first, min(first + AHEAD, quads))]
    for quad in range(first, quads):
        if quad + AHEAD < quads:
            ready.append(near_scores(quad + AHEAD))
        acc = near_finish(*ready[quad - first])
        if quad < global_quads:
            column = lax.broadcasted_iota(jnp.int32, (1, QUAD * B), 1) // B
            own = functools.reduce(
                jnp.logical_or,
                [(column == b) & (block_of(p) < GBLOCKS) for b, p in enumerate(places[quad])],
            )
            acc = jnp.where(own, glob[quad], acc)
        write(quad, acc)


def attention(query, key_value, ids, plan, per):
    rows, carried = plan[0], plan[-1]
    quads = query.shape[0]
    sources = key_value.shape[0]
    total = sources * rows
    pairs = QUAD * B * (quads * (G + NEAR * B) + total)
    if ids is None:
        ids = jnp.zeros((8, LANES), jnp.int32)
    return pl.pallas_call(
        functools.partial(attend, plan),
        out_shape=jax.ShapeDtypeStruct((quads // per, 2, HD, per * LANES), jnp.bfloat16),
        scratch_shapes=[
            pltpu.VMEM((sources, rows, LANES), jnp.bfloat16),
            pltpu.VMEM((total // B, HD, LANES), jnp.bfloat16),
            pltpu.VMEM((sources, LANES), jnp.int32),
            pltpu.SMEM((sources, LANES), jnp.int32),
            pltpu.SemaphoreType.DMA,
        ],
        compiler_params=pltpu.CompilerParams(vmem_limit_bytes=VMEM_LIMIT),
        cost_estimate=pl.CostEstimate(
            flops=16 * HD * pairs, bytes_accessed=4 << 20, transcendentals=pairs
        ),
        name="attend",
    )(query, key_value, ids)


def project_out(head_count, turned_ref, weight_ref, *refs):
    out_ref = refs[-1]
    axis = turned_ref.shape[0] // head_count
    heads = [
        turned_ref[(h % head_count) * axis + h // head_count] for h in range(turned_ref.shape[0])
    ]
    out_ref[...] = lax.dot_general(
        jnp.concatenate(heads, axis=0),
        weight_ref[...],
        (((0,), (0,)), ((), ())),
        preferred_element_type=jnp.float32,
    ).astype(jnp.bfloat16)


def output_rows(turned, weight, head_count, chunk, chunks, before):
    count, size, rows = turned.shape
    width = weight.shape[1]
    whole = [
        pl.BlockSpec(turned.shape, lambda i: (0, 0, 0)),
        pl.BlockSpec(weight.shape, lambda i: (0, 0)),
    ]
    return pl.pallas_call(
        functools.partial(project_out, head_count),
        grid=(1,),
        in_specs=whole + [pl.BlockSpec(memory_space=pl.ANY)] * len(before),
        out_specs=pl.BlockSpec((rows, width), lambda i: (chunk, 0)),
        out_shape=jax.ShapeDtypeStruct((rows * chunks, width), jnp.bfloat16),
        input_output_aliases={2: 0} if before else {},
        compiler_params=pltpu.CompilerParams(vmem_limit_bytes=VMEM_LIMIT),
        cost_estimate=pl.CostEstimate(
            flops=2 * rows * width * weight.shape[0], bytes_accessed=3 << 20, transcendentals=0
        ),
        name="project_out",
    )(turned, weight, *before)


def carried_ids(rand_blocks):
    heads = rand_blocks.shape[0]
    flat = rand_blocks.reshape(heads, 1, -1)
    flat = jnp.concatenate([flat % ID_BASE, flat // ID_BASE], axis=1)
    room = ((0, 0), (0, ID_ROWS - 2), (0, LANES - flat.shape[2]))
    return jnp.pad(flat, room).astype(jnp.bfloat16)


def shards(history, qkv_weight, out_weight, rand_blocks):
    tok_rows = history.shape[0]
    head_count = qkv_weight.shape[2] // HD
    seq_count = lax.axis_size("seq")
    blocks_dev = tok_rows // B
    total_blocks = blocks_dev * seq_count
    group_count = seq_count // head_count
    seq_at = lax.axis_index("seq")
    chunks = 2 if group_count == 1 else 1
    first, later = project(history, qkv_weight, carried_ids(rand_blocks), chunks)
    half = tok_rows // 2 // chunks

    if group_count == 1:
        first = lax.all_to_all(first, "seq", 0, 0, tiled=True)
        weight = lax.all_gather(out_weight, "head", tiled=True)
        per = half // (2 * B)
        outs = []
        for chunk in range(chunks):
            if chunk == 0:
                query = first[:, tok_rows : tok_rows + half]
            else:
                query = lax.all_to_all(later[chunk - 1], "seq", 0, 0, tiled=True)
            places = [
                [
                    (
                        n // per,
                        x * (blocks_dev // 2) + chunk * 2 * per + 2 * (n % per) + i,
                    )
                    for i in range(2)
                    for x in range(2)
                ]
                for n in range(seq_count * per)
            ]
            plan = (tok_rows, blocks_dev, total_blocks, places, per, False, True)
            out = attention(query.reshape(-1, 2 * B, LANES), first, None, plan, per)
            out = out.reshape(2 * seq_count, HD, half)
            outs.append(lax.all_to_all(out, ("seq", "head"), 0, 0, tiled=True))
        result = []
        for chunk in range(chunks):
            result = [output_rows(outs[chunk], weight, head_count, chunk, chunks, result)]
        return result[0]

    key_value = lax.all_gather(first[:, :tok_rows], "seq")
    key_value = lax.dynamic_index_in_dim(key_value, seq_at // group_count, 1, False)
    group_blocks = blocks_dev // group_count
    blocks = seq_count * group_blocks
    query = first[:, tok_rows : tok_rows + half]
    query = query.reshape(head_count, half, 2, HD).transpose(0, 2, 1, 3)
    query = lax.all_to_all(query.reshape(seq_count, -1, HD), "seq", 0, 0, tiled=True)
    query = query.reshape(blocks // QUAD, 2, 2, B, HD).transpose(0, 1, 3, 2, 4)
    query = query.reshape(blocks // QUAD, 2 * B, LANES)
    ids = rand_blocks.reshape(seq_count, group_blocks * R)
    ids = lax.all_to_all(ids, "seq", 0, 0, tiled=True)
    ids = jnp.pad(ids, ((0, 0), (0, LANES - ids.shape[1])))
    offset = seq_at % group_count * group_blocks
    ids = ids.at[:, LANES - 1].set(offset)
    places = [
        [((n * QUAD + b) // group_blocks, (n * QUAD + b) % group_blocks) for b in range(QUAD)]
        for n in range(blocks // QUAD)
    ]
    global_quads = -(-GBLOCKS // group_count // QUAD)
    plan = (tok_rows, blocks_dev, total_blocks, places, global_quads, True, False)
    out = attention(query, key_value, ids, plan, 1)
    out = out.reshape(blocks // QUAD, 2, HD, 2, B).transpose(0, 3, 1, 4, 2)
    out = lax.all_to_all(out.reshape(seq_count, -1, HD), "seq", 0, 0, tiled=True)
    attn = out.reshape(head_count, tok_rows, HD).transpose(1, 0, 2)
    return lax.psum_scatter(
        jnp.dot(
            attn.reshape(tok_rows, head_count * HD),
            out_weight,
            preferred_element_type=jnp.float32,
        ).astype(jnp.bfloat16),
        "head",
        scatter_dimension=0,
        tiled=True,
    )


def solution(mesh):
    placed = (
        P(("groups", "seq"), None),
        P(None, None, "head"),
        P("head", None),
        P("head", ("groups", "seq"), None),
    )
    return jax.shard_map(
        shards,
        mesh=mesh,
        in_specs=placed,
        out_specs=P(("groups", "seq", "head"), None),
        check_vma=False,
    )
```

```python
import functools
import math

import jax
import jax.numpy as jnp
from jax import lax
from jax.experimental import pallas as pl
from jax.experimental.pallas import tpu as pltpu
from jax.sharding import PartitionSpec as P

B = 64
R = 3
G = 1024
HD = 64
GBLOCKS = 16
LANES = 2 * HD
QUAD = 4
NEAR = 3 + R
SUM_ROWS = 16
ID_BASE = 256
MIB = 1024 * 1024

AHEAD = 8

masked_score = -1e30


def dot_nt(a, b):
    return lax.dot_general(a, b, (((1,), (1,)), ((), ())), preferred_element_type=jnp.float32)


def dot_nn(a, b):
    return jnp.dot(a, b, preferred_element_type=jnp.float32)


def left_half(rows):
    return lax.broadcasted_iota(jnp.int32, (rows, LANES), 1) < HD


def swap_halves(value):
    return jnp.concatenate([value[:, HD:], value[:, :HD]], axis=1)


def pair_rows(value):
    half = value.shape[0] // 2
    left = left_half(half)
    top, low = value[:half], value[half:]
    return jnp.where(left, top, swap_halves(low)), jnp.where(left, swap_halves(top), low)


def project_first(half, history_ref, query_ref, key_ref, value_ref, ids_ref, out_ref):
    rows = history_ref.shape[0]
    weight = jnp.concatenate([key_ref[0], value_ref[0]], axis=1)
    both = dot_nn(history_ref[...], weight)
    pairs = pair_rows(both[:, :LANES].astype(jnp.bfloat16))
    turned = both[:, LANES:].T.astype(jnp.bfloat16)
    queries = project_half(history_ref, query_ref[0], 0, half)
    for j in range(2):
        out_ref[j, : rows // 2] = pairs[j]
        for i in range(rows // LANES):
            tile = turned[j * HD : (j + 1) * HD, i * LANES : (i + 1) * LANES]
            out_ref[j, rows // 2 + i * HD : rows // 2 + (i + 1) * HD] = tile
        out_ref[j, rows : rows + half] = queries[j]
        ids = ids_ref[j]
        blocks = ids.shape[0]
        at = rows + half
        out_ref[j, at:] = jnp.zeros((2 * blocks, LANES), jnp.bfloat16)
        out_ref[j, at : at + blocks, :R] = (ids % ID_BASE).astype(jnp.bfloat16)
        out_ref[j, at + blocks :, :R] = (ids // ID_BASE).astype(jnp.bfloat16)


def project_half(history_ref, weight, first, half):
    middle = history_ref.shape[0] // 2
    chosen = jnp.concatenate(
        [
            history_ref[first : first + half],
            history_ref[middle + first : middle + first + half],
        ],
        axis=0,
    )
    query = dot_nn(chosen, weight).astype(jnp.bfloat16)
    query = query * jnp.bfloat16(1.0 / math.sqrt(HD))
    found = []
    for pair in range(query.shape[1] // LANES):
        found.extend(pair_rows(query[:, pair * LANES : (pair + 1) * LANES]))
    return found


def project_later(first, history_ref, weight_ref, out_ref):
    found = project_half(history_ref, weight_ref[0], first, out_ref.shape[1])
    for j, value in enumerate(found):
        out_ref[j] = value


def project(history, qkv_weight, ids, chunks):
    rows, width = history.shape
    heads = qkv_weight.shape[2] // HD
    half = rows // 2 // chunks
    blocks = ids.shape[1]
    total = rows + half + 2 * blocks
    whole = pl.BlockSpec((rows, width), lambda i: (0, 0))
    params = pltpu.CompilerParams(vmem_limit_bytes=56 * MIB)
    first = pl.pallas_call(
        functools.partial(project_first, half),
        grid=(heads // 2,),
        in_specs=[
            whole,
            pl.BlockSpec((1, width, LANES), lambda i: (0, 0, i)),
            pl.BlockSpec((1, width, LANES), lambda i: (1, 0, i)),
            pl.BlockSpec((1, width, LANES), lambda i: (2, 0, i)),
            pl.BlockSpec((2, blocks, R), lambda i: (i, 0, 0)),
        ],
        out_specs=pl.BlockSpec((2, total, LANES), lambda i: (i, 0, 0)),
        out_shape=jax.ShapeDtypeStruct((heads, total, LANES), jnp.bfloat16),
        compiler_params=params,
        cost_estimate=pl.CostEstimate(
            flops=5 * rows * width * heads * HD, bytes_accessed=6 << 20, transcendentals=0
        ),
        name="project_first",
    )(history, qkv_weight, qkv_weight, qkv_weight, ids)
    later = []
    step = min(4, heads)
    for chunk in range(1, chunks):
        history, first = lax.optimization_barrier((history, first))
        later.append(
            pl.pallas_call(
                functools.partial(project_later, chunk * half),
                grid=(heads // step,),
                in_specs=[whole, pl.BlockSpec((1, width, step * HD), lambda i: (0, 0, i))],
                out_specs=pl.BlockSpec((step, half, LANES), lambda i: (i, 0, 0)),
                out_shape=jax.ShapeDtypeStruct((heads, half, LANES), jnp.bfloat16),
                compiler_params=params,
                cost_estimate=pl.CostEstimate(
                    flops=4 * half * width * heads * HD, bytes_accessed=4 << 20, transcendentals=0
                ),
                name="project_later",
            )(history, qkv_weight)
        )
    return first, later


def attend(plan, kv_ref, *refs):
    rows, blocks_dev, total_blocks, places, global_quads, mixed, carried, within = plan
    query_ref = None if within else refs[0]
    out_ref, keys_ref, values_ref, ids_vmem, ids_ref, sem = refs[-6:]
    sources = kv_ref.shape[0]
    half = rows // 2
    quads = len(places)
    group_blocks = quads * QUAD // sources
    if carried:
        group_blocks = blocks_dev
    per = out_ref.shape[3] // LANES
    pairs = rows // LANES
    left = left_half(B)
    zero = jnp.zeros((B, LANES), jnp.bfloat16)

    if carried:
        end = kv_ref.shape[1]
        for source in range(sources):
            low = kv_ref[source, end - 2 * blocks_dev : end - blocks_dev].astype(jnp.float32)
            high = kv_ref[source, end - blocks_dev :].astype(jnp.float32)
            ids_vmem[source * blocks_dev : (source + 1) * blocks_dev] = (
                low + high * ID_BASE
            ).astype(jnp.int32)
        copy = pltpu.make_async_copy(ids_vmem, ids_ref, sem)
    else:
        copy = pltpu.make_async_copy(refs[1], ids_ref, sem)
    copy.start()

    def build(source):
        packed = kv_ref[source, :half]
        wide = left_half(half)
        other = swap_halves(packed)
        keys_ref[source, :half] = jnp.where(wide, packed, other)
        keys_ref[source, half:] = jnp.where(wide, other, packed)
        for i in range(pairs):
            tile = kv_ref[source, half + i * HD : half + (i + 1) * HD]
            turned = swap_halves(tile)
            values_ref[source * 2 * pairs + 2 * i] = jnp.where(left, tile, turned)
            values_ref[source * 2 * pairs + 2 * i + 1] = jnp.where(left, turned, tile)

    def turned_values(source):
        tiles = [kv_ref[source, half + i * HD : half + (i + 1) * HD] for i in range(pairs)]
        ones = jnp.ones((SUM_ROWS, rows), jnp.bfloat16)
        return jnp.concatenate([jnp.concatenate(tiles, axis=1), ones], axis=0)

    def queries_of(quad):
        parts = []
        for i in range(2):
            if within:
                at = rows + (quad % per * 2 + i) * B
                packed = kv_ref[quad // per, at : at + B]
            else:
                at = (quad % per * 2 + i) * B
                packed = query_ref[quad // per, at : at + B]
            parts.append(jnp.where(left, packed, zero))
            parts.append(jnp.where(left, zero, packed))
        return parts

    def write(quad, acc):
        value = acc[:HD] / acc[HD : HD + 1]
        first, second = value[:, :LANES], value[:, LANES:]
        at = slice(quad % per * LANES, (quad % per + 1) * LANES)
        out_ref[quad // per, 0, :, at] = jnp.where(left, first, swap_halves(second)).astype(
            jnp.bfloat16
        )
        out_ref[quad // per, 1, :, at] = jnp.where(left, swap_halves(first), second).astype(
            jnp.bfloat16
        )

    def full_rows():
        query = jnp.concatenate([p for n in range(global_quads) for p in queries_of(n)], axis=0)

        def score(source):
            return dot_nt(keys_ref[source], query)

        def fold(source, scores, carry):
            top, acc = carry
            new_top = jnp.maximum(top, jnp.max(scores, 0, keepdims=True))
            weights = jnp.exp(scores - new_top).astype(jnp.bfloat16)
            acc = acc * jnp.exp(top - new_top) + dot_nn(turned_values(source), weights)
            return new_top, acc

        carry = (
            jnp.full((1, query.shape[0]), -jnp.inf, jnp.float32),
            jnp.zeros((HD + SUM_ROWS, query.shape[0]), jnp.float32),
        )
        if sources <= 8:
            build(0)
            scores = score(0)
            for source in range(sources):
                later = None
                if source + 1 < sources:
                    build(source + 1)
                    later = score(source + 1)
                carry = fold(source, scores, carry)
                scores = later
        else:
            lax.fori_loop(0, sources, lambda i, _: (build(i), 0)[1], 0)
            carry = lax.fori_loop(0, sources, lambda i, c: fold(i, score(i), c), carry)
        width = QUAD * B
        return [carry[1][:, n * width : (n + 1) * width] for n in range(global_quads)]

    def block_of(place):
        source, local = place
        if carried:
            return source * blocks_dev + local
        return source * blocks_dev + ids_ref[source * group_blocks, LANES - 1] + local

    def key_block(block):
        at = block % blocks_dev if isinstance(block, int) else lax.rem(block, blocks_dev)
        source = block // blocks_dev if isinstance(block, int) else lax.div(block, blocks_dev)
        return keys_ref[source, pl.ds(at * B if isinstance(at, int) else pl.multiple_of(at * B, B), B)]

    def near_scores(quad):
        parts = queries_of(quad)
        glob_scores = dot_nt(keys_ref[0], jnp.concatenate(parts, axis=0))
        lists = []
        column = lax.broadcasted_iota(jnp.int32, (1, QUAD * B), 1) // B
        low = high = None
        for b, (source, local) in enumerate(places[quad]):
            block = block_of((source, local))
            if carried:
                window = [max(block - 1, 0), block, min(block + 1, total_blocks - 1)]
                dead_low, dead_high = block - 1 < GBLOCKS, block + 1 >= total_blocks
                if dead_low:
                    low = column == b if low is None else low | (column == b)
                if dead_high:
                    high = column == b if high is None else high | (column == b)
            else:
                window = [
                    jnp.maximum(block - 1, 0),
                    block,
                    jnp.minimum(block + 1, total_blocks - 1),
                ]
                one = (column == b) & (block - 1 < GBLOCKS)
                two = (column == b) & (block + 1 >= total_blocks)
                low = one if low is None else low | one
                high = two if high is None else high | two
            lists.append(window + [ids_ref[source * group_blocks + local, r] for r in range(R)])
        near_keys = []
        for b in range(0, QUAD, 2):
            tiles = [
                jnp.where(left, key_block(lists[b][k]), key_block(lists[b + 1][k]))
                for k in range(NEAR)
            ]
            near_keys.append(jnp.concatenate(tiles, axis=0))
        blank = jnp.zeros((2 * B, LANES), jnp.bfloat16)
        diagonal = jnp.concatenate(
            [
                jnp.concatenate(parts[:2] + [blank], axis=0),
                jnp.concatenate([blank] + parts[2:], axis=0),
            ],
            axis=1,
        )
        scores = dot_nt(jnp.concatenate(near_keys, axis=1), diagonal)
        if low is not None or high is not None:
            before, after = scores[:B], scores[2 * B : 3 * B]
            if low is not None:
                before = jnp.where(low, masked_score, before)
            if high is not None:
                after = jnp.where(high, masked_score, after)
            scores = jnp.concatenate([before, scores[B : 2 * B], after, scores[3 * B :]], axis=0)
        return glob_scores, scores, lists

    def near_finish(glob_scores, scores, lists):
        top = jnp.maximum(
            jnp.max(glob_scores, 0, keepdims=True), jnp.max(scores, 0, keepdims=True)
        )
        glob_weights = jnp.exp(glob_scores - top).astype(jnp.bfloat16)
        weights = jnp.exp(scores - top).astype(jnp.bfloat16)
        near_values = [
            jnp.concatenate(
                [
                    jnp.where(left, values_ref[lists[b][k]], values_ref[lists[b][k + 1]])
                    for k in range(0, NEAR, 2)
                ],
                axis=1,
            )
            for b in range(QUAD)
        ]
        near_values.append(jnp.ones((SUM_ROWS, NEAR * B), jnp.bfloat16))
        near = dot_nn(jnp.concatenate(near_values, axis=0), weights)
        own = jnp.concatenate(
            [
                jnp.where(left, near[:HD, :LANES], near[HD : 2 * HD, :LANES]),
                jnp.where(left, near[2 * HD : 3 * HD, LANES:], near[3 * HD : 4 * HD, LANES:]),
            ],
            axis=1,
        )
        return dot_nn(turned_values(0), glob_weights) + jnp.concatenate(
            [own, near[QUAD * HD :]], axis=0
        )

    glob = full_rows()
    copy.wait()
    if not mixed:
        for quad in range(global_quads):
            write(quad, glob[quad])
    first = 0 if mixed else global_quads
    ready = [near_scores(quad) for quad in range(first, min(first + AHEAD, quads))]
    for quad in range(first, quads):
        if quad + AHEAD < quads:
            ready.append(near_scores(quad + AHEAD))
        acc = near_finish(*ready[quad - first])
        if quad < global_quads:
            column = lax.broadcasted_iota(jnp.int32, (1, QUAD * B), 1) // B
            own = functools.reduce(
                jnp.logical_or,
                [(column == b) & (block_of(p) < GBLOCKS) for b, p in enumerate(places[quad])],
            )
            acc = jnp.where(own, glob[quad], acc)
        write(quad, acc)


def attention(operands, plan, per, limit):
    rows, blocks_dev, _, places = plan[:4]
    quads = len(places)
    key_value = operands[0]
    sources = key_value.shape[0]
    total = sources * rows
    pairs = QUAD * B * (quads * (G + NEAR * B) + total)
    id_rows = sources * blocks_dev if plan[6] else quads * QUAD
    return pl.pallas_call(
        functools.partial(attend, plan),
        out_shape=jax.ShapeDtypeStruct((quads // per, 2, HD, per * LANES), jnp.bfloat16),
        scratch_shapes=[
            pltpu.VMEM((sources, rows, LANES), jnp.bfloat16),
            pltpu.VMEM((total // B, HD, LANES), jnp.bfloat16),
            pltpu.VMEM((id_rows, LANES), jnp.int32),
            pltpu.SMEM((id_rows, LANES), jnp.int32),
            pltpu.SemaphoreType.DMA,
        ],
        compiler_params=pltpu.CompilerParams(vmem_limit_bytes=limit),
        cost_estimate=pl.CostEstimate(
            flops=16 * HD * pairs, bytes_accessed=4 << 20, transcendentals=pairs
        ),
        name="attend",
    )(*operands)


def project_out(head_count, own_ref, turned_ref, here_ref, there_ref, *refs):
    out_ref = refs[-1]
    axis = turned_ref.shape[0] // head_count
    total = None
    for weight_ref, at in ((here_ref, own_ref[0]), (there_ref, 1 - own_ref[0])):
        heads = [turned_ref[h * axis + at] for h in range(head_count)]
        value = lax.dot_general(
            jnp.concatenate(heads, axis=0),
            weight_ref[...],
            (((0,), (0,)), ((), ())),
            preferred_element_type=jnp.float32,
        )
        total = value if total is None else total + value
    out_ref[...] = total.astype(jnp.bfloat16)


def output_rows(turned, here, there, head_count, chunk, chunks, before):
    rows = turned.shape[2]
    width = here.shape[1]
    return pl.pallas_call(
        functools.partial(project_out, head_count),
        grid_spec=pltpu.PrefetchScalarGridSpec(
            num_scalar_prefetch=1,
            grid=(1,),
            in_specs=[
                pl.BlockSpec(turned.shape, lambda i, _: (0, 0, 0)),
                pl.BlockSpec(here.shape, lambda i, _: (0, 0)),
                pl.BlockSpec(there.shape, lambda i, _: (0, 0)),
            ]
            + [pl.BlockSpec(memory_space=pl.ANY)] * len(before),
            out_specs=pl.BlockSpec((rows, width), lambda i, _: (chunk, 0)),
        ),
        out_shape=jax.ShapeDtypeStruct((rows * chunks, width), jnp.bfloat16),
        input_output_aliases={4: 0} if before else {},
        compiler_params=pltpu.CompilerParams(vmem_limit_bytes=20 * MIB),
        cost_estimate=pl.CostEstimate(
            flops=4 * rows * width * here.shape[0], bytes_accessed=3 << 20, transcendentals=0
        ),
        name="project_out",
    )(lax.axis_index("head").reshape(1), turned, here, there, *before)


def shards(history, qkv_weight, out_weight, rand_blocks):
    tok_rows = history.shape[0]
    head_count = qkv_weight.shape[2] // HD
    seq_count = lax.axis_size("seq")
    blocks_dev = tok_rows // B
    total_blocks = blocks_dev * seq_count
    group_count = seq_count // head_count
    seq_at = lax.axis_index("seq")
    direct = group_count == 1 and lax.axis_size("head") == 2
    chunks = 2 if direct else 1
    first, later = project(history, qkv_weight, rand_blocks, chunks)
    half = tok_rows // 2 // chunks

    if direct:
        first = lax.all_to_all(first, "seq", 0, 0, tiled=True)
        there = lax.ppermute(out_weight, "head", [(0, 1), (1, 0)])
        per = half // (2 * B)
        outs = []
        for chunk in range(chunks):
            operands = [first]
            if chunk > 0:
                query, first = lax.optimization_barrier((later[chunk - 1], first))
                query = lax.all_to_all(query, "seq", 0, 0, tiled=True)
                query, outs[-1] = lax.optimization_barrier((query, outs[-1]))
                operands.append(query)
            places = [
                [
                    (
                        n // per,
                        x * (blocks_dev // 2) + chunk * 2 * per + 2 * (n % per) + i,
                    )
                    for i in range(2)
                    for x in range(2)
                ]
                for n in range(seq_count * per)
            ]
            plan = (tok_rows, blocks_dev, total_blocks, places, per, False, True, chunk == 0)
            out = attention(operands, plan, per, 36 * MIB)
            outs.append(out.reshape(2 * seq_count, HD, half))
        outs = [lax.all_to_all(out, ("seq", "head"), 0, 0, tiled=True) for out in outs]
        result = []
        for chunk in range(chunks):
            operands = (outs[chunk], out_weight, there)
            result = [output_rows(*operands, head_count, chunk, chunks, result)]
        return result[0]

    key_value = lax.all_gather(first[:, :tok_rows], "seq")
    key_value = lax.dynamic_index_in_dim(key_value, seq_at // group_count, 1, False)
    group_blocks = blocks_dev // group_count
    blocks = seq_count * group_blocks
    query = first[:, tok_rows : tok_rows + half]
    query = query.reshape(head_count, half, 2, HD).transpose(0, 2, 1, 3)
    query = lax.all_to_all(query.reshape(seq_count, -1, HD), "seq", 0, 0, tiled=True)
    query = query.reshape(blocks // QUAD, 2, 2, B, HD).transpose(0, 1, 3, 2, 4)
    query = query.reshape(blocks // QUAD, 2 * B, LANES)
    ids = rand_blocks.reshape(seq_count, group_blocks, R)
    ids = lax.all_to_all(ids, "seq", 0, 0, tiled=True).reshape(blocks, R)
    ids = jnp.pad(ids, ((0, 0), (0, LANES - R)))
    offset = seq_at % group_count * group_blocks
    ids = ids.at[:, LANES - 1].set(offset)
    places = [
        [((n * QUAD + b) // group_blocks, (n * QUAD + b) % group_blocks) for b in range(QUAD)]
        for n in range(blocks // QUAD)
    ]
    global_quads = -(-GBLOCKS // group_count // QUAD)
    plan = (tok_rows, blocks_dev, total_blocks, places, global_quads, True, False, False)
    out = attention([key_value, query, ids], plan, 1, 56 * MIB)
    out = out.reshape(blocks // QUAD, 2, HD, 2, B).transpose(0, 3, 1, 4, 2)
    out = lax.all_to_all(out.reshape(seq_count, -1, HD), "seq", 0, 0, tiled=True)
    attn = out.reshape(head_count, tok_rows, HD).transpose(1, 0, 2)
    return lax.psum_scatter(
        jnp.dot(
            attn.reshape(tok_rows, head_count * HD),
            out_weight,
            preferred_element_type=jnp.float32,
        ).astype(jnp.bfloat16),
        "head",
        scatter_dimension=0,
        tiled=True,
    )


def solution(mesh):
    placed = (
        P(("groups", "seq"), None),
        P(None, None, "head"),
        P("head", None),
        P("head", ("groups", "seq"), None),
    )
    return jax.shard_map(
        shards,
        mesh=mesh,
        in_specs=placed,
        out_specs=P(("groups", "seq", "head"), None),
        check_vma=False,
    )
```

```python
import functools
import math

import jax
import jax.numpy as jnp
from jax import lax
from jax.experimental import pallas as pl
from jax.experimental.pallas import tpu as pltpu
from jax.sharding import PartitionSpec as P

B = 64
R = 3
G = 1024
HD = 64
GBLOCKS = 16
LANES = 2 * HD
QUAD = 4
NEAR = 3 + R
SUM_ROWS = 16
ID_BASE = 256
ID_ROWS = 16
MIB = 1024 * 1024

AHEAD = 8

masked_score = -1e30


def dot_nt(a, b):
    return lax.dot_general(a, b, (((1,), (1,)), ((), ())), preferred_element_type=jnp.float32)


def dot_nn(a, b):
    return jnp.dot(a, b, preferred_element_type=jnp.float32)


def left_half(rows):
    return lax.broadcasted_iota(jnp.int32, (rows, LANES), 1) < HD


def swap_halves(value):
    return jnp.concatenate([value[:, HD:], value[:, :HD]], axis=1)


def pair_rows(value):
    half = value.shape[0] // 2
    left = left_half(half)
    top, low = value[:half], value[half:]
    return jnp.where(left, top, swap_halves(low)), jnp.where(left, swap_halves(top), low)


def project_first(half, history_hbm, weight_hbm, ids_ref, out_hbm, history_ref, weight_ref, out_ref, sems):
    rows = history_ref.shape[0]
    heads = out_ref.shape[0]
    pairs = heads // 2
    loads = [pltpu.make_async_copy(history_hbm, history_ref, sems.at[0])]
    for pair in range(pairs):
        at = (slice(None), slice(None), pl.ds(pair * LANES, LANES))
        loads.append(
            pltpu.make_async_copy(weight_hbm.at[at], weight_ref.at[at], sems.at[1 + pair])
        )
    stores = [
        pltpu.make_async_copy(
            out_ref.at[pl.ds(2 * pair, 2)], out_hbm.at[pl.ds(2 * pair, 2)], sems.at[1 + pairs + pair]
        )
        for pair in range(pairs)
    ]
    for load in loads:
        load.start()
    loads[0].wait()
    for pair in range(pairs):
        loads[1 + pair].wait()
        lanes = slice(pair * LANES, (pair + 1) * LANES)
        weight = jnp.concatenate([weight_ref[1, :, lanes], weight_ref[2, :, lanes]], axis=1)
        both = dot_nn(history_ref[...], weight)
        keys = pair_rows(both[:, :LANES].astype(jnp.bfloat16))
        turned = both[:, LANES:].T.astype(jnp.bfloat16)
        queries = project_half(history_ref, weight_ref[0, :, lanes], 0, half)
        for j in range(2):
            head = 2 * pair + j
            out_ref[head, : rows // 2] = keys[j]
            for i in range(rows // LANES):
                tile = turned[j * HD : (j + 1) * HD, i * LANES : (i + 1) * LANES]
                out_ref[head, rows // 2 + i * HD : rows // 2 + (i + 1) * HD] = tile
            out_ref[head, rows : rows + half] = queries[j]
            out_ref[head, rows + half :] = jnp.zeros((ID_ROWS, LANES), jnp.bfloat16)
            ids = [ids_ref[r, head : head + 1] for r in range(R)]
            ids = [v % ID_BASE for v in ids] + [v // ID_BASE for v in ids]
            ids.append(jnp.zeros((ID_ROWS - 2 * R, ids_ref.shape[2]), jnp.int32))
            ids = jnp.concatenate(ids, axis=0).astype(jnp.float32).astype(jnp.bfloat16)
            out_ref[head, rows + half :, : ids.shape[1]] = ids
        stores[pair].start()
    for store in stores:
        store.wait()


def project_half(history_ref, weight, first, half):
    middle = history_ref.shape[0] // 2
    chosen = jnp.concatenate(
        [
            history_ref[first : first + half],
            history_ref[middle + first : middle + first + half],
        ],
        axis=0,
    )
    query = dot_nn(chosen, weight).astype(jnp.bfloat16)
    query = query * jnp.bfloat16(1.0 / math.sqrt(HD))
    found = []
    for pair in range(query.shape[1] // LANES):
        found.extend(pair_rows(query[:, pair * LANES : (pair + 1) * LANES]))
    return found


def project_later(first, history_ref, weight_ref, out_ref):
    found = project_half(history_ref, weight_ref[0], first, out_ref.shape[1])
    for j, value in enumerate(found):
        out_ref[j] = value


def project(history, qkv_weight, ids, chunks):
    rows, width = history.shape
    heads = qkv_weight.shape[2] // HD
    half = rows // 2 // chunks
    total = rows + half + ID_ROWS
    whole = pl.BlockSpec((rows, width), lambda i: (0, 0))
    params = pltpu.CompilerParams(vmem_limit_bytes=56 * MIB)
    first = pl.pallas_call(
        functools.partial(project_first, half),
        in_specs=[
            pl.BlockSpec(memory_space=pltpu.HBM),
            pl.BlockSpec(memory_space=pltpu.HBM),
            pl.BlockSpec(memory_space=pltpu.VMEM),
        ],
        out_specs=pl.BlockSpec(memory_space=pltpu.HBM),
        out_shape=jax.ShapeDtypeStruct((heads, total, LANES), jnp.bfloat16),
        scratch_shapes=[
            pltpu.VMEM(history.shape, jnp.bfloat16),
            pltpu.VMEM(qkv_weight.shape, jnp.bfloat16),
            pltpu.VMEM((heads, total, LANES), jnp.bfloat16),
            pltpu.SemaphoreType.DMA((1 + heads,)),
        ],
        compiler_params=params,
        cost_estimate=pl.CostEstimate(
            flops=5 * rows * width * heads * HD, bytes_accessed=6 << 20, transcendentals=0
        ),
        name="project_first",
    )(history, qkv_weight, ids.transpose(2, 0, 1))
    later = []
    step = min(4, heads)
    for chunk in range(1, chunks):
        history, first = lax.optimization_barrier((history, first))
        later.append(
            pl.pallas_call(
                functools.partial(project_later, chunk * half),
                grid=(heads // step,),
                in_specs=[whole, pl.BlockSpec((1, width, step * HD), lambda i: (0, 0, i))],
                out_specs=pl.BlockSpec((step, half, LANES), lambda i: (i, 0, 0)),
                out_shape=jax.ShapeDtypeStruct((heads, half, LANES), jnp.bfloat16),
                compiler_params=params,
                cost_estimate=pl.CostEstimate(
                    flops=4 * half * width * heads * HD, bytes_accessed=4 << 20, transcendentals=0
                ),
                name="project_later",
            )(history, qkv_weight)
        )
    return first, later


def attend(plan, *refs):
    rows, blocks_dev, total_blocks, places, global_quads, mixed, carried, within = plan
    kv_ref, keys_ref, values_ref, turned_ref, ids_vmem, ids_ref, sems = refs[-7:]
    out_hbm, query_ref = refs[-9:-7]
    kv_hbm = refs[0]
    sources = kv_ref.shape[0]
    half = rows // 2
    quads = len(places)
    group_blocks = blocks_dev if carried else quads * QUAD // sources
    per = turned_ref.shape[3] // LANES
    pairs = rows // LANES
    left = left_half(B)
    zero = jnp.zeros((B, LANES), jnp.bfloat16)
    lead, rest = pl.ds(0, 1), pl.ds(1, sources - 1)
    loads = [
        pltpu.make_async_copy(kv_hbm.at[lead], kv_ref.at[lead], sems.at[0]),
        pltpu.make_async_copy(kv_hbm.at[rest], kv_ref.at[rest], sems.at[1]),
    ]
    if not within:
        loads.insert(1, pltpu.make_async_copy(refs[1], query_ref, sems.at[2]))
    if carried:
        ids_copy = pltpu.make_async_copy(ids_vmem, ids_ref, sems.at[3])
    else:
        ids_copy = pltpu.make_async_copy(refs[2], ids_ref, sems.at[3])
        loads.append(ids_copy)
    for load in loads:
        load.start()
    stores = [
        pltpu.make_async_copy(
            turned_ref.at[pl.ds(i, 1)], out_hbm.at[pl.ds(i, 1)], sems.at[4 + i]
        )
        for i in range(quads // per)
    ]

    def spread_ids():
        end = kv_ref.shape[1]
        for source in range(sources):
            ids_vmem[source * ID_ROWS : (source + 1) * ID_ROWS] = (
                kv_ref[source, end - ID_ROWS :].astype(jnp.float32).astype(jnp.int32)
            )
        ids_copy.start()

    def rand_of(source, local):
        if carried:
            at = source * ID_ROWS
            return [
                ids_ref[at + r, local] + ids_ref[at + R + r, local] * ID_BASE for r in range(R)
            ]
        return [ids_ref[source * group_blocks + local, r] for r in range(R)]

    def build(source):
        packed = kv_ref[source, :half]
        wide = left_half(half)
        other = swap_halves(packed)
        keys_ref[source, :half] = jnp.where(wide, packed, other)
        keys_ref[source, half:] = jnp.where(wide, other, packed)
        for i in range(pairs):
            tile = kv_ref[source, half + i * HD : half + (i + 1) * HD]
            turned = swap_halves(tile)
            values_ref[source * 2 * pairs + 2 * i] = jnp.where(left, tile, turned)
            values_ref[source * 2 * pairs + 2 * i + 1] = jnp.where(left, turned, tile)

    def turned_values(source):
        tiles = [kv_ref[source, half + i * HD : half + (i + 1) * HD] for i in range(pairs)]
        ones = jnp.ones((SUM_ROWS, rows), jnp.bfloat16)
        return jnp.concatenate([jnp.concatenate(tiles, axis=1), ones], axis=0)

    def queries_of(quad):
        parts = []
        for i in range(2):
            if within:
                at = rows + (quad % per * 2 + i) * B
                packed = kv_ref[quad // per, at : at + B]
            else:
                at = (quad % per * 2 + i) * B
                packed = query_ref[quad // per, at : at + B]
            parts.append(jnp.where(left, packed, zero))
            parts.append(jnp.where(left, zero, packed))
        return parts

    def write(quad, acc):
        value = acc[:HD] / acc[HD : HD + 1]
        first, second = value[:, :LANES], value[:, LANES:]
        at = slice(quad % per * LANES, (quad % per + 1) * LANES)
        turned_ref[quad // per, 0, :, at] = jnp.where(left, first, swap_halves(second)).astype(
            jnp.bfloat16
        )
        turned_ref[quad // per, 1, :, at] = jnp.where(left, swap_halves(first), second).astype(
            jnp.bfloat16
        )
        if quad % per == per - 1:
            stores[quad // per].start()

    def full_rows():
        query = jnp.concatenate([p for n in range(global_quads) for p in queries_of(n)], axis=0)

        def score(source):
            return dot_nt(keys_ref[source], query)

        def fold(source, scores, carry):
            top, acc = carry
            new_top = jnp.maximum(top, jnp.max(scores, 0, keepdims=True))
            weights = jnp.exp(scores - new_top).astype(jnp.bfloat16)
            acc = acc * jnp.exp(top - new_top) + dot_nn(turned_values(source), weights)
            return new_top, acc

        carry = (
            jnp.full((1, query.shape[0]), -jnp.inf, jnp.float32),
            jnp.zeros((HD + SUM_ROWS, query.shape[0]), jnp.float32),
        )
        if sources <= 8:
            build(0)
            scores = score(0)
            for load in loads[waited:]:
                load.wait()
            if carried:
                spread_ids()
            for source in range(sources):
                later = None
                if source + 1 < sources:
                    build(source + 1)
                    later = score(source + 1)
                carry = fold(source, scores, carry)
                scores = later
        else:
            for load in loads[waited:]:
                load.wait()
            if carried:
                spread_ids()
            lax.fori_loop(0, sources, lambda i, _: (build(i), 0)[1], 0)
            carry = lax.fori_loop(0, sources, lambda i, c: fold(i, score(i), c), carry)
        width = QUAD * B
        return [carry[1][:, n * width : (n + 1) * width] for n in range(global_quads)]

    def block_of(place):
        source, local = place
        if carried:
            return source * blocks_dev + local
        return source * blocks_dev + ids_ref[source * group_blocks, LANES - 1] + local

    def key_block(block):
        at = block % blocks_dev if isinstance(block, int) else lax.rem(block, blocks_dev)
        source = block // blocks_dev if isinstance(block, int) else lax.div(block, blocks_dev)
        return keys_ref[source, pl.ds(at * B if isinstance(at, int) else pl.multiple_of(at * B, B), B)]

    def near_scores(quad):
        parts = queries_of(quad)
        glob_scores = dot_nt(keys_ref[0], jnp.concatenate(parts, axis=0))
        lists = []
        column = lax.broadcasted_iota(jnp.int32, (1, QUAD * B), 1) // B
        low = high = None
        for b, (source, local) in enumerate(places[quad]):
            block = block_of((source, local))
            if carried:
                window = [max(block - 1, 0), block, min(block + 1, total_blocks - 1)]
                dead_low, dead_high = block - 1 < GBLOCKS, block + 1 >= total_blocks
                if dead_low:
                    low = column == b if low is None else low | (column == b)
                if dead_high:
                    high = column == b if high is None else high | (column == b)
            else:
                window = [
                    jnp.maximum(block - 1, 0),
                    block,
                    jnp.minimum(block + 1, total_blocks - 1),
                ]
                one = (column == b) & (block - 1 < GBLOCKS)
                two = (column == b) & (block + 1 >= total_blocks)
                low = one if low is None else low | one
                high = two if high is None else high | two
            lists.append(window + rand_of(source, local))
        near_keys = []
        for b in range(0, QUAD, 2):
            tiles = [
                jnp.where(left, key_block(lists[b][k]), key_block(lists[b + 1][k]))
                for k in range(NEAR)
            ]
            near_keys.append(jnp.concatenate(tiles, axis=0))
        blank = jnp.zeros((2 * B, LANES), jnp.bfloat16)
        diagonal = jnp.concatenate(
            [
                jnp.concatenate(parts[:2] + [blank], axis=0),
                jnp.concatenate([blank] + parts[2:], axis=0),
            ],
            axis=1,
        )
        scores = dot_nt(jnp.concatenate(near_keys, axis=1), diagonal)
        if low is not None or high is not None:
            before, after = scores[:B], scores[2 * B : 3 * B]
            if low is not None:
                before = jnp.where(low, masked_score, before)
            if high is not None:
                after = jnp.where(high, masked_score, after)
            scores = jnp.concatenate([before, scores[B : 2 * B], after, scores[3 * B :]], axis=0)
        return glob_scores, scores, lists

    def near_finish(glob_scores, scores, lists):
        top = jnp.maximum(
            jnp.max(glob_scores, 0, keepdims=True), jnp.max(scores, 0, keepdims=True)
        )
        glob_weights = jnp.exp(glob_scores - top).astype(jnp.bfloat16)
        weights = jnp.exp(scores - top).astype(jnp.bfloat16)
        near_values = [
            jnp.concatenate(
                [
                    jnp.where(left, values_ref[lists[b][k]], values_ref[lists[b][k + 1]])
                    for k in range(0, NEAR, 2)
                ],
                axis=1,
            )
            for b in range(QUAD)
        ]
        near_values.append(jnp.ones((SUM_ROWS, NEAR * B), jnp.bfloat16))
        near = dot_nn(jnp.concatenate(near_values, axis=0), weights)
        own = jnp.concatenate(
            [
                jnp.where(left, near[:HD, :LANES], near[HD : 2 * HD, :LANES]),
                jnp.where(left, near[2 * HD : 3 * HD, LANES:], near[3 * HD : 4 * HD, LANES:]),
            ],
            axis=1,
        )
        return dot_nn(turned_values(0), glob_weights) + jnp.concatenate(
            [own, near[QUAD * HD :]], axis=0
        )

    waited = 1 if within else 2
    for load in loads[:waited]:
        load.wait()
    glob = full_rows()
    if carried:
        ids_copy.wait()
    if not mixed:
        for quad in range(global_quads):
            write(quad, glob[quad])
    first = 0 if mixed else global_quads
    ready = [near_scores(quad) for quad in range(first, min(first + AHEAD, quads))]
    for quad in range(first, quads):
        if quad + AHEAD < quads:
            ready.append(near_scores(quad + AHEAD))
        acc = near_finish(*ready[quad - first])
        if quad < global_quads:
            column = lax.broadcasted_iota(jnp.int32, (1, QUAD * B), 1) // B
            own = functools.reduce(
                jnp.logical_or,
                [(column == b) & (block_of(p) < GBLOCKS) for b, p in enumerate(places[quad])],
            )
            acc = jnp.where(own, glob[quad], acc)
        write(quad, acc)
    for store in stores:
        store.wait()


def attention(operands, plan, per, limit):
    rows, blocks_dev, _, places = plan[:4]
    quads = len(places)
    key_value = operands[0]
    sources = key_value.shape[0]
    total = sources * rows
    pairs = QUAD * B * (quads * (G + NEAR * B) + total)
    id_rows = sources * ID_ROWS if plan[6] else quads * QUAD
    hbm = pl.BlockSpec(memory_space=pltpu.HBM)
    shape = (quads // per, 2, HD, per * LANES)
    query_shape = (8, LANES) if plan[7] else operands[1].shape
    return pl.pallas_call(
        functools.partial(attend, plan),
        in_specs=[hbm] * len(operands),
        out_specs=hbm,
        out_shape=jax.ShapeDtypeStruct(shape, jnp.bfloat16),
        scratch_shapes=[
            pltpu.VMEM(query_shape, jnp.bfloat16),
            pltpu.VMEM(key_value.shape, jnp.bfloat16),
            pltpu.VMEM((sources, rows, LANES), jnp.bfloat16),
            pltpu.VMEM((total // B, HD, LANES), jnp.bfloat16),
            pltpu.VMEM(shape, jnp.bfloat16),
            pltpu.VMEM((id_rows, LANES), jnp.int32),
            pltpu.SMEM((id_rows, LANES), jnp.int32),
            pltpu.SemaphoreType.DMA((4 + quads // per,)),
        ],
        compiler_params=pltpu.CompilerParams(vmem_limit_bytes=limit),
        cost_estimate=pl.CostEstimate(
            flops=16 * HD * pairs, bytes_accessed=4 << 20, transcendentals=pairs
        ),
        name="attend",
    )(*operands)


def project_out(head_count, own_ref, turned_ref, here_ref, there_ref, *refs):
    out_ref = refs[-1]
    axis = turned_ref.shape[0] // head_count
    total = None
    for weight_ref, at in ((here_ref, own_ref[0]), (there_ref, 1 - own_ref[0])):
        heads = [turned_ref[h * axis + at] for h in range(head_count)]
        value = lax.dot_general(
            jnp.concatenate(heads, axis=0),
            weight_ref[...],
            (((0,), (0,)), ((), ())),
            preferred_element_type=jnp.float32,
        )
        total = value if total is None else total + value
    out_ref[...] = total.astype(jnp.bfloat16)


def output_rows(turned, here, there, head_count, chunk, chunks, before):
    rows = turned.shape[2]
    width = here.shape[1]
    return pl.pallas_call(
        functools.partial(project_out, head_count),
        grid_spec=pltpu.PrefetchScalarGridSpec(
            num_scalar_prefetch=1,
            grid=(1,),
            in_specs=[
                pl.BlockSpec(turned.shape, lambda i, _: (0, 0, 0)),
                pl.BlockSpec(here.shape, lambda i, _: (0, 0)),
                pl.BlockSpec(there.shape, lambda i, _: (0, 0)),
            ]
            + [pl.BlockSpec(memory_space=pl.ANY)] * len(before),
            out_specs=pl.BlockSpec((rows, width), lambda i, _: (chunk, 0)),
        ),
        out_shape=jax.ShapeDtypeStruct((rows * chunks, width), jnp.bfloat16),
        input_output_aliases={4: 0} if before else {},
        compiler_params=pltpu.CompilerParams(vmem_limit_bytes=20 * MIB),
        cost_estimate=pl.CostEstimate(
            flops=4 * rows * width * here.shape[0], bytes_accessed=3 << 20, transcendentals=0
        ),
        name="project_out",
    )(lax.axis_index("head").reshape(1), turned, here, there, *before)


def shards(history, qkv_weight, out_weight, rand_blocks):
    tok_rows = history.shape[0]
    head_count = qkv_weight.shape[2] // HD
    seq_count = lax.axis_size("seq")
    blocks_dev = tok_rows // B
    total_blocks = blocks_dev * seq_count
    group_count = seq_count // head_count
    seq_at = lax.axis_index("seq")
    direct = group_count == 1 and lax.axis_size("head") == 2
    chunks = 2 if direct else 1
    first, later = project(history, qkv_weight, rand_blocks, chunks)
    half = tok_rows // 2 // chunks

    if direct:
        first = lax.all_to_all(first, "seq", 0, 0, tiled=True)
        there = lax.ppermute(out_weight, "head", [(0, 1), (1, 0)])
        per = half // (2 * B)
        outs = []
        for chunk in range(chunks):
            operands = [first]
            if chunk > 0:
                query, first = lax.optimization_barrier((later[chunk - 1], first))
                query = lax.all_to_all(query, "seq", 0, 0, tiled=True)
                query, outs[-1] = lax.optimization_barrier((query, outs[-1]))
                operands.append(query)
            places = [
                [
                    (
                        n // per,
                        x * (blocks_dev // 2) + chunk * 2 * per + 2 * (n % per) + i,
                    )
                    for i in range(2)
                    for x in range(2)
                ]
                for n in range(seq_count * per)
            ]
            plan = (tok_rows, blocks_dev, total_blocks, places, per, False, True, chunk == 0)
            out = attention(operands, plan, per, 48 * MIB)
            outs.append(out.reshape(2 * seq_count, HD, half))
        outs = [lax.all_to_all(out, ("seq", "head"), 0, 0, tiled=True) for out in outs]
        result = []
        for chunk in range(chunks):
            operands = (outs[chunk], out_weight, there)
            result = [output_rows(*operands, head_count, chunk, chunks, result)]
        return result[0]

    key_value = lax.all_gather(first[:, :tok_rows], "seq")
    key_value = lax.dynamic_index_in_dim(key_value, seq_at // group_count, 1, False)
    group_blocks = blocks_dev // group_count
    blocks = seq_count * group_blocks
    query = first[:, tok_rows : tok_rows + half]
    query = query.reshape(head_count, half, 2, HD).transpose(0, 2, 1, 3)
    query = lax.all_to_all(query.reshape(seq_count, -1, HD), "seq", 0, 0, tiled=True)
    query = query.reshape(blocks // QUAD, 2, 2, B, HD).transpose(0, 1, 3, 2, 4)
    query = query.reshape(blocks // QUAD, 2 * B, LANES)
    ids = rand_blocks.reshape(seq_count, group_blocks, R)
    ids = lax.all_to_all(ids, "seq", 0, 0, tiled=True).reshape(blocks, R)
    ids = jnp.pad(ids, ((0, 0), (0, LANES - R)))
    offset = seq_at % group_count * group_blocks
    ids = ids.at[:, LANES - 1].set(offset)
    places = [
        [((n * QUAD + b) // group_blocks, (n * QUAD + b) % group_blocks) for b in range(QUAD)]
        for n in range(blocks // QUAD)
    ]
    global_quads = -(-GBLOCKS // group_count // QUAD)
    plan = (tok_rows, blocks_dev, total_blocks, places, global_quads, True, False, False)
    out = attention([key_value, query, ids], plan, 1, 56 * MIB)
    out = out.reshape(blocks // QUAD, 2, HD, 2, B).transpose(0, 3, 1, 4, 2)
    out = lax.all_to_all(out.reshape(seq_count, -1, HD), "seq", 0, 0, tiled=True)
    attn = out.reshape(head_count, tok_rows, HD).transpose(1, 0, 2)
    return lax.psum_scatter(
        jnp.dot(
            attn.reshape(tok_rows, head_count * HD),
            out_weight,
            preferred_element_type=jnp.float32,
        ).astype(jnp.bfloat16),
        "head",
        scatter_dimension=0,
        tiled=True,
    )


def solution(mesh):
    placed = (
        P(("groups", "seq"), None),
        P(None, None, "head"),
        P("head", None),
        P("head", ("groups", "seq"), None),
    )
    return jax.shard_map(
        shards,
        mesh=mesh,
        in_specs=placed,
        out_specs=P(("groups", "seq", "head"), None),
        check_vma=False,
    )
```

```python
import functools
import math

import jax
import jax.numpy as jnp
from jax import lax
from jax.experimental import pallas as pl
from jax.experimental.pallas import tpu as pltpu
from jax.sharding import PartitionSpec as P

B = 64
R = 3
G = 1024
HD = 64
GBLOCKS = 16
LANES = 2 * HD
QUAD = 4
NEAR = 3 + R
SUM_ROWS = 16
ID_BASE = 256
ID_ROWS = 16
MIB = 1024 * 1024

AHEAD = 8

masked_score = -1e30


def dot_nt(a, b):
    return lax.dot_general(a, b, (((1,), (1,)), ((), ())), preferred_element_type=jnp.float32)


def dot_nn(a, b):
    return jnp.dot(a, b, preferred_element_type=jnp.float32)


def left_half(rows):
    return lax.broadcasted_iota(jnp.int32, (rows, LANES), 1) < HD


def swap_halves(value):
    return jnp.concatenate([value[:, HD:], value[:, :HD]], axis=1)


def pair_rows(value):
    half = value.shape[0] // 2
    left = left_half(half)
    top, low = value[:half], value[half:]
    return jnp.where(left, top, swap_halves(low)), jnp.where(left, swap_halves(top), low)


def project_first(
    half, history_hbm, weight_hbm, ids_ref, out_hbm, history_ref, weight_ref, out_ref, sems
):
    rows = history_ref.shape[0]
    heads = out_ref.shape[0]
    step = min(4, heads)
    runs = heads // step
    width = step * HD
    loads = [pltpu.make_async_copy(history_hbm, history_ref, sems.at[0])]
    for run in range(runs):
        at = (slice(None), slice(None), pl.ds(run * width, width))
        loads.append(
            pltpu.make_async_copy(weight_hbm.at[at], weight_ref.at[at], sems.at[1 + run])
        )
    for load in loads:
        load.start()
    for head in range(heads):
        out_ref[head, rows + half :] = jnp.zeros((ID_ROWS, LANES), jnp.bfloat16)
        ids = [ids_ref[r, head : head + 1] for r in range(R)]
        ids = [v % ID_BASE for v in ids] + [v // ID_BASE for v in ids]
        ids.append(jnp.zeros((ID_ROWS - 2 * R, ids_ref.shape[2]), jnp.int32))
        ids = jnp.concatenate(ids, axis=0).astype(jnp.float32).astype(jnp.bfloat16)
        out_ref[head, rows + half :, : ids.shape[1]] = ids

    def product(unit):
        run, kind = unit
        lanes = slice(run * width, (run + 1) * width)
        if kind == 0:
            return dot_nn(history_ref[...], weight_ref[1, :, lanes])
        if kind == 1:
            return lax.dot_general(
                weight_ref[2, :, lanes],
                history_ref[...],
                (((0,), (1,)), ((), ())),
                preferred_element_type=jnp.float32,
            )
        return project_half(history_ref, weight_ref[0, :, lanes], 0, half)

    def place(unit, value):
        run, kind = unit
        value = value.astype(jnp.bfloat16)
        for head in range(run * step, (run + 1) * step):
            j = head - run * step
            if kind == 1:
                for i in range(rows // LANES):
                    tile = value[j * HD : (j + 1) * HD, i * LANES : (i + 1) * LANES]
                    out_ref[head, rows // 2 + i * HD : rows // 2 + (i + 1) * HD] = tile
            elif j % 2 == 0:
                pair = pair_rows(value[:, j * HD : (j + 2) * HD])
                at = 0 if kind == 0 else rows
                for k in range(2):
                    out_ref[head + k, at : at + pair[k].shape[0]] = pair[k]

    units = [(run, kind) for run in range(runs) for kind in range(3)]
    spans = [(0, rows // 2), (rows // 2, rows // 2), (rows, half + ID_ROWS)]
    stores = []
    for load in loads[:2]:
        load.wait()
    value = product(units[0])
    for n, unit in enumerate(units):
        later = None
        if n + 1 < len(units):
            if units[n + 1][0] > unit[0]:
                loads[1 + units[n + 1][0]].wait()
            later = product(units[n + 1])
        place(unit, value)
        at = (pl.ds(unit[0] * step, step), pl.ds(*spans[unit[1]]))
        stores.append(
            pltpu.make_async_copy(out_ref.at[at], out_hbm.at[at], sems.at[1 + runs + n])
        )
        stores[-1].start()
        value = later
    for store in stores:
        store.wait()


def project_half(history_ref, weight, first, half):
    middle = history_ref.shape[0] // 2
    chosen = jnp.concatenate(
        [
            history_ref[first : first + half],
            history_ref[middle + first : middle + first + half],
        ],
        axis=0,
    )
    return dot_nn(chosen, weight) * (1.0 / math.sqrt(HD))


def project_later(first, history_ref, weight_ref, out_ref):
    half = out_ref.shape[1]
    query = project_half(history_ref, weight_ref[0], first, half).astype(jnp.bfloat16)
    for j in range(0, out_ref.shape[0], 2):
        pair = pair_rows(query[:, j * HD : (j + 2) * HD])
        out_ref[j] = pair[0]
        out_ref[j + 1] = pair[1]


def project(history, qkv_weight, ids, chunks):
    rows, width = history.shape
    heads = qkv_weight.shape[2] // HD
    half = rows // 2 // chunks
    total = rows + half + ID_ROWS
    whole = pl.BlockSpec((rows, width), lambda i: (0, 0))
    params = pltpu.CompilerParams(vmem_limit_bytes=56 * MIB)
    first = pl.pallas_call(
        functools.partial(project_first, half),
        in_specs=[
            pl.BlockSpec(memory_space=pltpu.HBM),
            pl.BlockSpec(memory_space=pltpu.HBM),
            pl.BlockSpec(memory_space=pltpu.VMEM),
        ],
        out_specs=pl.BlockSpec(memory_space=pltpu.HBM),
        out_shape=jax.ShapeDtypeStruct((heads, total, LANES), jnp.bfloat16),
        scratch_shapes=[
            pltpu.VMEM(history.shape, jnp.bfloat16),
            pltpu.VMEM(qkv_weight.shape, jnp.bfloat16),
            pltpu.VMEM((heads, total, LANES), jnp.bfloat16),
            pltpu.SemaphoreType.DMA((1 + 2 * heads,)),
        ],
        compiler_params=params,
        cost_estimate=pl.CostEstimate(
            flops=5 * rows * width * heads * HD, bytes_accessed=6 << 20, transcendentals=0
        ),
        name="project_first",
    )(history, qkv_weight, ids.transpose(2, 0, 1))
    later = []
    step = min(4, heads)
    for chunk in range(1, chunks):
        history, first = lax.optimization_barrier((history, first))
        later.append(
            pl.pallas_call(
                functools.partial(project_later, chunk * half),
                grid=(heads // step,),
                in_specs=[whole, pl.BlockSpec((1, width, step * HD), lambda i: (0, 0, i))],
                out_specs=pl.BlockSpec((step, half, LANES), lambda i: (i, 0, 0)),
                out_shape=jax.ShapeDtypeStruct((heads, half, LANES), jnp.bfloat16),
                compiler_params=params,
                cost_estimate=pl.CostEstimate(
                    flops=4 * half * width * heads * HD, bytes_accessed=4 << 20, transcendentals=0
                ),
                name="project_later",
            )(history, qkv_weight)
        )
    return first, later


def attend(plan, *refs):
    rows, blocks_dev, total_blocks, places, global_quads, mixed, carried, within = plan
    kv_ref, keys_ref, values_ref, turned_ref, ids_vmem, ids_ref, sems = refs[-7:]
    out_hbm, query_ref = refs[-9:-7]
    kv_hbm = refs[0]
    sources = kv_ref.shape[0]
    half = rows // 2
    quads = len(places)
    group_blocks = blocks_dev if carried else quads * QUAD // sources
    per = turned_ref.shape[3] // LANES
    pairs = rows // LANES
    left = left_half(B)
    zero = jnp.zeros((B, LANES), jnp.bfloat16)
    lead, rest = pl.ds(0, 1), pl.ds(1, sources - 1)
    loads = [
        pltpu.make_async_copy(kv_hbm.at[lead], kv_ref.at[lead], sems.at[0]),
        pltpu.make_async_copy(kv_hbm.at[rest], kv_ref.at[rest], sems.at[1]),
    ]
    if not within:
        loads.insert(1, pltpu.make_async_copy(refs[1], query_ref, sems.at[2]))
    if carried:
        ids_copy = pltpu.make_async_copy(ids_vmem, ids_ref, sems.at[3])
    else:
        ids_copy = pltpu.make_async_copy(refs[2], ids_ref, sems.at[3])
        loads.append(ids_copy)
    for load in loads:
        load.start()
    stores = [
        pltpu.make_async_copy(
            turned_ref.at[pl.ds(i, 1)], out_hbm.at[pl.ds(i, 1)], sems.at[4 + i]
        )
        for i in range(quads // per)
    ]

    def spread_ids():
        end = kv_ref.shape[1]
        for source in range(sources):
            ids_vmem[source * ID_ROWS : (source + 1) * ID_ROWS] = (
                kv_ref[source, end - ID_ROWS :].astype(jnp.float32).astype(jnp.int32)
            )
        ids_copy.start()

    def rand_of(source, local):
        if carried:
            at = source * ID_ROWS
            return [
                ids_ref[at + r, local] + ids_ref[at + R + r, local] * ID_BASE for r in range(R)
            ]
        return [ids_ref[source * group_blocks + local, r] for r in range(R)]

    def build(source):
        packed = kv_ref[source, :half]
        wide = left_half(half)
        other = swap_halves(packed)
        keys_ref[source, :half] = jnp.where(wide, packed, other)
        keys_ref[source, half:] = jnp.where(wide, other, packed)
        for i in range(pairs):
            tile = kv_ref[source, half + i * HD : half + (i + 1) * HD]
            turned = swap_halves(tile)
            values_ref[source * 2 * pairs + 2 * i] = jnp.where(left, tile, turned)
            values_ref[source * 2 * pairs + 2 * i + 1] = jnp.where(left, turned, tile)

    def turned_values(source):
        tiles = [kv_ref[source, half + i * HD : half + (i + 1) * HD] for i in range(pairs)]
        ones = jnp.ones((SUM_ROWS, rows), jnp.bfloat16)
        return jnp.concatenate([jnp.concatenate(tiles, axis=1), ones], axis=0)

    def queries_of(quad):
        parts = []
        for i in range(2):
            if within:
                at = rows + (quad % per * 2 + i) * B
                packed = kv_ref[quad // per, at : at + B]
            else:
                at = (quad % per * 2 + i) * B
                packed = query_ref[quad // per, at : at + B]
            parts.append(jnp.where(left, packed, zero))
            parts.append(jnp.where(left, zero, packed))
        return parts

    def write(quad, acc):
        value = acc[:HD] / acc[HD : HD + 1]
        first, second = value[:, :LANES], value[:, LANES:]
        at = slice(quad % per * LANES, (quad % per + 1) * LANES)
        turned_ref[quad // per, 0, :, at] = jnp.where(left, first, swap_halves(second)).astype(
            jnp.bfloat16
        )
        turned_ref[quad // per, 1, :, at] = jnp.where(left, swap_halves(first), second).astype(
            jnp.bfloat16
        )
        if quad % per == per - 1:
            stores[quad // per].start()

    def full_rows():
        query = jnp.concatenate([p for n in range(global_quads) for p in queries_of(n)], axis=0)

        def score(source):
            return dot_nt(keys_ref[source], query)

        def fold(source, scores, carry):
            top, acc = carry
            new_top = jnp.maximum(top, jnp.max(scores, 0, keepdims=True))
            weights = jnp.exp(scores - new_top).astype(jnp.bfloat16)
            acc = acc * jnp.exp(top - new_top) + dot_nn(turned_values(source), weights)
            return new_top, acc

        carry = (
            jnp.full((1, query.shape[0]), -jnp.inf, jnp.float32),
            jnp.zeros((HD + SUM_ROWS, query.shape[0]), jnp.float32),
        )
        if sources <= 8:
            build(0)
            scores = score(0)
            for load in loads[waited:]:
                load.wait()
            if carried:
                spread_ids()
            for source in range(sources):
                later = None
                if source + 1 < sources:
                    build(source + 1)
                    later = score(source + 1)
                carry = fold(source, scores, carry)
                scores = later
        else:
            for load in loads[waited:]:
                load.wait()
            if carried:
                spread_ids()
            lax.fori_loop(0, sources, lambda i, _: (build(i), 0)[1], 0)
            carry = lax.fori_loop(0, sources, lambda i, c: fold(i, score(i), c), carry)
        width = QUAD * B
        return [carry[1][:, n * width : (n + 1) * width] for n in range(global_quads)]

    def block_of(place):
        source, local = place
        if carried:
            return source * blocks_dev + local
        return source * blocks_dev + ids_ref[source * group_blocks, LANES - 1] + local

    def key_block(block):
        at = block % blocks_dev if isinstance(block, int) else lax.rem(block, blocks_dev)
        source = block // blocks_dev if isinstance(block, int) else lax.div(block, blocks_dev)
        return keys_ref[source, pl.ds(at * B if isinstance(at, int) else pl.multiple_of(at * B, B), B)]

    def near_scores(quad):
        parts = queries_of(quad)
        glob_scores = dot_nt(keys_ref[0], jnp.concatenate(parts, axis=0))
        lists = []
        column = lax.broadcasted_iota(jnp.int32, (1, QUAD * B), 1) // B
        low = high = None
        for b, (source, local) in enumerate(places[quad]):
            block = block_of((source, local))
            if carried:
                window = [max(block - 1, 0), block, min(block + 1, total_blocks - 1)]
                dead_low, dead_high = block - 1 < GBLOCKS, block + 1 >= total_blocks
                if dead_low:
                    low = column == b if low is None else low | (column == b)
                if dead_high:
                    high = column == b if high is None else high | (column == b)
            else:
                window = [
                    jnp.maximum(block - 1, 0),
                    block,
                    jnp.minimum(block + 1, total_blocks - 1),
                ]
                one = (column == b) & (block - 1 < GBLOCKS)
                two = (column == b) & (block + 1 >= total_blocks)
                low = one if low is None else low | one
                high = two if high is None else high | two
            lists.append(window + rand_of(source, local))
        near_keys = []
        for b in range(0, QUAD, 2):
            tiles = [
                jnp.where(left, key_block(lists[b][k]), key_block(lists[b + 1][k]))
                for k in range(NEAR)
            ]
            near_keys.append(jnp.concatenate(tiles, axis=0))
        blank = jnp.zeros((2 * B, LANES), jnp.bfloat16)
        diagonal = jnp.concatenate(
            [
                jnp.concatenate(parts[:2] + [blank], axis=0),
                jnp.concatenate([blank] + parts[2:], axis=0),
            ],
            axis=1,
        )
        scores = dot_nt(jnp.concatenate(near_keys, axis=1), diagonal)
        if low is not None or high is not None:
            before, after = scores[:B], scores[2 * B : 3 * B]
            if low is not None:
                before = jnp.where(low, masked_score, before)
            if high is not None:
                after = jnp.where(high, masked_score, after)
            scores = jnp.concatenate([before, scores[B : 2 * B], after, scores[3 * B :]], axis=0)
        return glob_scores, scores, lists

    def near_finish(glob_scores, scores, lists):
        top = jnp.maximum(
            jnp.max(glob_scores, 0, keepdims=True), jnp.max(scores, 0, keepdims=True)
        )
        glob_weights = jnp.exp(glob_scores - top).astype(jnp.bfloat16)
        weights = jnp.exp(scores - top).astype(jnp.bfloat16)
        near_values = [
            jnp.concatenate(
                [
                    jnp.where(left, values_ref[lists[b][k]], values_ref[lists[b][k + 1]])
                    for k in range(0, NEAR, 2)
                ],
                axis=1,
            )
            for b in range(QUAD)
        ]
        near_values.append(jnp.ones((SUM_ROWS, NEAR * B), jnp.bfloat16))
        near = dot_nn(jnp.concatenate(near_values, axis=0), weights)
        own = jnp.concatenate(
            [
                jnp.where(left, near[:HD, :LANES], near[HD : 2 * HD, :LANES]),
                jnp.where(left, near[2 * HD : 3 * HD, LANES:], near[3 * HD : 4 * HD, LANES:]),
            ],
            axis=1,
        )
        return dot_nn(turned_values(0), glob_weights) + jnp.concatenate(
            [own, near[QUAD * HD :]], axis=0
        )

    waited = 1 if within else 2
    for load in loads[:waited]:
        load.wait()
    glob = full_rows()
    if carried:
        ids_copy.wait()
    if not mixed:
        for quad in range(global_quads):
            write(quad, glob[quad])
    first = 0 if mixed else global_quads
    ready = [near_scores(quad) for quad in range(first, min(first + AHEAD, quads))]
    for quad in range(first, quads):
        if quad + AHEAD < quads:
            ready.append(near_scores(quad + AHEAD))
        acc = near_finish(*ready[quad - first])
        if quad < global_quads:
            column = lax.broadcasted_iota(jnp.int32, (1, QUAD * B), 1) // B
            own = functools.reduce(
                jnp.logical_or,
                [(column == b) & (block_of(p) < GBLOCKS) for b, p in enumerate(places[quad])],
            )
            acc = jnp.where(own, glob[quad], acc)
        write(quad, acc)
    for store in stores:
        store.wait()


def attention(operands, plan, per, limit):
    rows, blocks_dev, _, places = plan[:4]
    quads = len(places)
    key_value = operands[0]
    sources = key_value.shape[0]
    total = sources * rows
    pairs = QUAD * B * (quads * (G + NEAR * B) + total)
    id_rows = sources * ID_ROWS if plan[6] else quads * QUAD
    hbm = pl.BlockSpec(memory_space=pltpu.HBM)
    shape = (quads // per, 2, HD, per * LANES)
    query_shape = (8, LANES) if plan[7] else operands[1].shape
    return pl.pallas_call(
        functools.partial(attend, plan),
        in_specs=[hbm] * len(operands),
        out_specs=hbm,
        out_shape=jax.ShapeDtypeStruct(shape, jnp.bfloat16),
        scratch_shapes=[
            pltpu.VMEM(query_shape, jnp.bfloat16),
            pltpu.VMEM(key_value.shape, jnp.bfloat16),
            pltpu.VMEM((sources, rows, LANES), jnp.bfloat16),
            pltpu.VMEM((total // B, HD, LANES), jnp.bfloat16),
            pltpu.VMEM(shape, jnp.bfloat16),
            pltpu.VMEM((id_rows, LANES), jnp.int32),
            pltpu.SMEM((id_rows, LANES), jnp.int32),
            pltpu.SemaphoreType.DMA((4 + quads // per,)),
        ],
        compiler_params=pltpu.CompilerParams(vmem_limit_bytes=limit),
        cost_estimate=pl.CostEstimate(
            flops=16 * HD * pairs, bytes_accessed=4 << 20, transcendentals=pairs
        ),
        name="attend",
    )(*operands)


def project_out(head_count, own_ref, turned_ref, here_ref, there_ref, *refs):
    out_ref = refs[-1]
    axis = turned_ref.shape[0] // head_count
    total = None
    for weight_ref, at in ((here_ref, own_ref[0]), (there_ref, 1 - own_ref[0])):
        heads = [turned_ref[h * axis + at] for h in range(head_count)]
        value = lax.dot_general(
            jnp.concatenate(heads, axis=0),
            weight_ref[...],
            (((0,), (0,)), ((), ())),
            preferred_element_type=jnp.float32,
        )
        total = value if total is None else total + value
    out_ref[...] = total.astype(jnp.bfloat16)


def output_rows(turned, here, there, head_count, chunk, chunks, before):
    rows = turned.shape[2]
    width = here.shape[1]
    return pl.pallas_call(
        functools.partial(project_out, head_count),
        grid_spec=pltpu.PrefetchScalarGridSpec(
            num_scalar_prefetch=1,
            grid=(1,),
            in_specs=[
                pl.BlockSpec(turned.shape, lambda i, _: (0, 0, 0)),
                pl.BlockSpec(here.shape, lambda i, _: (0, 0)),
                pl.BlockSpec(there.shape, lambda i, _: (0, 0)),
            ]
            + [pl.BlockSpec(memory_space=pl.ANY)] * len(before),
            out_specs=pl.BlockSpec((rows, width), lambda i, _: (chunk, 0)),
        ),
        out_shape=jax.ShapeDtypeStruct((rows * chunks, width), jnp.bfloat16),
        input_output_aliases={4: 0} if before else {},
        compiler_params=pltpu.CompilerParams(vmem_limit_bytes=20 * MIB),
        cost_estimate=pl.CostEstimate(
            flops=4 * rows * width * here.shape[0], bytes_accessed=3 << 20, transcendentals=0
        ),
        name="project_out",
    )(lax.axis_index("head").reshape(1), turned, here, there, *before)


def shards(history, qkv_weight, out_weight, rand_blocks):
    tok_rows = history.shape[0]
    head_count = qkv_weight.shape[2] // HD
    seq_count = lax.axis_size("seq")
    blocks_dev = tok_rows // B
    total_blocks = blocks_dev * seq_count
    group_count = seq_count // head_count
    seq_at = lax.axis_index("seq")
    direct = group_count == 1 and lax.axis_size("head") == 2
    chunks = 2 if direct else 1
    first, later = project(history, qkv_weight, rand_blocks, chunks)
    half = tok_rows // 2 // chunks

    if direct:
        first = lax.all_to_all(first, "seq", 0, 0, tiled=True)
        there = lax.ppermute(out_weight, "head", [(0, 1), (1, 0)])
        first, there = lax.optimization_barrier((first, there))
        per = half // (2 * B)
        outs = []
        for chunk in range(chunks):
            operands = [first]
            if chunk > 0:
                query, first = lax.optimization_barrier((later[chunk - 1], first))
                query = lax.all_to_all(query, "seq", 0, 0, tiled=True)
                query, outs[-1] = lax.optimization_barrier((query, outs[-1]))
                operands.append(query)
            places = [
                [
                    (
                        n // per,
                        x * (blocks_dev // 2) + chunk * 2 * per + 2 * (n % per) + i,
                    )
                    for i in range(2)
                    for x in range(2)
                ]
                for n in range(seq_count * per)
            ]
            plan = (tok_rows, blocks_dev, total_blocks, places, per, False, True, chunk == 0)
            out = attention(operands, plan, per, 62 * MIB)
            outs.append(out.reshape(2 * seq_count, HD, half))
        outs = [lax.all_to_all(out, ("seq", "head"), 0, 0, tiled=True) for out in outs]
        result = []
        for chunk in range(chunks):
            operands = (outs[chunk], out_weight, there)
            result = [output_rows(*operands, head_count, chunk, chunks, result)]
        return result[0]

    key_value = lax.all_gather(first[:, :tok_rows], "seq")
    key_value = lax.dynamic_index_in_dim(key_value, seq_at // group_count, 1, False)
    group_blocks = blocks_dev // group_count
    blocks = seq_count * group_blocks
    query = first[:, tok_rows : tok_rows + half]
    query = query.reshape(head_count, half, 2, HD).transpose(0, 2, 1, 3)
    query = lax.all_to_all(query.reshape(seq_count, -1, HD), "seq", 0, 0, tiled=True)
    query = query.reshape(blocks // QUAD, 2, 2, B, HD).transpose(0, 1, 3, 2, 4)
    query = query.reshape(blocks // QUAD, 2 * B, LANES)
    ids = rand_blocks.reshape(seq_count, group_blocks, R)
    ids = lax.all_to_all(ids, "seq", 0, 0, tiled=True).reshape(blocks, R)
    ids = jnp.pad(ids, ((0, 0), (0, LANES - R)))
    offset = seq_at % group_count * group_blocks
    ids = ids.at[:, LANES - 1].set(offset)
    places = [
        [((n * QUAD + b) // group_blocks, (n * QUAD + b) % group_blocks) for b in range(QUAD)]
        for n in range(blocks // QUAD)
    ]
    global_quads = -(-GBLOCKS // group_count // QUAD)
    plan = (tok_rows, blocks_dev, total_blocks, places, global_quads, True, False, False)
    out = attention([key_value, query, ids], plan, 1, 56 * MIB)
    out = out.reshape(blocks // QUAD, 2, HD, 2, B).transpose(0, 3, 1, 4, 2)
    out = lax.all_to_all(out.reshape(seq_count, -1, HD), "seq", 0, 0, tiled=True)
    attn = out.reshape(head_count, tok_rows, HD).transpose(1, 0, 2)
    return lax.psum_scatter(
        jnp.dot(
            attn.reshape(tok_rows, head_count * HD),
            out_weight,
            preferred_element_type=jnp.float32,
        ).astype(jnp.bfloat16),
        "head",
        scatter_dimension=0,
        tiled=True,
    )


def solution(mesh):
    placed = (
        P(("groups", "seq"), None),
        P(None, None, "head"),
        P("head", None),
        P("head", ("groups", "seq"), None),
    )
    return jax.shard_map(
        shards,
        mesh=mesh,
        in_specs=placed,
        out_specs=P(("groups", "seq", "head"), None),
        check_vma=False,
    )
```

```python
import functools
import math

import jax
import jax.numpy as jnp
from jax import lax
from jax.experimental import pallas as pl
from jax.experimental.pallas import tpu as pltpu
from jax.sharding import PartitionSpec as P

B = 64
R = 3
G = 1024
HD = 64
GBLOCKS = 16
LANES = 2 * HD
QUAD = 4
NEAR = 3 + R
SUM_ROWS = 16
ID_BASE = 256
ID_ROWS = 16
MIB = 1024 * 1024

AHEAD = 2

masked_score = -1e30
least_sum, most_sum = 1e-25, 1e30


def dot_nt(a, b):
    return lax.dot_general(a, b, (((1,), (1,)), ((), ())), preferred_element_type=jnp.float32)


def dot_nn(a, b):
    return jnp.dot(a, b, preferred_element_type=jnp.float32)


def left_half(rows):
    return lax.broadcasted_iota(jnp.int32, (rows, LANES), 1) < HD


def swap_halves(value):
    return jnp.concatenate([value[:, HD:], value[:, :HD]], axis=1)


def pair_rows(value):
    half = value.shape[0] // 2
    left = left_half(half)
    top, low = value[:half], value[half:]
    return jnp.where(left, top, swap_halves(low)), jnp.where(left, swap_halves(top), low)


def project_first(
    half, history_hbm, weight_hbm, ids_ref, out_hbm, history_ref, weight_ref, out_ref, sems
):
    rows = history_ref.shape[0]
    heads = out_ref.shape[0]
    step = min(4, heads)
    runs = heads // step
    width = step * HD
    loads = [pltpu.make_async_copy(history_hbm, history_ref, sems.at[0])]
    for run in range(runs):
        at = (slice(None), slice(None), pl.ds(run * width, width))
        loads.append(
            pltpu.make_async_copy(weight_hbm.at[at], weight_ref.at[at], sems.at[1 + run])
        )
    for load in loads:
        load.start()
    for head in range(heads):
        out_ref[head, rows + half :] = jnp.zeros((ID_ROWS, LANES), jnp.bfloat16)
        ids = [ids_ref[r, head : head + 1] for r in range(R)]
        ids = [v % ID_BASE for v in ids] + [v // ID_BASE for v in ids]
        ids.append(jnp.zeros((ID_ROWS - 2 * R, ids_ref.shape[2]), jnp.int32))
        ids = jnp.concatenate(ids, axis=0).astype(jnp.float32).astype(jnp.bfloat16)
        out_ref[head, rows + half :, : ids.shape[1]] = ids

    def product(unit):
        run, kind = unit
        lanes = slice(run * width, (run + 1) * width)
        if kind == 0:
            return dot_nn(history_ref[...], weight_ref[1, :, lanes])
        if kind == 1:
            return lax.dot_general(
                weight_ref[2, :, lanes],
                history_ref[...],
                (((0,), (1,)), ((), ())),
                preferred_element_type=jnp.float32,
            )
        return project_half(history_ref, weight_ref[0, :, lanes], 0, half)

    def place(unit, value):
        run, kind = unit
        value = value.astype(jnp.bfloat16)
        for head in range(run * step, (run + 1) * step):
            j = head - run * step
            if kind == 1:
                for i in range(rows // LANES):
                    tile = value[j * HD : (j + 1) * HD, i * LANES : (i + 1) * LANES]
                    out_ref[head, rows // 2 + i * HD : rows // 2 + (i + 1) * HD] = tile
            elif j % 2 == 0:
                pair = pair_rows(value[:, j * HD : (j + 2) * HD])
                at = 0 if kind == 0 else rows
                for k in range(2):
                    out_ref[head + k, at : at + pair[k].shape[0]] = pair[k]

    units = [(run, kind) for run in range(runs) for kind in range(3)]
    spans = [(0, rows // 2), (rows // 2, rows // 2), (rows, half + ID_ROWS)]
    stores = []
    for load in loads[:2]:
        load.wait()
    value = product(units[0])
    for n, unit in enumerate(units):
        later = None
        if n + 1 < len(units):
            if units[n + 1][0] > unit[0]:
                loads[1 + units[n + 1][0]].wait()
            later = product(units[n + 1])
        place(unit, value)
        at = (pl.ds(unit[0] * step, step), pl.ds(*spans[unit[1]]))
        stores.append(
            pltpu.make_async_copy(out_ref.at[at], out_hbm.at[at], sems.at[1 + runs + n])
        )
        stores[-1].start()
        value = later
    for store in stores:
        store.wait()


def project_half(history_ref, weight, first, half):
    middle = history_ref.shape[0] // 2
    chosen = jnp.concatenate(
        [
            history_ref[first : first + half],
            history_ref[middle + first : middle + first + half],
        ],
        axis=0,
    )
    return dot_nn(chosen, weight) * (1.0 / math.sqrt(HD))


def project_later(first, history_ref, weight_ref, out_ref):
    half = out_ref.shape[1]
    query = project_half(history_ref, weight_ref[0], first, half).astype(jnp.bfloat16)
    for j in range(0, out_ref.shape[0], 2):
        pair = pair_rows(query[:, j * HD : (j + 2) * HD])
        out_ref[j] = pair[0]
        out_ref[j + 1] = pair[1]


def project(history, qkv_weight, ids, chunks):
    rows, width = history.shape
    heads = qkv_weight.shape[2] // HD
    half = rows // 2 // chunks
    total = rows + half + ID_ROWS
    whole = pl.BlockSpec((rows, width), lambda i: (0, 0))
    params = pltpu.CompilerParams(vmem_limit_bytes=56 * MIB)
    first = pl.pallas_call(
        functools.partial(project_first, half),
        in_specs=[
            pl.BlockSpec(memory_space=pltpu.HBM),
            pl.BlockSpec(memory_space=pltpu.HBM),
            pl.BlockSpec(memory_space=pltpu.VMEM),
        ],
        out_specs=pl.BlockSpec(memory_space=pltpu.HBM),
        out_shape=jax.ShapeDtypeStruct((heads, total, LANES), jnp.bfloat16),
        scratch_shapes=[
            pltpu.VMEM(history.shape, jnp.bfloat16),
            pltpu.VMEM(qkv_weight.shape, jnp.bfloat16),
            pltpu.VMEM((heads, total, LANES), jnp.bfloat16),
            pltpu.SemaphoreType.DMA((1 + 2 * heads,)),
        ],
        compiler_params=params,
        cost_estimate=pl.CostEstimate(
            flops=5 * rows * width * heads * HD, bytes_accessed=6 << 20, transcendentals=0
        ),
        name="project_first",
    )(history, qkv_weight, ids.transpose(2, 0, 1))
    later = []
    step = min(4, heads)
    for chunk in range(1, chunks):
        history, first = lax.optimization_barrier((history, first))
        later.append(
            pl.pallas_call(
                functools.partial(project_later, chunk * half),
                grid=(heads // step,),
                in_specs=[whole, pl.BlockSpec((1, width, step * HD), lambda i: (0, 0, i))],
                out_specs=pl.BlockSpec((step, half, LANES), lambda i: (i, 0, 0)),
                out_shape=jax.ShapeDtypeStruct((heads, half, LANES), jnp.bfloat16),
                compiler_params=params,
                cost_estimate=pl.CostEstimate(
                    flops=4 * half * width * heads * HD, bytes_accessed=4 << 20, transcendentals=0
                ),
                name="project_later",
            )(history, qkv_weight)
        )
    return first, later


def attend(plan, *refs):
    rows, blocks_dev, total_blocks, places, global_quads, mixed, carried, within = plan
    kv_ref, keys_ref, values_ref, turned_ref, ids_vmem, ids_ref, sems = refs[-7:]
    out_hbm, query_ref = refs[-9:-7]
    kv_hbm = refs[0]
    sources = kv_ref.shape[0]
    half = rows // 2
    quads = len(places)
    group_blocks = blocks_dev if carried else quads * QUAD // sources
    per = turned_ref.shape[3] // LANES
    pairs = rows // LANES
    left = left_half(B)
    zero = jnp.zeros((B, LANES), jnp.bfloat16)
    lead, rest = pl.ds(0, 1), pl.ds(1, sources - 1)
    loads = [
        pltpu.make_async_copy(kv_hbm.at[lead], kv_ref.at[lead], sems.at[0]),
        pltpu.make_async_copy(kv_hbm.at[rest], kv_ref.at[rest], sems.at[1]),
    ]
    if not within:
        loads.insert(1, pltpu.make_async_copy(refs[1], query_ref, sems.at[2]))
    if carried:
        ids_copy = pltpu.make_async_copy(ids_vmem, ids_ref, sems.at[3])
    else:
        ids_copy = pltpu.make_async_copy(refs[2], ids_ref, sems.at[3])
        loads.append(ids_copy)
    for load in loads:
        load.start()
    stores = [
        pltpu.make_async_copy(
            turned_ref.at[pl.ds(i, 1)], out_hbm.at[pl.ds(i, 1)], sems.at[4 + i]
        )
        for i in range(quads // per)
    ]

    def spread_ids():
        end = kv_ref.shape[1]
        for source in range(sources):
            ids_vmem[source * ID_ROWS : (source + 1) * ID_ROWS] = (
                kv_ref[source, end - ID_ROWS :].astype(jnp.float32).astype(jnp.int32)
            )
        ids_copy.start()

    def rand_of(source, local):
        if carried:
            at = source * ID_ROWS
            return [
                ids_ref[at + r, local] + ids_ref[at + R + r, local] * ID_BASE for r in range(R)
            ]
        return [ids_ref[source * group_blocks + local, r] for r in range(R)]

    def build(source):
        packed = kv_ref[source, :half]
        wide = left_half(half)
        other = swap_halves(packed)
        keys_ref[source, :half] = jnp.where(wide, packed, other)
        keys_ref[source, half:] = jnp.where(wide, other, packed)
        for i in range(pairs):
            tile = kv_ref[source, half + i * HD : half + (i + 1) * HD]
            turned = swap_halves(tile)
            values_ref[source * 2 * pairs + 2 * i] = jnp.where(left, tile, turned)
            values_ref[source * 2 * pairs + 2 * i + 1] = jnp.where(left, turned, tile)

    def turned_values(source):
        tiles = [kv_ref[source, half + i * HD : half + (i + 1) * HD] for i in range(pairs)]
        ones = jnp.ones((SUM_ROWS, rows), jnp.bfloat16)
        return jnp.concatenate([jnp.concatenate(tiles, axis=1), ones], axis=0)

    def queries_of(quad):
        parts = []
        for i in range(2):
            if within:
                at = rows + (quad % per * 2 + i) * B
                packed = kv_ref[quad // per, at : at + B]
            else:
                at = (quad % per * 2 + i) * B
                packed = query_ref[quad // per, at : at + B]
            parts.append(jnp.where(left, packed, zero))
            parts.append(jnp.where(left, zero, packed))
        return parts

    def write(quad, acc, sums):
        total = acc[HD : HD + 1]
        sums.append(total)
        value = acc[:HD] / total
        first, second = value[:, :LANES], value[:, LANES:]
        at = slice(quad % per * LANES, (quad % per + 1) * LANES)
        turned_ref[quad // per, 0, :, at] = jnp.where(left, first, swap_halves(second)).astype(
            jnp.bfloat16
        )
        turned_ref[quad // per, 1, :, at] = jnp.where(left, swap_halves(first), second).astype(
            jnp.bfloat16
        )
        if quad % per == per - 1:
            stores[quad // per].start()

    def full_rows(exact):
        query = jnp.concatenate([p for n in range(global_quads) for p in queries_of(n)], axis=0)

        def score(source):
            return dot_nt(keys_ref[source], query)

        def fold(source, scores, carry):
            top, acc = carry
            if exact:
                new_top = jnp.maximum(top, jnp.max(scores, 0, keepdims=True))
                acc = acc * jnp.exp(top - new_top)
                top = new_top
                scores = scores - top
            weights = jnp.exp(scores).astype(jnp.bfloat16)
            return top, acc + dot_nn(turned_values(source), weights)

        carry = (
            jnp.full((1, query.shape[0]), -jnp.inf, jnp.float32),
            jnp.zeros((HD + SUM_ROWS, query.shape[0]), jnp.float32),
        )
        if sources <= 8 and not exact:
            build(0)
            scores = score(0)
            for load in loads[waited:]:
                load.wait()
            if carried:
                spread_ids()
            for source in range(sources):
                later = None
                if source + 1 < sources:
                    build(source + 1)
                    later = score(source + 1)
                carry = fold(source, scores, carry)
                scores = later
        else:
            if not exact:
                for load in loads[waited:]:
                    load.wait()
                if carried:
                    spread_ids()
                lax.fori_loop(0, sources, lambda i, _: (build(i), 0)[1], 0)
            carry = lax.fori_loop(0, sources, lambda i, c: fold(i, score(i), c), carry)
        width = QUAD * B
        return [carry[1][:, n * width : (n + 1) * width] for n in range(global_quads)]

    def block_of(place):
        source, local = place
        if carried:
            return source * blocks_dev + local
        return source * blocks_dev + ids_ref[source * group_blocks, LANES - 1] + local

    def key_block(block):
        at = block % blocks_dev if isinstance(block, int) else lax.rem(block, blocks_dev)
        source = block // blocks_dev if isinstance(block, int) else lax.div(block, blocks_dev)
        return keys_ref[source, pl.ds(at * B if isinstance(at, int) else pl.multiple_of(at * B, B), B)]

    def near_scores(quad):
        parts = queries_of(quad)
        glob_scores = dot_nt(keys_ref[0], jnp.concatenate(parts, axis=0))
        lists = []
        column = lax.broadcasted_iota(jnp.int32, (1, QUAD * B), 1) // B
        low = high = None
        for b, (source, local) in enumerate(places[quad]):
            block = block_of((source, local))
            if carried:
                window = [max(block - 1, 0), block, min(block + 1, total_blocks - 1)]
                dead_low, dead_high = block - 1 < GBLOCKS, block + 1 >= total_blocks
                if dead_low:
                    low = column == b if low is None else low | (column == b)
                if dead_high:
                    high = column == b if high is None else high | (column == b)
            else:
                window = [
                    jnp.maximum(block - 1, 0),
                    block,
                    jnp.minimum(block + 1, total_blocks - 1),
                ]
                one = (column == b) & (block - 1 < GBLOCKS)
                two = (column == b) & (block + 1 >= total_blocks)
                low = one if low is None else low | one
                high = two if high is None else high | two
            lists.append(window + rand_of(source, local))
        near_keys = []
        for b in range(0, QUAD, 2):
            tiles = [
                jnp.where(left, key_block(lists[b][k]), key_block(lists[b + 1][k]))
                for k in range(NEAR)
            ]
            near_keys.append(jnp.concatenate(tiles, axis=0))
        blank = jnp.zeros((2 * B, LANES), jnp.bfloat16)
        diagonal = jnp.concatenate(
            [
                jnp.concatenate(parts[:2] + [blank], axis=0),
                jnp.concatenate([blank] + parts[2:], axis=0),
            ],
            axis=1,
        )
        scores = dot_nt(jnp.concatenate(near_keys, axis=1), diagonal)
        if low is not None or high is not None:
            before, after = scores[:B], scores[2 * B : 3 * B]
            if low is not None:
                before = jnp.where(low, masked_score, before)
            if high is not None:
                after = jnp.where(high, masked_score, after)
            scores = jnp.concatenate([before, scores[B : 2 * B], after, scores[3 * B :]], axis=0)
        return glob_scores, scores, lists

    def near_finish(exact, glob_scores, scores, lists):
        if exact:
            top = jnp.maximum(
                jnp.max(glob_scores, 0, keepdims=True), jnp.max(scores, 0, keepdims=True)
            )
            glob_scores, scores = glob_scores - top, scores - top
        glob_weights = jnp.exp(glob_scores).astype(jnp.bfloat16)
        weights = jnp.exp(scores).astype(jnp.bfloat16)
        near_values = [
            jnp.concatenate(
                [
                    jnp.where(left, values_ref[lists[b][k]], values_ref[lists[b][k + 1]])
                    for k in range(0, NEAR, 2)
                ],
                axis=1,
            )
            for b in range(QUAD)
        ]
        near_values.append(jnp.ones((SUM_ROWS, NEAR * B), jnp.bfloat16))
        near = dot_nn(jnp.concatenate(near_values, axis=0), weights)
        own = jnp.concatenate(
            [
                jnp.where(left, near[:HD, :LANES], near[HD : 2 * HD, :LANES]),
                jnp.where(left, near[2 * HD : 3 * HD, LANES:], near[3 * HD : 4 * HD, LANES:]),
            ],
            axis=1,
        )
        return dot_nn(turned_values(0), glob_weights) + jnp.concatenate(
            [own, near[QUAD * HD :]], axis=0
        )

    waited = 1 if within else 2
    for load in loads[:waited]:
        load.wait()

    def run(exact):
        sums = []
        glob = full_rows(exact)
        if carried and not exact:
            ids_copy.wait()
        if not mixed:
            for quad in range(global_quads):
                write(quad, glob[quad], sums)
        first = 0 if mixed else global_quads
        ahead = 1 if exact else AHEAD
        ready = [near_scores(quad) for quad in range(first, min(first + ahead, quads))]
        for quad in range(first, quads):
            if quad + ahead < quads:
                ready.append(near_scores(quad + ahead))
            acc = near_finish(exact, *ready[quad - first])
            if quad < global_quads:
                column = lax.broadcasted_iota(jnp.int32, (1, QUAD * B), 1) // B
                own = functools.reduce(
                    jnp.logical_or,
                    [
                        (column == b) & (block_of(p) < GBLOCKS)
                        for b, p in enumerate(places[quad])
                    ],
                )
                acc = jnp.where(own, glob[quad], acc)
            write(quad, acc, sums)
        for store in stores:
            store.wait()
        return jnp.concatenate(sums, axis=0)

    sums = run(False)
    bad = jnp.where((sums >= least_sum) & (sums <= most_sum), 0.0, 1.0)

    @pl.when(jnp.max(bad) > 0.0)
    def _():
        run(True)


def attention(operands, plan, per, limit):
    rows, blocks_dev, _, places = plan[:4]
    quads = len(places)
    key_value = operands[0]
    sources = key_value.shape[0]
    total = sources * rows
    pairs = QUAD * B * (quads * (G + NEAR * B) + total)
    id_rows = sources * ID_ROWS if plan[6] else quads * QUAD
    hbm = pl.BlockSpec(memory_space=pltpu.HBM)
    shape = (quads // per, 2, HD, per * LANES)
    query_shape = (8, LANES) if plan[7] else operands[1].shape
    return pl.pallas_call(
        functools.partial(attend, plan),
        in_specs=[hbm] * len(operands),
        out_specs=hbm,
        out_shape=jax.ShapeDtypeStruct(shape, jnp.bfloat16),
        scratch_shapes=[
            pltpu.VMEM(query_shape, jnp.bfloat16),
            pltpu.VMEM(key_value.shape, jnp.bfloat16),
            pltpu.VMEM((sources, rows, LANES), jnp.bfloat16),
            pltpu.VMEM((total // B, HD, LANES), jnp.bfloat16),
            pltpu.VMEM(shape, jnp.bfloat16),
            pltpu.VMEM((id_rows, LANES), jnp.int32),
            pltpu.SMEM((id_rows, LANES), jnp.int32),
            pltpu.SemaphoreType.DMA((4 + quads // per,)),
        ],
        compiler_params=pltpu.CompilerParams(vmem_limit_bytes=limit),
        cost_estimate=pl.CostEstimate(
            flops=16 * HD * pairs, bytes_accessed=4 << 20, transcendentals=pairs
        ),
        name="attend",
    )(*operands)


def project_out(head_count, own_ref, turned_ref, here_ref, there_ref, *refs):
    out_ref = refs[-1]
    axis = turned_ref.shape[0] // head_count
    total = None
    for weight_ref, at in ((here_ref, own_ref[0]), (there_ref, 1 - own_ref[0])):
        heads = [turned_ref[h * axis + at] for h in range(head_count)]
        value = lax.dot_general(
            jnp.concatenate(heads, axis=0),
            weight_ref[...],
            (((0,), (0,)), ((), ())),
            preferred_element_type=jnp.float32,
        )
        total = value if total is None else total + value
    out_ref[...] = total.astype(jnp.bfloat16)


def output_rows(turned, here, there, head_count, chunk, chunks, before):
    rows = turned.shape[2]
    width = here.shape[1]
    return pl.pallas_call(
        functools.partial(project_out, head_count),
        grid_spec=pltpu.PrefetchScalarGridSpec(
            num_scalar_prefetch=1,
            grid=(1,),
            in_specs=[
                pl.BlockSpec(turned.shape, lambda i, _: (0, 0, 0)),
                pl.BlockSpec(here.shape, lambda i, _: (0, 0)),
                pl.BlockSpec(there.shape, lambda i, _: (0, 0)),
            ]
            + [pl.BlockSpec(memory_space=pl.ANY)] * len(before),
            out_specs=pl.BlockSpec((rows, width), lambda i, _: (chunk, 0)),
        ),
        out_shape=jax.ShapeDtypeStruct((rows * chunks, width), jnp.bfloat16),
        input_output_aliases={4: 0} if before else {},
        compiler_params=pltpu.CompilerParams(vmem_limit_bytes=20 * MIB),
        cost_estimate=pl.CostEstimate(
            flops=4 * rows * width * here.shape[0], bytes_accessed=3 << 20, transcendentals=0
        ),
        name="project_out",
    )(lax.axis_index("head").reshape(1), turned, here, there, *before)


def shards(history, qkv_weight, out_weight, rand_blocks):
    tok_rows = history.shape[0]
    head_count = qkv_weight.shape[2] // HD
    seq_count = lax.axis_size("seq")
    blocks_dev = tok_rows // B
    total_blocks = blocks_dev * seq_count
    group_count = seq_count // head_count
    seq_at = lax.axis_index("seq")
    direct = group_count == 1 and lax.axis_size("head") == 2
    chunks = 2 if direct else 1
    first, later = project(history, qkv_weight, rand_blocks, chunks)
    half = tok_rows // 2 // chunks

    if direct:
        first = lax.all_to_all(first, "seq", 0, 0, tiled=True)
        there = lax.ppermute(out_weight, "head", [(0, 1), (1, 0)])
        first, there = lax.optimization_barrier((first, there))
        per = half // (2 * B)
        outs = []
        for chunk in range(chunks):
            operands = [first]
            if chunk > 0:
                query, first = lax.optimization_barrier((later[chunk - 1], first))
                query = lax.all_to_all(query, "seq", 0, 0, tiled=True)
                query, outs[-1] = lax.optimization_barrier((query, outs[-1]))
                operands.append(query)
            places = [
                [
                    (
                        n // per,
                        x * (blocks_dev // 2) + chunk * 2 * per + 2 * (n % per) + i,
                    )
                    for i in range(2)
                    for x in range(2)
                ]
                for n in range(seq_count * per)
            ]
            plan = (tok_rows, blocks_dev, total_blocks, places, per, False, True, chunk == 0)
            out = attention(operands, plan, per, 62 * MIB)
            outs.append(out.reshape(2 * seq_count, HD, half))
        outs = [lax.all_to_all(out, ("seq", "head"), 0, 0, tiled=True) for out in outs]
        result = []
        for chunk in range(chunks):
            operands = (outs[chunk], out_weight, there)
            result = [output_rows(*operands, head_count, chunk, chunks, result)]
        return result[0]

    key_value = lax.all_gather(first[:, :tok_rows], "seq")
    key_value = lax.dynamic_index_in_dim(key_value, seq_at // group_count, 1, False)
    group_blocks = blocks_dev // group_count
    blocks = seq_count * group_blocks
    query = first[:, tok_rows : tok_rows + half]
    query = query.reshape(head_count, half, 2, HD).transpose(0, 2, 1, 3)
    query = lax.all_to_all(query.reshape(seq_count, -1, HD), "seq", 0, 0, tiled=True)
    query = query.reshape(blocks // QUAD, 2, 2, B, HD).transpose(0, 1, 3, 2, 4)
    query = query.reshape(blocks // QUAD, 2 * B, LANES)
    ids = rand_blocks.reshape(seq_count, group_blocks, R)
    ids = lax.all_to_all(ids, "seq", 0, 0, tiled=True).reshape(blocks, R)
    ids = jnp.pad(ids, ((0, 0), (0, LANES - R)))
    offset = seq_at % group_count * group_blocks
    ids = ids.at[:, LANES - 1].set(offset)
    places = [
        [((n * QUAD + b) // group_blocks, (n * QUAD + b) % group_blocks) for b in range(QUAD)]
        for n in range(blocks // QUAD)
    ]
    global_quads = -(-GBLOCKS // group_count // QUAD)
    plan = (tok_rows, blocks_dev, total_blocks, places, global_quads, True, False, False)
    out = attention([key_value, query, ids], plan, 1, 56 * MIB)
    out = out.reshape(blocks // QUAD, 2, HD, 2, B).transpose(0, 3, 1, 4, 2)
    out = lax.all_to_all(out.reshape(seq_count, -1, HD), "seq", 0, 0, tiled=True)
    attn = out.reshape(head_count, tok_rows, HD).transpose(1, 0, 2)
    return lax.psum_scatter(
        jnp.dot(
            attn.reshape(tok_rows, head_count * HD),
            out_weight,
            preferred_element_type=jnp.float32,
        ).astype(jnp.bfloat16),
        "head",
        scatter_dimension=0,
        tiled=True,
    )


def solution(mesh):
    placed = (
        P(("groups", "seq"), None),
        P(None, None, "head"),
        P("head", None),
        P("head", ("groups", "seq"), None),
    )
    return jax.shard_map(
        shards,
        mesh=mesh,
        in_specs=placed,
        out_specs=P(("groups", "seq", "head"), None),
        check_vma=False,
    )
```

```python
import functools
import math

import jax
import jax.numpy as jnp
from jax import lax
from jax.experimental import pallas as pl
from jax.experimental.pallas import tpu as pltpu
from jax.sharding import PartitionSpec as P

B = 64
R = 3
G = 1024
HD = 64
GBLOCKS = 16
LANES = 2 * HD
QUAD = 4
NEAR = 3 + R
SUM_ROWS = 16
ID_BASE = 256
ID_ROWS = 16
MIB = 1024 * 1024

AHEAD = 2

masked_score = -1e30
least_sum, most_sum = 1e-25, 1e30


def dot_nt(a, b):
    return lax.dot_general(a, b, (((1,), (1,)), ((), ())), preferred_element_type=jnp.float32)


def dot_nn(a, b):
    return jnp.dot(a, b, preferred_element_type=jnp.float32)


def left_half(rows):
    return lax.broadcasted_iota(jnp.int32, (rows, LANES), 1) < HD


def swap_halves(value):
    return jnp.concatenate([value[:, HD:], value[:, :HD]], axis=1)


def pair_rows(value):
    half = value.shape[0] // 2
    left = left_half(half)
    top, low = value[:half], value[half:]
    return jnp.where(left, top, swap_halves(low)), jnp.where(left, swap_halves(top), low)


def project_first(half, place_ref, history_hbm, weight_hbm, ids_ref, *refs):
    *outs, history_ref, weight_ref, out_ref, sems = refs
    rows = history_ref.shape[0]
    heads = out_ref.shape[0]
    step = min(4, heads)
    runs = heads // step
    width = step * HD
    loads = [pltpu.make_async_copy(history_hbm, history_ref, sems.at[0])]
    for run in range(runs):
        at = (slice(None), slice(None), pl.ds(run * width, width))
        loads.append(
            pltpu.make_async_copy(weight_hbm.at[at], weight_ref.at[at], sems.at[1 + run])
        )
    for load in loads:
        load.start()
    for head in range(heads):
        out_ref[head, rows + half :] = jnp.zeros((ID_ROWS, LANES), jnp.bfloat16)
        ids = [ids_ref[r, head : head + 1] for r in range(R)]
        ids = [v % ID_BASE for v in ids] + [v // ID_BASE for v in ids]
        ids.append(jnp.zeros((ID_ROWS - 2 * R, ids_ref.shape[2]), jnp.int32))
        ids = jnp.concatenate(ids, axis=0).astype(jnp.float32).astype(jnp.bfloat16)
        out_ref[head, rows + half :, : ids.shape[1]] = ids

    def product(unit):
        run, kind = unit
        lanes = slice(run * width, (run + 1) * width)
        if kind == 0:
            return dot_nn(history_ref[...], weight_ref[1, :, lanes])
        if kind == 1:
            return lax.dot_general(
                weight_ref[2, :, lanes],
                history_ref[...],
                (((0,), (1,)), ((), ())),
                preferred_element_type=jnp.float32,
            )
        return project_half(history_ref, weight_ref[0, :, lanes], 0, half)

    def place(unit, value):
        run, kind = unit
        value = value.astype(jnp.bfloat16)
        for head in range(run * step, (run + 1) * step):
            j = head - run * step
            if kind == 1:
                for i in range(rows // LANES):
                    tile = value[j * HD : (j + 1) * HD, i * LANES : (i + 1) * LANES]
                    out_ref[head, rows // 2 + i * HD : rows // 2 + (i + 1) * HD] = tile
            elif j % 2 == 0:
                pair = pair_rows(value[:, j * HD : (j + 2) * HD])
                at = 0 if kind == 0 else rows
                for k in range(2):
                    out_ref[head + k, at : at + pair[k].shape[0]] = pair[k]

    units = [(run, kind) for run in range(runs) for kind in range(3)]
    for load in loads[:2]:
        load.wait()
    value = product(units[0])
    for n, unit in enumerate(units):
        later = None
        if n + 1 < len(units):
            if units[n + 1][0] > unit[0]:
                loads[1 + units[n + 1][0]].wait()
            later = product(units[n + 1])
        place(unit, value)
        value = later
    stores = [
        pltpu.make_async_copy(
            out_ref.at[lax.rem(place_ref[0] + k, heads)], out, sems.at[1 + runs + k]
        )
        for k, out in enumerate(outs)
    ]
    for store in stores:
        store.start()
    for store in stores:
        store.wait()


def project_half(history_ref, weight, first, half):
    middle = history_ref.shape[0] // 2
    chosen = jnp.concatenate(
        [
            history_ref[first : first + half],
            history_ref[middle + first : middle + first + half],
        ],
        axis=0,
    )
    return dot_nn(chosen, weight) * (1.0 / math.sqrt(HD))


def project_later(first, history_ref, weight_ref, out_ref):
    half = out_ref.shape[1]
    query = project_half(history_ref, weight_ref[0], first, half).astype(jnp.bfloat16)
    for j in range(0, out_ref.shape[0], 2):
        pair = pair_rows(query[:, j * HD : (j + 2) * HD])
        out_ref[j] = pair[0]
        out_ref[j + 1] = pair[1]


def project(history, qkv_weight, ids, place, chunks):
    rows, width = history.shape
    heads = qkv_weight.shape[2] // HD
    half = rows // 2 // chunks
    total = rows + half + ID_ROWS
    whole = pl.BlockSpec((rows, width), lambda i: (0, 0))
    params = pltpu.CompilerParams(vmem_limit_bytes=56 * MIB)
    first = pl.pallas_call(
        functools.partial(project_first, half),
        in_specs=[
            pl.BlockSpec(memory_space=pltpu.SMEM),
            pl.BlockSpec(memory_space=pltpu.HBM),
            pl.BlockSpec(memory_space=pltpu.HBM),
            pl.BlockSpec(memory_space=pltpu.VMEM),
        ],
        out_specs=[pl.BlockSpec(memory_space=pltpu.HBM)] * heads,
        out_shape=[jax.ShapeDtypeStruct((total, LANES), jnp.bfloat16)] * heads,
        scratch_shapes=[
            pltpu.VMEM(history.shape, jnp.bfloat16),
            pltpu.VMEM(qkv_weight.shape, jnp.bfloat16),
            pltpu.VMEM((heads, total, LANES), jnp.bfloat16),
            pltpu.SemaphoreType.DMA((1 + 2 * heads,)),
        ],
        compiler_params=params,
        cost_estimate=pl.CostEstimate(
            flops=5 * rows * width * heads * HD, bytes_accessed=6 << 20, transcendentals=0
        ),
        name="project_first",
    )(place.reshape(1), history, qkv_weight, ids.transpose(2, 0, 1))
    later = []
    step = min(4, heads)
    for chunk in range(1, chunks):
        history, first = lax.optimization_barrier((history, first))
        later.append(
            pl.pallas_call(
                functools.partial(project_later, chunk * half),
                grid=(heads // step,),
                in_specs=[whole, pl.BlockSpec((1, width, step * HD), lambda i: (0, 0, i))],
                out_specs=pl.BlockSpec((step, half, LANES), lambda i: (i, 0, 0)),
                out_shape=jax.ShapeDtypeStruct((heads, half, LANES), jnp.bfloat16),
                compiler_params=params,
                cost_estimate=pl.CostEstimate(
                    flops=4 * half * width * heads * HD, bytes_accessed=4 << 20, transcendentals=0
                ),
                name="project_later",
            )(history, qkv_weight)
        )
    return first, later


def attend(plan, *refs):
    rows, blocks_dev, total_blocks, places, global_quads, mixed, carried, within = plan
    kv_ref, keys_ref, values_ref, turned_ref, ids_vmem, ids_ref, sems = refs[-7:]
    out_hbm, query_ref = refs[-9:-7]
    sources = kv_ref.shape[0]
    half = rows // 2
    quads = len(places)
    group_blocks = blocks_dev if carried else quads * QUAD // sources
    per = turned_ref.shape[3] // LANES
    pairs = rows // LANES
    left = left_half(B)
    zero = jnp.zeros((B, LANES), jnp.bfloat16)
    if carried:
        place_ref, *pieces = refs[: 1 + sources]
        loads = [
            pltpu.make_async_copy(
                piece, kv_ref.at[lax.rem(place_ref[0] + sources - k, sources)], sems.at[k]
            )
            for k, piece in enumerate(pieces)
        ]
        ids_copy = pltpu.make_async_copy(ids_vmem, ids_ref, sems.at[sources + 1])
    else:
        loads = [pltpu.make_async_copy(refs[0], kv_ref, sems.at[0])]
        ids_copy = pltpu.make_async_copy(refs[2], ids_ref, sems.at[sources + 1])
        loads.append(ids_copy)
    if not within:
        query_hbm = refs[1 + sources] if carried else refs[1]
        loads.append(pltpu.make_async_copy(query_hbm, query_ref, sems.at[sources]))
    for load in loads:
        load.start()
    stores = [
        pltpu.make_async_copy(
            turned_ref.at[pl.ds(i, 1)], out_hbm.at[pl.ds(i, 1)], sems.at[sources + 2 + i]
        )
        for i in range(quads // per)
    ]

    def spread_ids():
        end = kv_ref.shape[1]
        for source in range(sources):
            ids_vmem[source * ID_ROWS : (source + 1) * ID_ROWS] = (
                kv_ref[source, end - ID_ROWS :].astype(jnp.float32).astype(jnp.int32)
            )
        ids_copy.start()

    def rand_of(source, local):
        if carried:
            at = source * ID_ROWS
            return [
                ids_ref[at + r, local] + ids_ref[at + R + r, local] * ID_BASE for r in range(R)
            ]
        return [ids_ref[source * group_blocks + local, r] for r in range(R)]

    def build(source):
        packed = kv_ref[source, :half]
        wide = left_half(half)
        other = swap_halves(packed)
        keys_ref[source, :half] = jnp.where(wide, packed, other)
        keys_ref[source, half:] = jnp.where(wide, other, packed)
        for i in range(pairs):
            tile = kv_ref[source, half + i * HD : half + (i + 1) * HD]
            turned = swap_halves(tile)
            values_ref[source * 2 * pairs + 2 * i] = jnp.where(left, tile, turned)
            values_ref[source * 2 * pairs + 2 * i + 1] = jnp.where(left, turned, tile)

    def turned_values(source):
        tiles = [kv_ref[source, half + i * HD : half + (i + 1) * HD] for i in range(pairs)]
        ones = jnp.ones((SUM_ROWS, rows), jnp.bfloat16)
        return jnp.concatenate([jnp.concatenate(tiles, axis=1), ones], axis=0)

    def queries_of(quad):
        parts = []
        for i in range(2):
            if within:
                at = rows + (quad % per * 2 + i) * B
                packed = kv_ref[quad // per, at : at + B]
            else:
                at = (quad % per * 2 + i) * B
                packed = query_ref[quad // per, at : at + B]
            parts.append(jnp.where(left, packed, zero))
            parts.append(jnp.where(left, zero, packed))
        return parts

    def write(quad, acc, sums):
        total = acc[HD : HD + 1]
        sums.append(total)
        value = acc[:HD] / total
        first, second = value[:, :LANES], value[:, LANES:]
        at = slice(quad % per * LANES, (quad % per + 1) * LANES)
        turned_ref[quad // per, 0, :, at] = jnp.where(left, first, swap_halves(second)).astype(
            jnp.bfloat16
        )
        turned_ref[quad // per, 1, :, at] = jnp.where(left, swap_halves(first), second).astype(
            jnp.bfloat16
        )
        if quad % per == per - 1:
            stores[quad // per].start()

    def full_rows(exact):
        query = jnp.concatenate([p for n in range(global_quads) for p in queries_of(n)], axis=0)

        def score(source):
            return dot_nt(keys_ref[source], query)

        def fold(source, scores, carry):
            top, acc = carry
            if exact:
                new_top = jnp.maximum(top, jnp.max(scores, 0, keepdims=True))
                acc = acc * jnp.exp(top - new_top)
                top = new_top
                scores = scores - top
            weights = jnp.exp(scores).astype(jnp.bfloat16)
            return top, acc + dot_nn(turned_values(source), weights)

        carry = (
            jnp.full((1, query.shape[0]), -jnp.inf, jnp.float32),
            jnp.zeros((HD + SUM_ROWS, query.shape[0]), jnp.float32),
        )
        if sources <= 8 and not exact:
            build(0)
            scores = score(0)
            if carried:
                spread_ids()
            for source in range(sources):
                later = None
                if source + 1 < sources:
                    build(source + 1)
                    later = score(source + 1)
                carry = fold(source, scores, carry)
                scores = later
        else:
            if not exact:
                if carried:
                    spread_ids()
                lax.fori_loop(0, sources, lambda i, _: (build(i), 0)[1], 0)
            carry = lax.fori_loop(0, sources, lambda i, c: fold(i, score(i), c), carry)
        width = QUAD * B
        return [carry[1][:, n * width : (n + 1) * width] for n in range(global_quads)]

    def block_of(place):
        source, local = place
        if carried:
            return source * blocks_dev + local
        return source * blocks_dev + ids_ref[source * group_blocks, LANES - 1] + local

    def key_block(block):
        at = block % blocks_dev if isinstance(block, int) else lax.rem(block, blocks_dev)
        source = block // blocks_dev if isinstance(block, int) else lax.div(block, blocks_dev)
        return keys_ref[source, pl.ds(at * B if isinstance(at, int) else pl.multiple_of(at * B, B), B)]

    def near_scores(quad):
        parts = queries_of(quad)
        glob_scores = dot_nt(keys_ref[0], jnp.concatenate(parts, axis=0))
        lists = []
        column = lax.broadcasted_iota(jnp.int32, (1, QUAD * B), 1) // B
        low = high = None
        for b, (source, local) in enumerate(places[quad]):
            block = block_of((source, local))
            if carried:
                window = [max(block - 1, 0), block, min(block + 1, total_blocks - 1)]
                dead_low, dead_high = block - 1 < GBLOCKS, block + 1 >= total_blocks
                if dead_low:
                    low = column == b if low is None else low | (column == b)
                if dead_high:
                    high = column == b if high is None else high | (column == b)
            else:
                window = [
                    jnp.maximum(block - 1, 0),
                    block,
                    jnp.minimum(block + 1, total_blocks - 1),
                ]
                one = (column == b) & (block - 1 < GBLOCKS)
                two = (column == b) & (block + 1 >= total_blocks)
                low = one if low is None else low | one
                high = two if high is None else high | two
            lists.append(window + rand_of(source, local))
        near_keys = []
        for b in range(0, QUAD, 2):
            tiles = [
                jnp.where(left, key_block(lists[b][k]), key_block(lists[b + 1][k]))
                for k in range(NEAR)
            ]
            near_keys.append(jnp.concatenate(tiles, axis=0))
        blank = jnp.zeros((2 * B, LANES), jnp.bfloat16)
        diagonal = jnp.concatenate(
            [
                jnp.concatenate(parts[:2] + [blank], axis=0),
                jnp.concatenate([blank] + parts[2:], axis=0),
            ],
            axis=1,
        )
        scores = dot_nt(jnp.concatenate(near_keys, axis=1), diagonal)
        if low is not None or high is not None:
            before, after = scores[:B], scores[2 * B : 3 * B]
            if low is not None:
                before = jnp.where(low, masked_score, before)
            if high is not None:
                after = jnp.where(high, masked_score, after)
            scores = jnp.concatenate([before, scores[B : 2 * B], after, scores[3 * B :]], axis=0)
        return glob_scores, scores, lists

    def near_finish(exact, glob_scores, scores, lists):
        if exact:
            top = jnp.maximum(
                jnp.max(glob_scores, 0, keepdims=True), jnp.max(scores, 0, keepdims=True)
            )
            glob_scores, scores = glob_scores - top, scores - top
        glob_weights = jnp.exp(glob_scores).astype(jnp.bfloat16)
        weights = jnp.exp(scores).astype(jnp.bfloat16)
        near_values = [
            jnp.concatenate(
                [
                    jnp.where(left, values_ref[lists[b][k]], values_ref[lists[b][k + 1]])
                    for k in range(0, NEAR, 2)
                ],
                axis=1,
            )
            for b in range(QUAD)
        ]
        near_values.append(jnp.ones((SUM_ROWS, NEAR * B), jnp.bfloat16))
        near = dot_nn(jnp.concatenate(near_values, axis=0), weights)
        own = jnp.concatenate(
            [
                jnp.where(left, near[:HD, :LANES], near[HD : 2 * HD, :LANES]),
                jnp.where(left, near[2 * HD : 3 * HD, LANES:], near[3 * HD : 4 * HD, LANES:]),
            ],
            axis=1,
        )
        return dot_nn(turned_values(0), glob_weights) + jnp.concatenate(
            [own, near[QUAD * HD :]], axis=0
        )

    for load in loads:
        load.wait()

    def run(exact):
        sums = []
        glob = full_rows(exact)
        if carried and not exact:
            ids_copy.wait()
        if not mixed:
            for quad in range(global_quads):
                write(quad, glob[quad], sums)
        first = 0 if mixed else global_quads
        ahead = 1 if exact else AHEAD
        ready = [near_scores(quad) for quad in range(first, min(first + ahead, quads))]
        for quad in range(first, quads):
            if quad + ahead < quads:
                ready.append(near_scores(quad + ahead))
            acc = near_finish(exact, *ready[quad - first])
            if quad < global_quads:
                column = lax.broadcasted_iota(jnp.int32, (1, QUAD * B), 1) // B
                own = functools.reduce(
                    jnp.logical_or,
                    [
                        (column == b) & (block_of(p) < GBLOCKS)
                        for b, p in enumerate(places[quad])
                    ],
                )
                acc = jnp.where(own, glob[quad], acc)
            write(quad, acc, sums)
        for store in stores:
            store.wait()
        return jnp.concatenate(sums, axis=0)

    sums = run(False)
    bad = jnp.where((sums >= least_sum) & (sums <= most_sum), 0.0, 1.0)

    @pl.when(jnp.max(bad) > 0.0)
    def _():
        run(True)


def attention(operands, plan, per, sources, limit):
    rows, blocks_dev, _, places = plan[:4]
    quads = len(places)
    carried, within = plan[6:]
    size = operands[1].shape if carried else operands[0].shape[1:]
    total = sources * rows
    pairs = QUAD * B * (quads * (G + NEAR * B) + total)
    id_rows = sources * ID_ROWS if carried else quads * QUAD
    hbm = pl.BlockSpec(memory_space=pltpu.HBM)
    shape = (quads // per, 2, HD, per * LANES)
    query_shape = (8, LANES) if within else operands[-1 if carried else 1].shape
    specs = [hbm] * len(operands)
    if carried:
        specs[0] = pl.BlockSpec(memory_space=pltpu.SMEM)
    return pl.pallas_call(
        functools.partial(attend, plan),
        in_specs=specs,
        out_specs=hbm,
        out_shape=jax.ShapeDtypeStruct(shape, jnp.bfloat16),
        scratch_shapes=[
            pltpu.VMEM(query_shape, jnp.bfloat16),
            pltpu.VMEM((sources,) + size, jnp.bfloat16),
            pltpu.VMEM((sources, rows, LANES), jnp.bfloat16),
            pltpu.VMEM((total // B, HD, LANES), jnp.bfloat16),
            pltpu.VMEM(shape, jnp.bfloat16),
            pltpu.VMEM((id_rows, LANES), jnp.int32),
            pltpu.SMEM((id_rows, LANES), jnp.int32),
            pltpu.SemaphoreType.DMA((sources + 2 + quads // per,)),
        ],
        compiler_params=pltpu.CompilerParams(vmem_limit_bytes=limit),
        cost_estimate=pl.CostEstimate(
            flops=16 * HD * pairs, bytes_accessed=4 << 20, transcendentals=pairs
        ),
        name="attend",
    )(*operands)


def project_out(head_count, own_ref, turned_ref, here_ref, there_ref, *refs):
    out_ref = refs[-1]
    axis = turned_ref.shape[0] // head_count
    total = None
    for weight_ref, at in ((here_ref, own_ref[0]), (there_ref, 1 - own_ref[0])):
        heads = [turned_ref[h * axis + at] for h in range(head_count)]
        value = lax.dot_general(
            jnp.concatenate(heads, axis=0),
            weight_ref[...],
            (((0,), (0,)), ((), ())),
            preferred_element_type=jnp.float32,
        )
        total = value if total is None else total + value
    out_ref[...] = total.astype(jnp.bfloat16)


def output_rows(turned, here, there, head_count, chunk, chunks, before):
    rows = turned.shape[2]
    width = here.shape[1]
    return pl.pallas_call(
        functools.partial(project_out, head_count),
        grid_spec=pltpu.PrefetchScalarGridSpec(
            num_scalar_prefetch=1,
            grid=(1,),
            in_specs=[
                pl.BlockSpec(turned.shape, lambda i, _: (0, 0, 0)),
                pl.BlockSpec(here.shape, lambda i, _: (0, 0)),
                pl.BlockSpec(there.shape, lambda i, _: (0, 0)),
            ]
            + [pl.BlockSpec(memory_space=pl.ANY)] * len(before),
            out_specs=pl.BlockSpec((rows, width), lambda i, _: (chunk, 0)),
        ),
        out_shape=jax.ShapeDtypeStruct((rows * chunks, width), jnp.bfloat16),
        input_output_aliases={4: 0} if before else {},
        compiler_params=pltpu.CompilerParams(vmem_limit_bytes=20 * MIB),
        cost_estimate=pl.CostEstimate(
            flops=4 * rows * width * here.shape[0], bytes_accessed=3 << 20, transcendentals=0
        ),
        name="project_out",
    )(lax.axis_index("head").reshape(1), turned, here, there, *before)


def shards(history, qkv_weight, out_weight, rand_blocks):
    tok_rows = history.shape[0]
    head_count = qkv_weight.shape[2] // HD
    seq_count = lax.axis_size("seq")
    blocks_dev = tok_rows // B
    total_blocks = blocks_dev * seq_count
    group_count = seq_count // head_count
    seq_at = lax.axis_index("seq")
    direct = group_count == 1 and lax.axis_size("head") == 2
    chunks = 2 if direct else 1
    place = seq_at if direct else jnp.zeros((), jnp.int32)
    first, later = project(history, qkv_weight, rand_blocks, place, chunks)
    half = tok_rows // 2 // chunks

    if direct:
        pieces = list(first)
        for k in sorted(range(1, seq_count), key=lambda k: abs(2 * k - seq_count)):
            pairs = [(i, (i + k) % seq_count) for i in range(seq_count)]
            pieces[k] = lax.ppermute(first[k], "seq", pairs)
        here, later[0] = lax.optimization_barrier((out_weight, later[0]))
        there = lax.ppermute(here, "head", [(0, 1), (1, 0)])
        place = place.reshape(1)
        per = half // (2 * B)
        outs = []
        for chunk in range(chunks):
            operands = [place] + pieces
            if chunk > 0:
                query, pieces = lax.optimization_barrier((later[chunk - 1], pieces))
                query = lax.all_to_all(query, "seq", 0, 0, tiled=True)
                query, outs[-1] = lax.optimization_barrier((query, outs[-1]))
                operands.append(query)
            places = [
                [
                    (
                        n // per,
                        x * (blocks_dev // 2) + chunk * 2 * per + 2 * (n % per) + i,
                    )
                    for i in range(2)
                    for x in range(2)
                ]
                for n in range(seq_count * per)
            ]
            plan = (tok_rows, blocks_dev, total_blocks, places, per, False, True, chunk == 0)
            out = attention(operands, plan, per, seq_count, 62 * MIB)
            outs.append(out.reshape(2 * seq_count, HD, half))
        outs = [lax.all_to_all(out, ("seq", "head"), 0, 0, tiled=True) for out in outs]
        result = []
        for chunk in range(chunks):
            operands = (outs[chunk], out_weight, there)
            result = [output_rows(*operands, head_count, chunk, chunks, result)]
        return result[0]

    first = jnp.stack(first)
    key_value = lax.all_gather(first[:, :tok_rows], "seq")
    key_value = lax.dynamic_index_in_dim(key_value, seq_at // group_count, 1, False)
    group_blocks = blocks_dev // group_count
    blocks = seq_count * group_blocks
    query = first[:, tok_rows : tok_rows + half]
    query = query.reshape(head_count, half, 2, HD).transpose(0, 2, 1, 3)
    query = lax.all_to_all(query.reshape(seq_count, -1, HD), "seq", 0, 0, tiled=True)
    query = query.reshape(blocks // QUAD, 2, 2, B, HD).transpose(0, 1, 3, 2, 4)
    query = query.reshape(blocks // QUAD, 2 * B, LANES)
    ids = rand_blocks.reshape(seq_count, group_blocks, R)
    ids = lax.all_to_all(ids, "seq", 0, 0, tiled=True).reshape(blocks, R)
    ids = jnp.pad(ids, ((0, 0), (0, LANES - R)))
    offset = seq_at % group_count * group_blocks
    ids = ids.at[:, LANES - 1].set(offset)
    places = [
        [((n * QUAD + b) // group_blocks, (n * QUAD + b) % group_blocks) for b in range(QUAD)]
        for n in range(blocks // QUAD)
    ]
    global_quads = -(-GBLOCKS // group_count // QUAD)
    plan = (tok_rows, blocks_dev, total_blocks, places, global_quads, True, False, False)
    out = attention([key_value, query, ids], plan, 1, seq_count, 56 * MIB)
    out = out.reshape(blocks // QUAD, 2, HD, 2, B).transpose(0, 3, 1, 4, 2)
    out = lax.all_to_all(out.reshape(seq_count, -1, HD), "seq", 0, 0, tiled=True)
    attn = out.reshape(head_count, tok_rows, HD).transpose(1, 0, 2)
    return lax.psum_scatter(
        jnp.dot(
            attn.reshape(tok_rows, head_count * HD),
            out_weight,
            preferred_element_type=jnp.float32,
        ).astype(jnp.bfloat16),
        "head",
        scatter_dimension=0,
        tiled=True,
    )


def solution(mesh):
    placed = (
        P(("groups", "seq"), None),
        P(None, None, "head"),
        P("head", None),
        P("head", ("groups", "seq"), None),
    )
    return jax.shard_map(
        shards,
        mesh=mesh,
        in_specs=placed,
        out_specs=P(("groups", "seq", "head"), None),
        check_vma=False,
    )
```

```python
import functools
import math

import jax
import jax.numpy as jnp
from jax import lax
from jax.experimental import pallas as pl
from jax.experimental.pallas import tpu as pltpu
from jax.sharding import PartitionSpec as P

B = 64
R = 3
G = 1024
HD = 64
GBLOCKS = 16
LANES = 2 * HD
QUAD = 4
NEAR = 3 + R
SUM_ROWS = 16
ID_BASE = 256
ID_ROWS = 16
MIB = 1024 * 1024

AHEAD = 2

masked_score = -1e30
least_sum, most_sum = 1e-25, 1e30


def dot_nt(a, b):
    return lax.dot_general(a, b, (((1,), (1,)), ((), ())), preferred_element_type=jnp.float32)


def dot_nn(a, b):
    return jnp.dot(a, b, preferred_element_type=jnp.float32)


def left_half(rows):
    return lax.broadcasted_iota(jnp.int32, (rows, LANES), 1) < HD


def swap_halves(value):
    return jnp.concatenate([value[:, HD:], value[:, :HD]], axis=1)


def pair_rows(value):
    half = value.shape[0] // 2
    left = left_half(half)
    top, low = value[:half], value[half:]
    return jnp.where(left, top, swap_halves(low)), jnp.where(left, swap_halves(top), low)


def project_first(half, place_ref, history_hbm, weight_hbm, ids_ref, *refs):
    *outs, history_ref, weight_ref, out_ref, sems = refs
    rows = history_ref.shape[0]
    heads = out_ref.shape[0]
    step = min(4, heads)
    runs = heads // step
    width = step * HD
    loads = [pltpu.make_async_copy(history_hbm, history_ref, sems.at[0])]
    for run in range(runs):
        at = (slice(None), slice(None), pl.ds(run * width, width))
        loads.append(
            pltpu.make_async_copy(weight_hbm.at[at], weight_ref.at[at], sems.at[1 + run])
        )
    for load in loads:
        load.start()
    for head in range(heads):
        out_ref[head, rows + half :] = jnp.zeros((ID_ROWS, LANES), jnp.bfloat16)
        ids = [ids_ref[r, head : head + 1] for r in range(R)]
        ids = [v % ID_BASE for v in ids] + [v // ID_BASE for v in ids]
        ids.append(jnp.zeros((ID_ROWS - 2 * R, ids_ref.shape[2]), jnp.int32))
        ids = jnp.concatenate(ids, axis=0).astype(jnp.float32).astype(jnp.bfloat16)
        out_ref[head, rows + half :, : ids.shape[1]] = ids

    def product(unit):
        run, kind = unit
        lanes = slice(run * width, (run + 1) * width)
        if kind == 0:
            return dot_nn(history_ref[...], weight_ref[1, :, lanes])
        if kind == 1:
            return lax.dot_general(
                weight_ref[2, :, lanes],
                history_ref[...],
                (((0,), (1,)), ((), ())),
                preferred_element_type=jnp.float32,
            )
        return project_half(history_ref, weight_ref[0, :, lanes], 0, half)

    def place(unit, value):
        run, kind = unit
        value = value.astype(jnp.bfloat16)
        for head in range(run * step, (run + 1) * step):
            j = head - run * step
            if kind == 1:
                for i in range(rows // LANES):
                    tile = value[j * HD : (j + 1) * HD, i * LANES : (i + 1) * LANES]
                    out_ref[head, rows // 2 + i * HD : rows // 2 + (i + 1) * HD] = tile
            elif j % 2 == 0:
                pair = pair_rows(value[:, j * HD : (j + 2) * HD])
                at = 0 if kind == 0 else rows
                for k in range(2):
                    out_ref[head + k, at : at + pair[k].shape[0]] = pair[k]

    units = [(run, kind) for run in range(runs) for kind in range(3)]
    for load in loads[:2]:
        load.wait()
    value = product(units[0])
    for n, unit in enumerate(units):
        later = None
        if n + 1 < len(units):
            if units[n + 1][0] > unit[0]:
                loads[1 + units[n + 1][0]].wait()
            later = product(units[n + 1])
        place(unit, value)
        value = later
    stores = [
        pltpu.make_async_copy(
            out_ref.at[lax.rem(place_ref[0] + k, heads)], out, sems.at[1 + runs + k]
        )
        for k, out in enumerate(outs)
    ]
    for store in stores:
        store.start()
    for store in stores:
        store.wait()


def project_half(history_ref, weight, first, half):
    middle = history_ref.shape[0] // 2
    chosen = jnp.concatenate(
        [
            history_ref[first : first + half],
            history_ref[middle + first : middle + first + half],
        ],
        axis=0,
    )
    return dot_nn(chosen, weight) * (1.0 / math.sqrt(HD))


def project_later(first, history_ref, weight_ref, out_ref):
    half = out_ref.shape[1]
    query = project_half(history_ref, weight_ref[0], first, half).astype(jnp.bfloat16)
    for j in range(0, out_ref.shape[0], 2):
        pair = pair_rows(query[:, j * HD : (j + 2) * HD])
        out_ref[j] = pair[0]
        out_ref[j + 1] = pair[1]


def project(history, qkv_weight, ids, place, chunks):
    rows, width = history.shape
    heads = qkv_weight.shape[2] // HD
    half = rows // 2 // chunks
    total = rows + half + ID_ROWS
    whole = pl.BlockSpec((rows, width), lambda i: (0, 0))
    params = pltpu.CompilerParams(vmem_limit_bytes=56 * MIB)
    first = pl.pallas_call(
        functools.partial(project_first, half),
        in_specs=[
            pl.BlockSpec(memory_space=pltpu.SMEM),
            pl.BlockSpec(memory_space=pltpu.HBM),
            pl.BlockSpec(memory_space=pltpu.HBM),
            pl.BlockSpec(memory_space=pltpu.VMEM),
        ],
        out_specs=[pl.BlockSpec(memory_space=pltpu.HBM)] * heads,
        out_shape=[jax.ShapeDtypeStruct((total, LANES), jnp.bfloat16)] * heads,
        scratch_shapes=[
            pltpu.VMEM(history.shape, jnp.bfloat16),
            pltpu.VMEM(qkv_weight.shape, jnp.bfloat16),
            pltpu.VMEM((heads, total, LANES), jnp.bfloat16),
            pltpu.SemaphoreType.DMA((1 + 2 * heads,)),
        ],
        compiler_params=params,
        cost_estimate=pl.CostEstimate(
            flops=5 * rows * width * heads * HD, bytes_accessed=6 << 20, transcendentals=0
        ),
        name="project_first",
    )(place.reshape(1), history, qkv_weight, ids.transpose(2, 0, 1))
    later = []
    step = min(4, heads)
    for chunk in range(1, chunks):
        history, first = lax.optimization_barrier((history, first))
        later.append(
            pl.pallas_call(
                functools.partial(project_later, chunk * half),
                grid=(heads // step,),
                in_specs=[whole, pl.BlockSpec((1, width, step * HD), lambda i: (0, 0, i))],
                out_specs=pl.BlockSpec((step, half, LANES), lambda i: (i, 0, 0)),
                out_shape=jax.ShapeDtypeStruct((heads, half, LANES), jnp.bfloat16),
                compiler_params=params,
                cost_estimate=pl.CostEstimate(
                    flops=4 * half * width * heads * HD, bytes_accessed=4 << 20, transcendentals=0
                ),
                name="project_later",
            )(history, qkv_weight)
        )
    return first, later


def attend(plan, *refs):
    rows, blocks_dev, total_blocks, places, global_quads, mixed, carried, within = plan
    kv_ref, keys_ref, values_ref, turned_ref, ids_vmem, ids_ref, sems = refs[-7:]
    out_hbm, query_ref = refs[-9:-7]
    sources = kv_ref.shape[0]
    half = rows // 2
    quads = len(places)
    group_blocks = blocks_dev if carried else quads * QUAD // sources
    per = turned_ref.shape[3] // LANES
    pairs = rows // LANES
    left = left_half(B)
    zero = jnp.zeros((B, LANES), jnp.bfloat16)
    if carried:
        place_ref, *pieces = refs[: 1 + sources]
        loads = [
            pltpu.make_async_copy(
                piece, kv_ref.at[lax.rem(place_ref[0] + sources - k, sources)], sems.at[k]
            )
            for k, piece in enumerate(pieces)
        ]
        ids_copy = pltpu.make_async_copy(ids_vmem, ids_ref, sems.at[sources + 1])
    else:
        loads = [pltpu.make_async_copy(refs[0], kv_ref, sems.at[0])]
        ids_copy = pltpu.make_async_copy(refs[2], ids_ref, sems.at[sources + 1])
        loads.append(ids_copy)
    if not within:
        query_hbm = refs[1 + sources] if carried else refs[1]
        loads.append(pltpu.make_async_copy(query_hbm, query_ref, sems.at[sources]))
    for load in loads:
        load.start()
    stores = [
        pltpu.make_async_copy(
            turned_ref.at[pl.ds(i, 1)], out_hbm.at[pl.ds(i, 1)], sems.at[sources + 2 + i]
        )
        for i in range(quads // per)
    ]

    def spread_ids():
        end = kv_ref.shape[1]
        for source in range(sources):
            ids_vmem[source * ID_ROWS : (source + 1) * ID_ROWS] = (
                kv_ref[source, end - ID_ROWS :].astype(jnp.float32).astype(jnp.int32)
            )
        ids_copy.start()

    def rand_of(source, local):
        if carried:
            at = source * ID_ROWS
            return [
                ids_ref[at + r, local] + ids_ref[at + R + r, local] * ID_BASE for r in range(R)
            ]
        return [ids_ref[source * group_blocks + local, r] for r in range(R)]

    def build(source):
        packed = kv_ref[source, :half]
        wide = left_half(half)
        other = swap_halves(packed)
        keys_ref[source, :half] = jnp.where(wide, packed, other)
        keys_ref[source, half:] = jnp.where(wide, other, packed)
        for i in range(pairs):
            tile = kv_ref[source, half + i * HD : half + (i + 1) * HD]
            turned = swap_halves(tile)
            values_ref[source * 2 * pairs + 2 * i] = jnp.where(left, tile, turned)
            values_ref[source * 2 * pairs + 2 * i + 1] = jnp.where(left, turned, tile)

    def turned_values(source):
        tiles = [kv_ref[source, half + i * HD : half + (i + 1) * HD] for i in range(pairs)]
        ones = jnp.ones((SUM_ROWS, rows), jnp.bfloat16)
        return jnp.concatenate([jnp.concatenate(tiles, axis=1), ones], axis=0)

    def queries_of(quad):
        parts = []
        for i in range(2):
            if within:
                at = rows + (quad % per * 2 + i) * B
                packed = kv_ref[quad // per, at : at + B]
            else:
                at = (quad % per * 2 + i) * B
                packed = query_ref[quad // per, at : at + B]
            parts.append(jnp.where(left, packed, zero))
            parts.append(jnp.where(left, zero, packed))
        return parts

    def write(quad, acc, sums):
        total = acc[HD : HD + 1]
        sums.append(total)
        value = acc[:HD] / total
        first, second = value[:, :LANES], value[:, LANES:]
        at = slice(quad % per * LANES, (quad % per + 1) * LANES)
        turned_ref[quad // per, 0, :, at] = jnp.where(left, first, swap_halves(second)).astype(
            jnp.bfloat16
        )
        turned_ref[quad // per, 1, :, at] = jnp.where(left, swap_halves(first), second).astype(
            jnp.bfloat16
        )
        if quad % per == per - 1:
            stores[quad // per].start()

    def full_rows(exact):
        query = jnp.concatenate([p for n in range(global_quads) for p in queries_of(n)], axis=0)

        def score(source):
            return dot_nt(keys_ref[source], query)

        def fold(source, scores, carry):
            top, acc = carry
            if exact:
                new_top = jnp.maximum(top, jnp.max(scores, 0, keepdims=True))
                acc = acc * jnp.exp(top - new_top)
                top = new_top
                scores = scores - top
            weights = jnp.exp(scores).astype(jnp.bfloat16)
            return top, acc + dot_nn(turned_values(source), weights)

        carry = (
            jnp.full((1, query.shape[0]), -jnp.inf, jnp.float32),
            jnp.zeros((HD + SUM_ROWS, query.shape[0]), jnp.float32),
        )
        if sources <= 8 and not exact:
            build(0)
            scores = score(0)
            if carried:
                spread_ids()
            for source in range(sources):
                later = None
                if source + 1 < sources:
                    build(source + 1)
                    later = score(source + 1)
                carry = fold(source, scores, carry)
                scores = later
        else:
            if not exact:
                if carried:
                    spread_ids()
                lax.fori_loop(0, sources, lambda i, _: (build(i), 0)[1], 0)
            carry = lax.fori_loop(0, sources, lambda i, c: fold(i, score(i), c), carry)
        width = QUAD * B
        return [carry[1][:, n * width : (n + 1) * width] for n in range(global_quads)]

    def block_of(place):
        source, local = place
        if carried:
            return source * blocks_dev + local
        return source * blocks_dev + ids_ref[source * group_blocks, LANES - 1] + local

    def key_block(block):
        at = block % blocks_dev if isinstance(block, int) else lax.rem(block, blocks_dev)
        source = block // blocks_dev if isinstance(block, int) else lax.div(block, blocks_dev)
        return keys_ref[source, pl.ds(at * B if isinstance(at, int) else pl.multiple_of(at * B, B), B)]

    def near_scores(quad):
        parts = queries_of(quad)
        glob_scores = dot_nt(keys_ref[0], jnp.concatenate(parts, axis=0))
        lists = []
        column = lax.broadcasted_iota(jnp.int32, (1, QUAD * B), 1) // B
        low = high = None
        for b, (source, local) in enumerate(places[quad]):
            block = block_of((source, local))
            if carried:
                window = [max(block - 1, 0), block, min(block + 1, total_blocks - 1)]
                dead_low, dead_high = block - 1 < GBLOCKS, block + 1 >= total_blocks
                if dead_low:
                    low = column == b if low is None else low | (column == b)
                if dead_high:
                    high = column == b if high is None else high | (column == b)
            else:
                window = [
                    jnp.maximum(block - 1, 0),
                    block,
                    jnp.minimum(block + 1, total_blocks - 1),
                ]
                one = (column == b) & (block - 1 < GBLOCKS)
                two = (column == b) & (block + 1 >= total_blocks)
                low = one if low is None else low | one
                high = two if high is None else high | two
            lists.append(window + rand_of(source, local))
        near_keys = []
        for b in range(0, QUAD, 2):
            tiles = [
                jnp.where(left, key_block(lists[b][k]), key_block(lists[b + 1][k]))
                for k in range(NEAR)
            ]
            near_keys.append(jnp.concatenate(tiles, axis=0))
        blank = jnp.zeros((2 * B, LANES), jnp.bfloat16)
        diagonal = jnp.concatenate(
            [
                jnp.concatenate(parts[:2] + [blank], axis=0),
                jnp.concatenate([blank] + parts[2:], axis=0),
            ],
            axis=1,
        )
        scores = dot_nt(jnp.concatenate(near_keys, axis=1), diagonal)
        if low is not None or high is not None:
            before, after = scores[:B], scores[2 * B : 3 * B]
            if low is not None:
                before = jnp.where(low, masked_score, before)
            if high is not None:
                after = jnp.where(high, masked_score, after)
            scores = jnp.concatenate([before, scores[B : 2 * B], after, scores[3 * B :]], axis=0)
        return glob_scores, scores, lists

    def near_finish(exact, glob_scores, scores, lists):
        if exact:
            top = jnp.maximum(
                jnp.max(glob_scores, 0, keepdims=True), jnp.max(scores, 0, keepdims=True)
            )
            glob_scores, scores = glob_scores - top, scores - top
        glob_weights = jnp.exp(glob_scores).astype(jnp.bfloat16)
        weights = jnp.exp(scores).astype(jnp.bfloat16)
        near_values = [
            jnp.concatenate(
                [
                    jnp.where(left, values_ref[lists[b][k]], values_ref[lists[b][k + 1]])
                    for k in range(0, NEAR, 2)
                ],
                axis=1,
            )
            for b in range(QUAD)
        ]
        near_values.append(jnp.ones((SUM_ROWS, NEAR * B), jnp.bfloat16))
        near = dot_nn(jnp.concatenate(near_values, axis=0), weights)
        own = jnp.concatenate(
            [
                jnp.where(left, near[:HD, :LANES], near[HD : 2 * HD, :LANES]),
                jnp.where(left, near[2 * HD : 3 * HD, LANES:], near[3 * HD : 4 * HD, LANES:]),
            ],
            axis=1,
        )
        return dot_nn(turned_values(0), glob_weights) + jnp.concatenate(
            [own, near[QUAD * HD :]], axis=0
        )

    for load in loads:
        load.wait()

    def run(exact):
        sums = []
        glob = full_rows(exact)
        if carried and not exact:
            ids_copy.wait()
        if not mixed:
            for quad in range(global_quads):
                write(quad, glob[quad], sums)
        first = 0 if mixed else global_quads
        ahead = 1 if exact else AHEAD
        ready = [near_scores(quad) for quad in range(first, min(first + ahead, quads))]
        for quad in range(first, quads):
            if quad + ahead < quads:
                ready.append(near_scores(quad + ahead))
            acc = near_finish(exact, *ready[quad - first])
            if quad < global_quads:
                column = lax.broadcasted_iota(jnp.int32, (1, QUAD * B), 1) // B
                own = functools.reduce(
                    jnp.logical_or,
                    [
                        (column == b) & (block_of(p) < GBLOCKS)
                        for b, p in enumerate(places[quad])
                    ],
                )
                acc = jnp.where(own, glob[quad], acc)
            write(quad, acc, sums)
        for store in stores:
            store.wait()
        return jnp.concatenate(sums, axis=0)

    sums = run(False)
    bad = jnp.where((sums >= least_sum) & (sums <= most_sum), 0.0, 1.0)

    @pl.when(jnp.max(bad) > 0.0)
    def _():
        run(True)


def attention(operands, plan, per, sources, limit):
    rows, blocks_dev, _, places = plan[:4]
    quads = len(places)
    carried, within = plan[6:]
    size = operands[1].shape if carried else operands[0].shape[1:]
    total = sources * rows
    pairs = QUAD * B * (quads * (G + NEAR * B) + total)
    id_rows = sources * ID_ROWS if carried else quads * QUAD
    hbm = pl.BlockSpec(memory_space=pltpu.HBM)
    shape = (quads // per, 2, HD, per * LANES)
    query_shape = (8, LANES) if within else operands[-1 if carried else 1].shape
    specs = [hbm] * len(operands)
    if carried:
        specs[0] = pl.BlockSpec(memory_space=pltpu.SMEM)
    return pl.pallas_call(
        functools.partial(attend, plan),
        in_specs=specs,
        out_specs=hbm,
        out_shape=jax.ShapeDtypeStruct(shape, jnp.bfloat16),
        scratch_shapes=[
            pltpu.VMEM(query_shape, jnp.bfloat16),
            pltpu.VMEM((sources,) + size, jnp.bfloat16),
            pltpu.VMEM((sources, rows, LANES), jnp.bfloat16),
            pltpu.VMEM((total // B, HD, LANES), jnp.bfloat16),
            pltpu.VMEM(shape, jnp.bfloat16),
            pltpu.VMEM((id_rows, LANES), jnp.int32),
            pltpu.SMEM((id_rows, LANES), jnp.int32),
            pltpu.SemaphoreType.DMA((sources + 2 + quads // per,)),
        ],
        compiler_params=pltpu.CompilerParams(vmem_limit_bytes=limit),
        cost_estimate=pl.CostEstimate(
            flops=16 * HD * pairs, bytes_accessed=4 << 20, transcendentals=pairs
        ),
        name="attend",
    )(*operands)


def project_out(head_count, own_ref, turned_ref, here_ref, there_ref, *refs):
    out_ref = refs[-1]
    axis = turned_ref.shape[0] // head_count
    total = None
    for weight_ref, at in ((here_ref, own_ref[0]), (there_ref, 1 - own_ref[0])):
        heads = [turned_ref[h * axis + at] for h in range(head_count)]
        value = lax.dot_general(
            jnp.concatenate(heads, axis=0),
            weight_ref[...],
            (((0,), (0,)), ((), ())),
            preferred_element_type=jnp.float32,
        )
        total = value if total is None else total + value
    out_ref[...] = total.astype(jnp.bfloat16)


def output_rows(turned, here, there, head_count, chunk, chunks, before):
    rows = turned.shape[2]
    width = here.shape[1]
    return pl.pallas_call(
        functools.partial(project_out, head_count),
        grid_spec=pltpu.PrefetchScalarGridSpec(
            num_scalar_prefetch=1,
            grid=(1,),
            in_specs=[
                pl.BlockSpec(turned.shape, lambda i, _: (0, 0, 0)),
                pl.BlockSpec(here.shape, lambda i, _: (0, 0)),
                pl.BlockSpec(there.shape, lambda i, _: (0, 0)),
            ]
            + [pl.BlockSpec(memory_space=pl.ANY)] * len(before),
            out_specs=pl.BlockSpec((rows, width), lambda i, _: (chunk, 0)),
        ),
        out_shape=jax.ShapeDtypeStruct((rows * chunks, width), jnp.bfloat16),
        input_output_aliases={4: 0} if before else {},
        compiler_params=pltpu.CompilerParams(vmem_limit_bytes=20 * MIB),
        cost_estimate=pl.CostEstimate(
            flops=4 * rows * width * here.shape[0], bytes_accessed=3 << 20, transcendentals=0
        ),
        name="project_out",
    )(lax.axis_index("head").reshape(1), turned, here, there, *before)


def shards(history, qkv_weight, out_weight, rand_blocks):
    tok_rows = history.shape[0]
    head_count = qkv_weight.shape[2] // HD
    seq_count = lax.axis_size("seq")
    blocks_dev = tok_rows // B
    total_blocks = blocks_dev * seq_count
    group_count = seq_count // head_count
    seq_at = lax.axis_index("seq")
    direct = group_count == 1 and lax.axis_size("head") == 2
    chunks = 2 if direct else 1
    place = seq_at if direct else jnp.zeros((), jnp.int32)
    first, later = project(history, qkv_weight, rand_blocks, place, chunks)
    half = tok_rows // 2 // chunks

    if direct:
        pieces = list(first)
        for k in sorted(range(1, seq_count), key=lambda k: abs(2 * k - seq_count)):
            pairs = [(i, (i + k) % seq_count) for i in range(seq_count)]
            pieces[k] = lax.ppermute(first[k], "seq", pairs)
        here, later[0] = lax.optimization_barrier((out_weight, later[0]))
        there = lax.ppermute(here, "head", [(0, 1), (1, 0)])
        early = pieces[1 : seq_count // 2 + 1]
        early, later[0], there = lax.optimization_barrier((early, later[0], there))
        pieces[1 : seq_count // 2 + 1] = early
        place = place.reshape(1)
        per = half // (2 * B)
        outs = []
        for chunk in range(chunks):
            operands = [place] + pieces
            if chunk > 0:
                query = lax.all_to_all(later[chunk - 1], "seq", 0, 0, tiled=True)
                query, outs[-1] = lax.optimization_barrier((query, outs[-1]))
                operands.append(query)
            places = [
                [
                    (
                        n // per,
                        x * (blocks_dev // 2) + chunk * 2 * per + 2 * (n % per) + i,
                    )
                    for i in range(2)
                    for x in range(2)
                ]
                for n in range(seq_count * per)
            ]
            plan = (tok_rows, blocks_dev, total_blocks, places, per, False, True, chunk == 0)
            out = attention(operands, plan, per, seq_count, 62 * MIB)
            outs.append(out.reshape(2 * seq_count, HD, half))
        outs = [lax.all_to_all(out, ("seq", "head"), 0, 0, tiled=True) for out in outs]
        result = []
        for chunk in range(chunks):
            operands = (outs[chunk], out_weight, there)
            result = [output_rows(*operands, head_count, chunk, chunks, result)]
        return result[0]

    first = jnp.stack(first)
    key_value = lax.all_gather(first[:, :tok_rows], "seq")
    key_value = lax.dynamic_index_in_dim(key_value, seq_at // group_count, 1, False)
    group_blocks = blocks_dev // group_count
    blocks = seq_count * group_blocks
    query = first[:, tok_rows : tok_rows + half]
    query = query.reshape(head_count, half, 2, HD).transpose(0, 2, 1, 3)
    query = lax.all_to_all(query.reshape(seq_count, -1, HD), "seq", 0, 0, tiled=True)
    query = query.reshape(blocks // QUAD, 2, 2, B, HD).transpose(0, 1, 3, 2, 4)
    query = query.reshape(blocks // QUAD, 2 * B, LANES)
    ids = rand_blocks.reshape(seq_count, group_blocks, R)
    ids = lax.all_to_all(ids, "seq", 0, 0, tiled=True).reshape(blocks, R)
    ids = jnp.pad(ids, ((0, 0), (0, LANES - R)))
    offset = seq_at % group_count * group_blocks
    ids = ids.at[:, LANES - 1].set(offset)
    places = [
        [((n * QUAD + b) // group_blocks, (n * QUAD + b) % group_blocks) for b in range(QUAD)]
        for n in range(blocks // QUAD)
    ]
    global_quads = -(-GBLOCKS // group_count // QUAD)
    plan = (tok_rows, blocks_dev, total_blocks, places, global_quads, True, False, False)
    out = attention([key_value, query, ids], plan, 1, seq_count, 56 * MIB)
    out = out.reshape(blocks // QUAD, 2, HD, 2, B).transpose(0, 3, 1, 4, 2)
    out = lax.all_to_all(out.reshape(seq_count, -1, HD), "seq", 0, 0, tiled=True)
    attn = out.reshape(head_count, tok_rows, HD).transpose(1, 0, 2)
    return lax.psum_scatter(
        jnp.dot(
            attn.reshape(tok_rows, head_count * HD),
            out_weight,
            preferred_element_type=jnp.float32,
        ).astype(jnp.bfloat16),
        "head",
        scatter_dimension=0,
        tiled=True,
    )


def solution(mesh):
    placed = (
        P(("groups", "seq"), None),
        P(None, None, "head"),
        P("head", None),
        P("head", ("groups", "seq"), None),
    )
    return jax.shard_map(
        shards,
        mesh=mesh,
        in_specs=placed,
        out_specs=P(("groups", "seq", "head"), None),
        check_vma=False,
    )
```

```python
import functools
import math

import jax
import jax.numpy as jnp
from jax import lax
from jax.experimental import pallas as pl
from jax.experimental.pallas import tpu as pltpu
from jax.sharding import PartitionSpec as P

B = 64
R = 3
G = 1024
HD = 64
GBLOCKS = 16
LANES = 2 * HD
QUAD = 4
NEAR = 3 + R
SUM_ROWS = 16
ID_BASE = 256
ID_ROWS = 16
MIB = 1024 * 1024

AHEAD = 2

masked_score = -1e30
least_sum, most_sum = 1e-25, 1e30


def dot_nt(a, b):
    return lax.dot_general(a, b, (((1,), (1,)), ((), ())), preferred_element_type=jnp.float32)


def dot_nn(a, b):
    return jnp.dot(a, b, preferred_element_type=jnp.float32)


def left_half(rows):
    return lax.broadcasted_iota(jnp.int32, (rows, LANES), 1) < HD


def swap_halves(value):
    return jnp.concatenate([value[:, HD:], value[:, :HD]], axis=1)


def pair_rows(value):
    half = value.shape[0] // 2
    left = left_half(half)
    top, low = value[:half], value[half:]
    return jnp.where(left, top, swap_halves(low)), jnp.where(left, swap_halves(top), low)


def project_first(half, place_ref, history_hbm, weight_hbm, ids_ref, *refs):
    *outs, history_ref, weight_ref, out_ref, sems = refs
    rows = history_ref.shape[0]
    heads = out_ref.shape[0]
    step = min(4, heads)
    runs = heads // step
    width = step * HD
    loads = [pltpu.make_async_copy(history_hbm, history_ref, sems.at[0])]
    for run in range(runs):
        at = (slice(None), slice(None), pl.ds(run * width, width))
        loads.append(
            pltpu.make_async_copy(weight_hbm.at[at], weight_ref.at[at], sems.at[1 + run])
        )
    for load in loads:
        load.start()
    for head in range(heads):
        out_ref[head, rows + half :] = jnp.zeros((ID_ROWS, LANES), jnp.bfloat16)
        ids = [ids_ref[r, head : head + 1] for r in range(R)]
        ids = [v % ID_BASE for v in ids] + [v // ID_BASE for v in ids]
        ids.append(jnp.zeros((ID_ROWS - 2 * R, ids_ref.shape[2]), jnp.int32))
        ids = jnp.concatenate(ids, axis=0).astype(jnp.float32).astype(jnp.bfloat16)
        out_ref[head, rows + half :, : ids.shape[1]] = ids

    def product(unit):
        run, kind = unit
        lanes = slice(run * width, (run + 1) * width)
        if kind == 0:
            return dot_nn(history_ref[...], weight_ref[1, :, lanes])
        if kind == 1:
            return lax.dot_general(
                weight_ref[2, :, lanes],
                history_ref[...],
                (((0,), (1,)), ((), ())),
                preferred_element_type=jnp.float32,
            )
        return project_half(history_ref, weight_ref[0, :, lanes], 0, half)

    def place(unit, value):
        run, kind = unit
        value = value.astype(jnp.bfloat16)
        for head in range(run * step, (run + 1) * step):
            j = head - run * step
            if kind == 1:
                for i in range(rows // LANES):
                    tile = value[j * HD : (j + 1) * HD, i * LANES : (i + 1) * LANES]
                    out_ref[head, rows // 2 + i * HD : rows // 2 + (i + 1) * HD] = tile
            elif j % 2 == 0:
                pair = pair_rows(value[:, j * HD : (j + 2) * HD])
                at = 0 if kind == 0 else rows
                for k in range(2):
                    out_ref[head + k, at : at + pair[k].shape[0]] = pair[k]

    units = [(run, kind) for run in range(runs) for kind in range(3)]
    for load in loads[:2]:
        load.wait()
    value = product(units[0])
    for n, unit in enumerate(units):
        later = None
        if n + 1 < len(units):
            if units[n + 1][0] > unit[0]:
                loads[1 + units[n + 1][0]].wait()
            later = product(units[n + 1])
        place(unit, value)
        value = later
    stores = [
        pltpu.make_async_copy(
            out_ref.at[lax.rem(place_ref[0] + k, heads)], out, sems.at[1 + runs + k]
        )
        for k, out in enumerate(outs)
    ]
    for store in stores:
        store.start()
    for store in stores:
        store.wait()


def project_half(history_ref, weight, first, half):
    middle = history_ref.shape[0] // 2
    chosen = jnp.concatenate(
        [
            history_ref[first : first + half],
            history_ref[middle + first : middle + first + half],
        ],
        axis=0,
    )
    return dot_nn(chosen, weight) * (1.0 / math.sqrt(HD))


def project_later(first, history_ref, weight_ref, out_ref):
    half = out_ref.shape[1]
    query = project_half(history_ref, weight_ref[0], first, half).astype(jnp.bfloat16)
    for j in range(0, out_ref.shape[0], 2):
        pair = pair_rows(query[:, j * HD : (j + 2) * HD])
        out_ref[j] = pair[0]
        out_ref[j + 1] = pair[1]


def project(history, qkv_weight, ids, place, chunks):
    rows, width = history.shape
    heads = qkv_weight.shape[2] // HD
    half = rows // 2 // chunks
    total = rows + half + ID_ROWS
    whole = pl.BlockSpec((rows, width), lambda i: (0, 0))
    params = pltpu.CompilerParams(vmem_limit_bytes=56 * MIB)
    first = pl.pallas_call(
        functools.partial(project_first, half),
        in_specs=[
            pl.BlockSpec(memory_space=pltpu.SMEM),
            pl.BlockSpec(memory_space=pltpu.HBM),
            pl.BlockSpec(memory_space=pltpu.HBM),
            pl.BlockSpec(memory_space=pltpu.VMEM),
        ],
        out_specs=[pl.BlockSpec(memory_space=pltpu.HBM)] * heads,
        out_shape=[jax.ShapeDtypeStruct((total, LANES), jnp.bfloat16)] * heads,
        scratch_shapes=[
            pltpu.VMEM(history.shape, jnp.bfloat16),
            pltpu.VMEM(qkv_weight.shape, jnp.bfloat16),
            pltpu.VMEM((heads, total, LANES), jnp.bfloat16),
            pltpu.SemaphoreType.DMA((1 + 2 * heads,)),
        ],
        compiler_params=params,
        cost_estimate=pl.CostEstimate(
            flops=5 * rows * width * heads * HD, bytes_accessed=6 << 20, transcendentals=0
        ),
        name="project_first",
    )(place.reshape(1), history, qkv_weight, ids.transpose(2, 0, 1))
    later = []
    step = min(4, heads)
    for chunk in range(1, chunks):
        history, first = lax.optimization_barrier((history, first))
        later.append(
            pl.pallas_call(
                functools.partial(project_later, chunk * half),
                grid=(heads // step,),
                in_specs=[whole, pl.BlockSpec((1, width, step * HD), lambda i: (0, 0, i))],
                out_specs=pl.BlockSpec((step, half, LANES), lambda i: (i, 0, 0)),
                out_shape=jax.ShapeDtypeStruct((heads, half, LANES), jnp.bfloat16),
                compiler_params=params,
                cost_estimate=pl.CostEstimate(
                    flops=4 * half * width * heads * HD, bytes_accessed=4 << 20, transcendentals=0
                ),
                name="project_later",
            )(history, qkv_weight)
        )
    return first, later


def attend(plan, *refs):
    rows, blocks_dev, total_blocks, places, global_quads, mixed, carried, within = plan
    kv_ref, keys_ref, values_ref, turned_ref, ids_vmem, ids_ref, sems = refs[-7:]
    out_hbm, query_ref = refs[-9:-7]
    sources = kv_ref.shape[0]
    half = rows // 2
    quads = len(places)
    group_blocks = blocks_dev if carried else quads * QUAD // sources
    per = turned_ref.shape[3] // LANES
    pairs = rows // LANES
    left = left_half(B)
    zero = jnp.zeros((B, LANES), jnp.bfloat16)
    if carried:
        place_ref, *pieces = refs[: 1 + sources]
        loads = [
            pltpu.make_async_copy(
                piece, kv_ref.at[lax.rem(place_ref[0] + sources - k, sources)], sems.at[k]
            )
            for k, piece in enumerate(pieces)
        ]
        ids_copy = pltpu.make_async_copy(ids_vmem, ids_ref, sems.at[sources + 1])
    else:
        loads = [pltpu.make_async_copy(refs[0], kv_ref, sems.at[0])]
        ids_copy = pltpu.make_async_copy(refs[2], ids_ref, sems.at[sources + 1])
        loads.append(ids_copy)
    if not within:
        query_hbm = refs[1 + sources] if carried else refs[1]
        loads.append(pltpu.make_async_copy(query_hbm, query_ref, sems.at[sources]))
    for load in loads:
        load.start()
    stores = [
        pltpu.make_async_copy(
            turned_ref.at[pl.ds(i, 1)], out_hbm.at[pl.ds(i, 1)], sems.at[sources + 2 + i]
        )
        for i in range(quads // per)
    ]

    def spread_ids():
        end = kv_ref.shape[1]
        for source in range(sources):
            ids_vmem[source * ID_ROWS : (source + 1) * ID_ROWS] = (
                kv_ref[source, end - ID_ROWS :].astype(jnp.float32).astype(jnp.int32)
            )
        ids_copy.start()

    def rand_of(source, local):
        if carried:
            at = source * ID_ROWS
            return [
                ids_ref[at + r, local] + ids_ref[at + R + r, local] * ID_BASE for r in range(R)
            ]
        return [ids_ref[source * group_blocks + local, r] for r in range(R)]

    def build(source):
        packed = kv_ref[source, :half]
        wide = left_half(half)
        other = swap_halves(packed)
        keys_ref[source, :half] = jnp.where(wide, packed, other)
        keys_ref[source, half:] = jnp.where(wide, other, packed)
        for i in range(pairs):
            tile = kv_ref[source, half + i * HD : half + (i + 1) * HD]
            turned = swap_halves(tile)
            values_ref[source * 2 * pairs + 2 * i] = jnp.where(left, tile, turned)
            values_ref[source * 2 * pairs + 2 * i + 1] = jnp.where(left, turned, tile)

    def turned_values(source):
        tiles = [kv_ref[source, half + i * HD : half + (i + 1) * HD] for i in range(pairs)]
        ones = jnp.ones((SUM_ROWS, rows), jnp.bfloat16)
        return jnp.concatenate([jnp.concatenate(tiles, axis=1), ones], axis=0)

    def queries_of(quad):
        parts = []
        for i in range(2):
            if within:
                at = rows + (quad % per * 2 + i) * B
                packed = kv_ref[quad // per, at : at + B]
            else:
                at = (quad % per * 2 + i) * B
                packed = query_ref[quad // per, at : at + B]
            parts.append(jnp.where(left, packed, zero))
            parts.append(jnp.where(left, zero, packed))
        return parts

    def write(quad, acc, sums):
        total = acc[HD : HD + 1]
        sums.append(total)
        value = acc[:HD] / total
        first, second = value[:, :LANES], value[:, LANES:]
        at = slice(quad % per * LANES, (quad % per + 1) * LANES)
        turned_ref[quad // per, 0, :, at] = jnp.where(left, first, swap_halves(second)).astype(
            jnp.bfloat16
        )
        turned_ref[quad // per, 1, :, at] = jnp.where(left, swap_halves(first), second).astype(
            jnp.bfloat16
        )
        if quad % per == per - 1:
            stores[quad // per].start()

    def full_rows(exact):
        query = jnp.concatenate([p for n in range(global_quads) for p in queries_of(n)], axis=0)

        def score(source):
            return dot_nt(keys_ref[source], query)

        def fold(source, scores, carry):
            top, acc = carry
            if exact:
                new_top = jnp.maximum(top, jnp.max(scores, 0, keepdims=True))
                acc = acc * jnp.exp(top - new_top)
                top = new_top
                scores = scores - top
            weights = jnp.exp(scores).astype(jnp.bfloat16)
            return top, acc + dot_nn(turned_values(source), weights)

        carry = (
            jnp.full((1, query.shape[0]), -jnp.inf, jnp.float32),
            jnp.zeros((HD + SUM_ROWS, query.shape[0]), jnp.float32),
        )
        if sources <= 8 and not exact:
            build(0)
            scores = score(0)
            if carried:
                spread_ids()
            for source in range(sources):
                later = None
                if source + 1 < sources:
                    build(source + 1)
                    later = score(source + 1)
                carry = fold(source, scores, carry)
                scores = later
        else:
            if not exact:
                if carried:
                    spread_ids()
                lax.fori_loop(0, sources, lambda i, _: (build(i), 0)[1], 0)
            carry = lax.fori_loop(0, sources, lambda i, c: fold(i, score(i), c), carry)
        width = QUAD * B
        return [carry[1][:, n * width : (n + 1) * width] for n in range(global_quads)]

    def block_of(place):
        source, local = place
        if carried:
            return source * blocks_dev + local
        return source * blocks_dev + ids_ref[source * group_blocks, LANES - 1] + local

    def key_block(block):
        at = block % blocks_dev if isinstance(block, int) else lax.rem(block, blocks_dev)
        source = block // blocks_dev if isinstance(block, int) else lax.div(block, blocks_dev)
        return keys_ref[source, pl.ds(at * B if isinstance(at, int) else pl.multiple_of(at * B, B), B)]

    def near_scores(quad):
        parts = queries_of(quad)
        glob_scores = dot_nt(keys_ref[0], jnp.concatenate(parts, axis=0))
        lists = []
        column = lax.broadcasted_iota(jnp.int32, (1, QUAD * B), 1) // B
        low = high = None
        for b, (source, local) in enumerate(places[quad]):
            block = block_of((source, local))
            if carried:
                window = [max(block - 1, 0), block, min(block + 1, total_blocks - 1)]
                dead_low, dead_high = block - 1 < GBLOCKS, block + 1 >= total_blocks
                if dead_low:
                    low = column == b if low is None else low | (column == b)
                if dead_high:
                    high = column == b if high is None else high | (column == b)
            else:
                window = [
                    jnp.maximum(block - 1, 0),
                    block,
                    jnp.minimum(block + 1, total_blocks - 1),
                ]
                one = (column == b) & (block - 1 < GBLOCKS)
                two = (column == b) & (block + 1 >= total_blocks)
                low = one if low is None else low | one
                high = two if high is None else high | two
            lists.append(window + rand_of(source, local))
        near_keys = []
        for b in range(0, QUAD, 2):
            tiles = [
                jnp.where(left, key_block(lists[b][k]), key_block(lists[b + 1][k]))
                for k in range(NEAR)
            ]
            near_keys.append(jnp.concatenate(tiles, axis=0))
        blank = jnp.zeros((2 * B, LANES), jnp.bfloat16)
        diagonal = jnp.concatenate(
            [
                jnp.concatenate(parts[:2] + [blank], axis=0),
                jnp.concatenate([blank] + parts[2:], axis=0),
            ],
            axis=1,
        )
        scores = dot_nt(jnp.concatenate(near_keys, axis=1), diagonal)
        if low is not None or high is not None:
            before, after = scores[:B], scores[2 * B : 3 * B]
            if low is not None:
                before = jnp.where(low, masked_score, before)
            if high is not None:
                after = jnp.where(high, masked_score, after)
            scores = jnp.concatenate([before, scores[B : 2 * B], after, scores[3 * B :]], axis=0)
        return glob_scores, scores, lists

    def near_finish(exact, glob_scores, scores, lists):
        if exact:
            top = jnp.maximum(
                jnp.max(glob_scores, 0, keepdims=True), jnp.max(scores, 0, keepdims=True)
            )
            glob_scores, scores = glob_scores - top, scores - top
        glob_weights = jnp.exp(glob_scores).astype(jnp.bfloat16)
        weights = jnp.exp(scores).astype(jnp.bfloat16)
        near_values = [
            jnp.concatenate(
                [
                    jnp.where(left, values_ref[lists[b][k]], values_ref[lists[b][k + 1]])
                    for k in range(0, NEAR, 2)
                ],
                axis=1,
            )
            for b in range(QUAD)
        ]
        near_values.append(jnp.ones((SUM_ROWS, NEAR * B), jnp.bfloat16))
        near = dot_nn(jnp.concatenate(near_values, axis=0), weights)
        own = jnp.concatenate(
            [
                jnp.where(left, near[:HD, :LANES], near[HD : 2 * HD, :LANES]),
                jnp.where(left, near[2 * HD : 3 * HD, LANES:], near[3 * HD : 4 * HD, LANES:]),
            ],
            axis=1,
        )
        return dot_nn(turned_values(0), glob_weights) + jnp.concatenate(
            [own, near[QUAD * HD :]], axis=0
        )

    for load in loads:
        load.wait()

    def run(exact):
        sums = []
        glob = full_rows(exact)
        if carried and not exact:
            ids_copy.wait()
        if not mixed:
            for quad in range(global_quads):
                write(quad, glob[quad], sums)
        first = 0 if mixed else global_quads
        ahead = 1 if exact else AHEAD
        ready = [near_scores(quad) for quad in range(first, min(first + ahead, quads))]
        for quad in range(first, quads):
            if quad + ahead < quads:
                ready.append(near_scores(quad + ahead))
            acc = near_finish(exact, *ready[quad - first])
            if quad < global_quads:
                column = lax.broadcasted_iota(jnp.int32, (1, QUAD * B), 1) // B
                own = functools.reduce(
                    jnp.logical_or,
                    [
                        (column == b) & (block_of(p) < GBLOCKS)
                        for b, p in enumerate(places[quad])
                    ],
                )
                acc = jnp.where(own, glob[quad], acc)
            write(quad, acc, sums)
        for store in stores:
            store.wait()
        return jnp.concatenate(sums, axis=0)

    sums = run(False)
    bad = jnp.where((sums >= least_sum) & (sums <= most_sum), 0.0, 1.0)

    @pl.when(jnp.max(bad) > 0.0)
    def _():
        run(True)


def attention(operands, plan, per, sources, limit):
    rows, blocks_dev, _, places = plan[:4]
    quads = len(places)
    carried, within = plan[6:]
    size = operands[1].shape if carried else operands[0].shape[1:]
    total = sources * rows
    pairs = QUAD * B * (quads * (G + NEAR * B) + total)
    id_rows = sources * ID_ROWS if carried else quads * QUAD
    hbm = pl.BlockSpec(memory_space=pltpu.HBM)
    shape = (quads // per, 2, HD, per * LANES)
    query_shape = (8, LANES) if within else operands[-1 if carried else 1].shape
    specs = [hbm] * len(operands)
    if carried:
        specs[0] = pl.BlockSpec(memory_space=pltpu.SMEM)
    return pl.pallas_call(
        functools.partial(attend, plan),
        in_specs=specs,
        out_specs=hbm,
        out_shape=jax.ShapeDtypeStruct(shape, jnp.bfloat16),
        scratch_shapes=[
            pltpu.VMEM(query_shape, jnp.bfloat16),
            pltpu.VMEM((sources,) + size, jnp.bfloat16),
            pltpu.VMEM((sources, rows, LANES), jnp.bfloat16),
            pltpu.VMEM((total // B, HD, LANES), jnp.bfloat16),
            pltpu.VMEM(shape, jnp.bfloat16),
            pltpu.VMEM((id_rows, LANES), jnp.int32),
            pltpu.SMEM((id_rows, LANES), jnp.int32),
            pltpu.SemaphoreType.DMA((sources + 2 + quads // per,)),
        ],
        compiler_params=pltpu.CompilerParams(vmem_limit_bytes=limit),
        cost_estimate=pl.CostEstimate(
            flops=16 * HD * pairs, bytes_accessed=4 << 20, transcendentals=pairs
        ),
        name="attend",
    )(*operands)


def project_out(head_count, own_ref, turned_ref, here_ref, there_ref, *refs):
    out_ref = refs[-1]
    axis = turned_ref.shape[0] // head_count
    total = None
    for weight_ref, at in ((here_ref, own_ref[0]), (there_ref, 1 - own_ref[0])):
        heads = [turned_ref[h * axis + at] for h in range(head_count)]
        value = lax.dot_general(
            jnp.concatenate(heads, axis=0),
            weight_ref[...],
            (((0,), (0,)), ((), ())),
            preferred_element_type=jnp.float32,
        )
        total = value if total is None else total + value
    out_ref[...] = total.astype(jnp.bfloat16)


def output_rows(turned, here, there, head_count, chunk, chunks, before):
    rows = turned.shape[2]
    width = here.shape[1]
    return pl.pallas_call(
        functools.partial(project_out, head_count),
        grid_spec=pltpu.PrefetchScalarGridSpec(
            num_scalar_prefetch=1,
            grid=(1,),
            in_specs=[
                pl.BlockSpec(turned.shape, lambda i, _: (0, 0, 0)),
                pl.BlockSpec(here.shape, lambda i, _: (0, 0)),
                pl.BlockSpec(there.shape, lambda i, _: (0, 0)),
            ]
            + [pl.BlockSpec(memory_space=pl.ANY)] * len(before),
            out_specs=pl.BlockSpec((rows, width), lambda i, _: (chunk, 0)),
        ),
        out_shape=jax.ShapeDtypeStruct((rows * chunks, width), jnp.bfloat16),
        input_output_aliases={4: 0} if before else {},
        compiler_params=pltpu.CompilerParams(vmem_limit_bytes=20 * MIB),
        cost_estimate=pl.CostEstimate(
            flops=4 * rows * width * here.shape[0], bytes_accessed=3 << 20, transcendentals=0
        ),
        name="project_out",
    )(lax.axis_index("head").reshape(1), turned, here, there, *before)


def shards(history, qkv_weight, out_weight, rand_blocks):
    tok_rows = history.shape[0]
    head_count = qkv_weight.shape[2] // HD
    seq_count = lax.axis_size("seq")
    blocks_dev = tok_rows // B
    total_blocks = blocks_dev * seq_count
    group_count = seq_count // head_count
    seq_at = lax.axis_index("seq")
    direct = group_count == 1 and lax.axis_size("head") == 2
    chunks = 2 if direct else 1
    place = seq_at if direct else jnp.zeros((), jnp.int32)
    first, later = project(history, qkv_weight, rand_blocks, place, chunks)
    half = tok_rows // 2 // chunks

    if direct:
        pieces = list(first)
        for k in sorted(range(1, seq_count), key=lambda k: abs(2 * k - seq_count)):
            pairs = [(i, (i + k) % seq_count) for i in range(seq_count)]
            pieces[k] = lax.ppermute(first[k], "seq", pairs)
        there = lax.ppermute(out_weight, "head", [(0, 1), (1, 0)])
        pieces, there, later = lax.optimization_barrier((pieces, there, later))
        place = place.reshape(1)
        per = half // (2 * B)
        outs = []
        for chunk in range(chunks):
            operands = [place] + pieces
            if chunk > 0:
                query = lax.all_to_all(later[chunk - 1], "seq", 0, 0, tiled=True)
                query, outs[-1] = lax.optimization_barrier((query, outs[-1]))
                operands.append(query)
            places = [
                [
                    (
                        n // per,
                        x * (blocks_dev // 2) + chunk * 2 * per + 2 * (n % per) + i,
                    )
                    for i in range(2)
                    for x in range(2)
                ]
                for n in range(seq_count * per)
            ]
            plan = (tok_rows, blocks_dev, total_blocks, places, per, False, True, chunk == 0)
            out = attention(operands, plan, per, seq_count, 64 * MIB - 400 * 1024)
            outs.append(out.reshape(2 * seq_count, HD, half))
        outs = [lax.all_to_all(out, ("seq", "head"), 0, 0, tiled=True) for out in outs]
        result = []
        for chunk in range(chunks):
            operands = (outs[chunk], out_weight, there)
            result = [output_rows(*operands, head_count, chunk, chunks, result)]
        return result[0]

    first = jnp.stack(first)
    key_value = lax.all_gather(first[:, :tok_rows], "seq")
    key_value = lax.dynamic_index_in_dim(key_value, seq_at // group_count, 1, False)
    group_blocks = blocks_dev // group_count
    blocks = seq_count * group_blocks
    query = first[:, tok_rows : tok_rows + half]
    query = query.reshape(head_count, half, 2, HD).transpose(0, 2, 1, 3)
    query = lax.all_to_all(query.reshape(seq_count, -1, HD), "seq", 0, 0, tiled=True)
    query = query.reshape(blocks // QUAD, 2, 2, B, HD).transpose(0, 1, 3, 2, 4)
    query = query.reshape(blocks // QUAD, 2 * B, LANES)
    ids = rand_blocks.reshape(seq_count, group_blocks, R)
    ids = lax.all_to_all(ids, "seq", 0, 0, tiled=True).reshape(blocks, R)
    ids = jnp.pad(ids, ((0, 0), (0, LANES - R)))
    offset = seq_at % group_count * group_blocks
    ids = ids.at[:, LANES - 1].set(offset)
    places = [
        [((n * QUAD + b) // group_blocks, (n * QUAD + b) % group_blocks) for b in range(QUAD)]
        for n in range(blocks // QUAD)
    ]
    global_quads = -(-GBLOCKS // group_count // QUAD)
    plan = (tok_rows, blocks_dev, total_blocks, places, global_quads, True, False, False)
    out = attention([key_value, query, ids], plan, 1, seq_count, 56 * MIB)
    out = out.reshape(blocks // QUAD, 2, HD, 2, B).transpose(0, 3, 1, 4, 2)
    out = lax.all_to_all(out.reshape(seq_count, -1, HD), "seq", 0, 0, tiled=True)
    attn = out.reshape(head_count, tok_rows, HD).transpose(1, 0, 2)
    return lax.psum_scatter(
        jnp.dot(
            attn.reshape(tok_rows, head_count * HD),
            out_weight,
            preferred_element_type=jnp.float32,
        ).astype(jnp.bfloat16),
        "head",
        scatter_dimension=0,
        tiled=True,
    )


def solution(mesh):
    placed = (
        P(("groups", "seq"), None),
        P(None, None, "head"),
        P("head", None),
        P("head", ("groups", "seq"), None),
    )
    return jax.shard_map(
        shards,
        mesh=mesh,
        in_specs=placed,
        out_specs=P(("groups", "seq", "head"), None),
        check_vma=False,
    )
```

```python
import functools
import math

import jax
import jax.numpy as jnp
from jax import lax
from jax.experimental import pallas as pl
from jax.experimental.pallas import tpu as pltpu
from jax.sharding import PartitionSpec as P

B = 64
R = 3
G = 1024
HD = 64
GBLOCKS = 16
LANES = 2 * HD
QUAD = 4
NEAR = 3 + R
SUM_ROWS = 16
ID_BASE = 256
ID_ROWS = 16
MIB = 1024 * 1024

AHEAD = 3

masked_score = -1e30
least_sum, most_sum = 1e-25, 1e30


def dot_nt(a, b):
    return lax.dot_general(a, b, (((1,), (1,)), ((), ())), preferred_element_type=jnp.float32)


def dot_nn(a, b):
    return jnp.dot(a, b, preferred_element_type=jnp.float32)


def left_half(rows):
    return lax.broadcasted_iota(jnp.int32, (rows, LANES), 1) < HD


def swap_halves(value):
    return jnp.concatenate([value[:, HD:], value[:, :HD]], axis=1)


def pair_rows(value):
    half = value.shape[0] // 2
    left = left_half(half)
    top, low = value[:half], value[half:]
    return jnp.where(left, top, swap_halves(low)), jnp.where(left, swap_halves(top), low)


def project_first(half, place_ref, history_hbm, weight_hbm, ids_ref, *refs):
    *outs, history_ref, weight_ref, out_ref, sems = refs
    rows = history_ref.shape[0]
    heads = out_ref.shape[0]
    step = min(4, heads)
    runs = heads // step
    width = step * HD
    loads = [pltpu.make_async_copy(history_hbm, history_ref, sems.at[0])]
    for run in range(runs):
        at = (slice(None), slice(None), pl.ds(run * width, width))
        loads.append(
            pltpu.make_async_copy(weight_hbm.at[at], weight_ref.at[at], sems.at[1 + run])
        )
    for load in loads:
        load.start()
    for head in range(heads):
        out_ref[head, rows + half :] = jnp.zeros((ID_ROWS, LANES), jnp.bfloat16)
        ids = [ids_ref[r, head : head + 1] for r in range(R)]
        ids = [v % ID_BASE for v in ids] + [v // ID_BASE for v in ids]
        ids.append(jnp.zeros((ID_ROWS - 2 * R, ids_ref.shape[2]), jnp.int32))
        ids = jnp.concatenate(ids, axis=0).astype(jnp.float32).astype(jnp.bfloat16)
        out_ref[head, rows + half :, : ids.shape[1]] = ids

    def product(unit):
        run, kind = unit
        lanes = slice(run * width, (run + 1) * width)
        if kind == 0:
            return dot_nn(history_ref[...], weight_ref[1, :, lanes])
        if kind == 1:
            return lax.dot_general(
                weight_ref[2, :, lanes],
                history_ref[...],
                (((0,), (1,)), ((), ())),
                preferred_element_type=jnp.float32,
            )
        return project_half(history_ref, weight_ref[0, :, lanes], 0, half)

    def place(unit, value):
        run, kind = unit
        value = value.astype(jnp.bfloat16)
        for head in range(run * step, (run + 1) * step):
            j = head - run * step
            if kind == 1:
                for i in range(rows // LANES):
                    tile = value[j * HD : (j + 1) * HD, i * LANES : (i + 1) * LANES]
                    out_ref[head, rows // 2 + i * HD : rows // 2 + (i + 1) * HD] = tile
            elif j % 2 == 0:
                pair = pair_rows(value[:, j * HD : (j + 2) * HD])
                at = 0 if kind == 0 else rows
                for k in range(2):
                    out_ref[head + k, at : at + pair[k].shape[0]] = pair[k]

    def store(k):
        head = lax.rem(place_ref[0] + k, heads)
        return pltpu.make_async_copy(out_ref.at[head], outs[k], sems.at[1 + runs + k])

    units = [(run, kind) for run in range(runs) for kind in range(3)]
    for load in loads[:2]:
        load.wait()
    value = product(units[0])
    for n, unit in enumerate(units):
        later = None
        if n + 1 < len(units):
            if units[n + 1][0] > unit[0]:
                loads[1 + units[n + 1][0]].wait()
            later = product(units[n + 1])
        place(unit, value)
        value = later
        if unit[1] == 2:
            for k in range(heads):
                head = lax.rem(place_ref[0] + k, heads)

                @pl.when(head // step == unit[0])
                def _():
                    store(k).start()

    for k in range(heads):
        store(k).wait()


def project_half(history_ref, weight, first, half):
    middle = history_ref.shape[0] // 2
    chosen = jnp.concatenate(
        [
            history_ref[first : first + half],
            history_ref[middle + first : middle + first + half],
        ],
        axis=0,
    )
    return dot_nn(chosen, weight) * (1.0 / math.sqrt(HD))


def project_later(first, history_ref, weight_ref, out_ref):
    half = out_ref.shape[1]
    query = project_half(history_ref, weight_ref[0], first, half).astype(jnp.bfloat16)
    for j in range(0, out_ref.shape[0], 2):
        pair = pair_rows(query[:, j * HD : (j + 2) * HD])
        out_ref[j] = pair[0]
        out_ref[j + 1] = pair[1]


def project(history, qkv_weight, ids, place, chunks):
    rows, width = history.shape
    heads = qkv_weight.shape[2] // HD
    half = rows // 2 // chunks
    total = rows + half + ID_ROWS
    whole = pl.BlockSpec((rows, width), lambda i: (0, 0))
    params = pltpu.CompilerParams(vmem_limit_bytes=56 * MIB)
    first = pl.pallas_call(
        functools.partial(project_first, half),
        in_specs=[
            pl.BlockSpec(memory_space=pltpu.SMEM),
            pl.BlockSpec(memory_space=pltpu.HBM),
            pl.BlockSpec(memory_space=pltpu.HBM),
            pl.BlockSpec(memory_space=pltpu.VMEM),
        ],
        out_specs=[pl.BlockSpec(memory_space=pltpu.HBM)] * heads,
        out_shape=[jax.ShapeDtypeStruct((total, LANES), jnp.bfloat16)] * heads,
        scratch_shapes=[
            pltpu.VMEM(history.shape, jnp.bfloat16),
            pltpu.VMEM(qkv_weight.shape, jnp.bfloat16),
            pltpu.VMEM((heads, total, LANES), jnp.bfloat16),
            pltpu.SemaphoreType.DMA((1 + 2 * heads,)),
        ],
        compiler_params=params,
        cost_estimate=pl.CostEstimate(
            flops=5 * rows * width * heads * HD, bytes_accessed=6 << 20, transcendentals=0
        ),
        name="project_first",
    )(place.reshape(1), history, qkv_weight, ids.transpose(2, 0, 1))
    later = []
    step = min(4, heads)
    for chunk in range(1, chunks):
        history, first = lax.optimization_barrier((history, first))
        later.append(
            pl.pallas_call(
                functools.partial(project_later, chunk * half),
                grid=(heads // step,),
                in_specs=[whole, pl.BlockSpec((1, width, step * HD), lambda i: (0, 0, i))],
                out_specs=pl.BlockSpec((step, half, LANES), lambda i: (i, 0, 0)),
                out_shape=jax.ShapeDtypeStruct((heads, half, LANES), jnp.bfloat16),
                compiler_params=params,
                cost_estimate=pl.CostEstimate(
                    flops=4 * half * width * heads * HD, bytes_accessed=4 << 20, transcendentals=0
                ),
                name="project_later",
            )(history, qkv_weight)
        )
    return first, later


def attend(plan, *refs):
    rows, blocks_dev, total_blocks, places, global_quads, mixed, carried, within = plan
    kv_ref, keys_ref, values_ref, turned_ref, ids_vmem, ids_ref, sems = refs[-7:]
    out_hbm, query_ref = refs[-9:-7]
    sources = kv_ref.shape[0]
    half = rows // 2
    quads = len(places)
    group_blocks = blocks_dev if carried else quads * QUAD // sources
    per = turned_ref.shape[3] // LANES
    pairs = rows // LANES
    left = left_half(B)
    zero = jnp.zeros((B, LANES), jnp.bfloat16)
    if carried:
        place_ref, *pieces = refs[: 1 + sources]
        loads = [
            pltpu.make_async_copy(
                piece, kv_ref.at[lax.rem(place_ref[0] + sources - k, sources)], sems.at[k]
            )
            for k, piece in enumerate(pieces)
        ]
        ids_copy = pltpu.make_async_copy(ids_vmem, ids_ref, sems.at[sources + 1])
    else:
        loads = [pltpu.make_async_copy(refs[0], kv_ref, sems.at[0])]
        ids_copy = pltpu.make_async_copy(refs[2], ids_ref, sems.at[sources + 1])
        loads.append(ids_copy)
    if not within:
        query_hbm = refs[1 + sources] if carried else refs[1]
        loads.append(pltpu.make_async_copy(query_hbm, query_ref, sems.at[sources]))
    for load in loads:
        load.start()
    stores = [
        pltpu.make_async_copy(
            turned_ref.at[pl.ds(i, 1)], out_hbm.at[pl.ds(i, 1)], sems.at[sources + 2 + i]
        )
        for i in range(quads // per)
    ]

    def spread_ids():
        end = kv_ref.shape[1]
        for source in range(sources):
            ids_vmem[source * ID_ROWS : (source + 1) * ID_ROWS] = (
                kv_ref[source, end - ID_ROWS :].astype(jnp.float32).astype(jnp.int32)
            )
        ids_copy.start()

    def rand_of(source, local):
        if carried:
            at = source * ID_ROWS
            return [
                ids_ref[at + r, local] + ids_ref[at + R + r, local] * ID_BASE for r in range(R)
            ]
        return [ids_ref[source * group_blocks + local, r] for r in range(R)]

    def build(source):
        packed = kv_ref[source, :half]
        wide = left_half(half)
        other = swap_halves(packed)
        keys_ref[source, :half] = jnp.where(wide, packed, other)
        keys_ref[source, half:] = jnp.where(wide, other, packed)
        for i in range(pairs):
            tile = kv_ref[source, half + i * HD : half + (i + 1) * HD]
            turned = swap_halves(tile)
            values_ref[source * 2 * pairs + 2 * i] = jnp.where(left, tile, turned)
            values_ref[source * 2 * pairs + 2 * i + 1] = jnp.where(left, turned, tile)

    def turned_values(source):
        tiles = [kv_ref[source, half + i * HD : half + (i + 1) * HD] for i in range(pairs)]
        ones = jnp.ones((SUM_ROWS, rows), jnp.bfloat16)
        return jnp.concatenate([jnp.concatenate(tiles, axis=1), ones], axis=0)

    def queries_of(quad):
        parts = []
        for i in range(2):
            if within:
                at = rows + (quad % per * 2 + i) * B
                packed = kv_ref[quad // per, at : at + B]
            else:
                at = (quad % per * 2 + i) * B
                packed = query_ref[quad // per, at : at + B]
            parts.append(jnp.where(left, packed, zero))
            parts.append(jnp.where(left, zero, packed))
        return parts

    def write(quad, acc, sums):
        total = acc[HD : HD + 1]
        sums.append(total)
        value = acc[:HD] / total
        first, second = value[:, :LANES], value[:, LANES:]
        at = slice(quad % per * LANES, (quad % per + 1) * LANES)
        turned_ref[quad // per, 0, :, at] = jnp.where(left, first, swap_halves(second)).astype(
            jnp.bfloat16
        )
        turned_ref[quad // per, 1, :, at] = jnp.where(left, swap_halves(first), second).astype(
            jnp.bfloat16
        )
        if quad % per == per - 1:
            stores[quad // per].start()

    def full_rows(exact):
        query = jnp.concatenate([p for n in range(global_quads) for p in queries_of(n)], axis=0)

        def score(source):
            return dot_nt(keys_ref[source], query)

        def fold(source, scores, carry):
            top, acc = carry
            if exact:
                new_top = jnp.maximum(top, jnp.max(scores, 0, keepdims=True))
                acc = acc * jnp.exp(top - new_top)
                top = new_top
                scores = scores - top
            weights = jnp.exp(scores).astype(jnp.bfloat16)
            return top, acc + dot_nn(turned_values(source), weights)

        carry = (
            jnp.full((1, query.shape[0]), -jnp.inf, jnp.float32),
            jnp.zeros((HD + SUM_ROWS, query.shape[0]), jnp.float32),
        )
        if sources <= 8 and not exact:
            build(0)
            scores = score(0)
            if carried:
                spread_ids()
            for source in range(sources):
                later = None
                if source + 1 < sources:
                    build(source + 1)
                    later = score(source + 1)
                carry = fold(source, scores, carry)
                scores = later
        else:
            if not exact:
                if carried:
                    spread_ids()
                lax.fori_loop(0, sources, lambda i, _: (build(i), 0)[1], 0)
            carry = lax.fori_loop(0, sources, lambda i, c: fold(i, score(i), c), carry)
        width = QUAD * B
        return [carry[1][:, n * width : (n + 1) * width] for n in range(global_quads)]

    def block_of(place):
        source, local = place
        if carried:
            return source * blocks_dev + local
        return source * blocks_dev + ids_ref[source * group_blocks, LANES - 1] + local

    def key_block(block):
        at = block % blocks_dev if isinstance(block, int) else lax.rem(block, blocks_dev)
        source = block // blocks_dev if isinstance(block, int) else lax.div(block, blocks_dev)
        return keys_ref[source, pl.ds(at * B if isinstance(at, int) else pl.multiple_of(at * B, B), B)]

    def near_scores(quad):
        parts = queries_of(quad)
        glob_scores = dot_nt(keys_ref[0], jnp.concatenate(parts, axis=0))
        lists = []
        column = lax.broadcasted_iota(jnp.int32, (1, QUAD * B), 1) // B
        low = high = None
        for b, (source, local) in enumerate(places[quad]):
            block = block_of((source, local))
            if carried:
                window = [max(block - 1, 0), block, min(block + 1, total_blocks - 1)]
                dead_low, dead_high = block - 1 < GBLOCKS, block + 1 >= total_blocks
                if dead_low:
                    low = column == b if low is None else low | (column == b)
                if dead_high:
                    high = column == b if high is None else high | (column == b)
            else:
                window = [
                    jnp.maximum(block - 1, 0),
                    block,
                    jnp.minimum(block + 1, total_blocks - 1),
                ]
                one = (column == b) & (block - 1 < GBLOCKS)
                two = (column == b) & (block + 1 >= total_blocks)
                low = one if low is None else low | one
                high = two if high is None else high | two
            lists.append(window + rand_of(source, local))
        near_keys = []
        for b in range(0, QUAD, 2):
            tiles = [
                jnp.where(left, key_block(lists[b][k]), key_block(lists[b + 1][k]))
                for k in range(NEAR)
            ]
            near_keys.append(jnp.concatenate(tiles, axis=0))
        blank = jnp.zeros((2 * B, LANES), jnp.bfloat16)
        diagonal = jnp.concatenate(
            [
                jnp.concatenate(parts[:2] + [blank], axis=0),
                jnp.concatenate([blank] + parts[2:], axis=0),
            ],
            axis=1,
        )
        scores = dot_nt(jnp.concatenate(near_keys, axis=1), diagonal)
        if low is not None or high is not None:
            before, after = scores[:B], scores[2 * B : 3 * B]
            if low is not None:
                before = jnp.where(low, masked_score, before)
            if high is not None:
                after = jnp.where(high, masked_score, after)
            scores = jnp.concatenate([before, scores[B : 2 * B], after, scores[3 * B :]], axis=0)
        return glob_scores, scores, lists

    def near_finish(exact, glob_scores, scores, lists):
        if exact:
            top = jnp.maximum(
                jnp.max(glob_scores, 0, keepdims=True), jnp.max(scores, 0, keepdims=True)
            )
            glob_scores, scores = glob_scores - top, scores - top
        glob_weights = jnp.exp(glob_scores).astype(jnp.bfloat16)
        weights = jnp.exp(scores).astype(jnp.bfloat16)
        near_values = [
            jnp.concatenate(
                [
                    jnp.where(left, values_ref[lists[b][k]], values_ref[lists[b][k + 1]])
                    for k in range(0, NEAR, 2)
                ],
                axis=1,
            )
            for b in range(QUAD)
        ]
        near_values.append(jnp.ones((SUM_ROWS, NEAR * B), jnp.bfloat16))
        near = dot_nn(jnp.concatenate(near_values, axis=0), weights)
        own = jnp.concatenate(
            [
                jnp.where(left, near[:HD, :LANES], near[HD : 2 * HD, :LANES]),
                jnp.where(left, near[2 * HD : 3 * HD, LANES:], near[3 * HD : 4 * HD, LANES:]),
            ],
            axis=1,
        )
        return dot_nn(turned_values(0), glob_weights) + jnp.concatenate(
            [own, near[QUAD * HD :]], axis=0
        )

    for load in loads:
        load.wait()

    def run(exact):
        sums = []
        glob = full_rows(exact)
        if carried and not exact:
            ids_copy.wait()
        if not mixed:
            for quad in range(global_quads):
                write(quad, glob[quad], sums)
        first = 0 if mixed else global_quads
        ahead = 1 if exact else AHEAD
        ready = [near_scores(quad) for quad in range(first, min(first + ahead, quads))]
        for quad in range(first, quads):
            if quad + ahead < quads:
                ready.append(near_scores(quad + ahead))
            acc = near_finish(exact, *ready[quad - first])
            if quad < global_quads:
                column = lax.broadcasted_iota(jnp.int32, (1, QUAD * B), 1) // B
                own = functools.reduce(
                    jnp.logical_or,
                    [
                        (column == b) & (block_of(p) < GBLOCKS)
                        for b, p in enumerate(places[quad])
                    ],
                )
                acc = jnp.where(own, glob[quad], acc)
            write(quad, acc, sums)
        for store in stores:
            store.wait()
        return jnp.concatenate(sums, axis=0)

    sums = run(False)
    bad = jnp.where((sums >= least_sum) & (sums <= most_sum), 0.0, 1.0)

    @pl.when(jnp.max(bad) > 0.0)
    def _():
        run(True)


def attention(operands, plan, per, sources, limit):
    rows, blocks_dev, _, places = plan[:4]
    quads = len(places)
    carried, within = plan[6:]
    size = operands[1].shape if carried else operands[0].shape[1:]
    total = sources * rows
    pairs = QUAD * B * (quads * (G + NEAR * B) + total)
    id_rows = sources * ID_ROWS if carried else quads * QUAD
    hbm = pl.BlockSpec(memory_space=pltpu.HBM)
    shape = (quads // per, 2, HD, per * LANES)
    query_shape = (8, LANES) if within else operands[-1 if carried else 1].shape
    specs = [hbm] * len(operands)
    if carried:
        specs[0] = pl.BlockSpec(memory_space=pltpu.SMEM)
    return pl.pallas_call(
        functools.partial(attend, plan),
        in_specs=specs,
        out_specs=hbm,
        out_shape=jax.ShapeDtypeStruct(shape, jnp.bfloat16),
        scratch_shapes=[
            pltpu.VMEM(query_shape, jnp.bfloat16),
            pltpu.VMEM((sources,) + size, jnp.bfloat16),
            pltpu.VMEM((sources, rows, LANES), jnp.bfloat16),
            pltpu.VMEM((total // B, HD, LANES), jnp.bfloat16),
            pltpu.VMEM(shape, jnp.bfloat16),
            pltpu.VMEM((id_rows, LANES), jnp.int32),
            pltpu.SMEM((id_rows, LANES), jnp.int32),
            pltpu.SemaphoreType.DMA((sources + 2 + quads // per,)),
        ],
        compiler_params=pltpu.CompilerParams(vmem_limit_bytes=limit),
        cost_estimate=pl.CostEstimate(
            flops=16 * HD * pairs, bytes_accessed=4 << 20, transcendentals=pairs
        ),
        name="attend",
    )(*operands)


def project_out(head_count, own_ref, turned_ref, here_ref, there_ref, *refs):
    out_ref = refs[-1]
    axis = turned_ref.shape[0] // head_count
    total = None
    for weight_ref, at in ((here_ref, own_ref[0]), (there_ref, 1 - own_ref[0])):
        heads = [turned_ref[h * axis + at] for h in range(head_count)]
        value = lax.dot_general(
            jnp.concatenate(heads, axis=0),
            weight_ref[...],
            (((0,), (0,)), ((), ())),
            preferred_element_type=jnp.float32,
        )
        total = value if total is None else total + value
    out_ref[...] = total.astype(jnp.bfloat16)


def output_rows(turned, here, there, head_count, chunk, chunks, before):
    rows = turned.shape[2]
    width = here.shape[1]
    return pl.pallas_call(
        functools.partial(project_out, head_count),
        grid_spec=pltpu.PrefetchScalarGridSpec(
            num_scalar_prefetch=1,
            grid=(1,),
            in_specs=[
                pl.BlockSpec(turned.shape, lambda i, _: (0, 0, 0)),
                pl.BlockSpec(here.shape, lambda i, _: (0, 0)),
                pl.BlockSpec(there.shape, lambda i, _: (0, 0)),
            ]
            + [pl.BlockSpec(memory_space=pl.ANY)] * len(before),
            out_specs=pl.BlockSpec((rows, width), lambda i, _: (chunk, 0)),
        ),
        out_shape=jax.ShapeDtypeStruct((rows * chunks, width), jnp.bfloat16),
        input_output_aliases={4: 0} if before else {},
        compiler_params=pltpu.CompilerParams(vmem_limit_bytes=20 * MIB),
        cost_estimate=pl.CostEstimate(
            flops=4 * rows * width * here.shape[0], bytes_accessed=3 << 20, transcendentals=0
        ),
        name="project_out",
    )(lax.axis_index("head").reshape(1), turned, here, there, *before)


def shards(history, qkv_weight, out_weight, rand_blocks):
    tok_rows = history.shape[0]
    head_count = qkv_weight.shape[2] // HD
    seq_count = lax.axis_size("seq")
    blocks_dev = tok_rows // B
    total_blocks = blocks_dev * seq_count
    group_count = seq_count // head_count
    seq_at = lax.axis_index("seq")
    direct = group_count == 1 and lax.axis_size("head") == 2
    chunks = 2 if direct else 1
    place = seq_at if direct else jnp.zeros((), jnp.int32)
    first, later = project(history, qkv_weight, rand_blocks, place, chunks)
    half = tok_rows // 2 // chunks

    if direct:
        pieces = list(first)
        for k in sorted(range(1, seq_count), key=lambda k: abs(2 * k - seq_count)):
            pairs = [(i, (i + k) % seq_count) for i in range(seq_count)]
            pieces[k] = lax.ppermute(first[k], "seq", pairs)
        there = lax.ppermute(out_weight, "head", [(0, 1), (1, 0)])
        pieces, there, later = lax.optimization_barrier((pieces, there, later))
        place = place.reshape(1)
        per = half // (2 * B)
        outs = []
        for chunk in range(chunks):
            operands = [place] + pieces
            if chunk > 0:
                query = lax.all_to_all(later[chunk - 1], "seq", 0, 0, tiled=True)
                query, outs[-1] = lax.optimization_barrier((query, outs[-1]))
                operands.append(query)
            places = [
                [
                    (
                        n // per,
                        x * (blocks_dev // 2) + chunk * 2 * per + 2 * (n % per) + i,
                    )
                    for i in range(2)
                    for x in range(2)
                ]
                for n in range(seq_count * per)
            ]
            plan = (tok_rows, blocks_dev, total_blocks, places, per, False, True, chunk == 0)
            out = attention(operands, plan, per, seq_count, 64 * MIB - 400 * 1024)
            outs.append(out.reshape(2 * seq_count, HD, half))
        outs = [lax.all_to_all(out, ("seq", "head"), 0, 0, tiled=True) for out in outs]
        result = []
        for chunk in range(chunks):
            operands = (outs[chunk], out_weight, there)
            result = [output_rows(*operands, head_count, chunk, chunks, result)]
        return result[0]

    first = jnp.stack(first)
    key_value = lax.all_gather(first[:, :tok_rows], "seq")
    key_value = lax.dynamic_index_in_dim(key_value, seq_at // group_count, 1, False)
    group_blocks = blocks_dev // group_count
    blocks = seq_count * group_blocks
    query = first[:, tok_rows : tok_rows + half]
    query = query.reshape(head_count, half, 2, HD).transpose(0, 2, 1, 3)
    query = lax.all_to_all(query.reshape(seq_count, -1, HD), "seq", 0, 0, tiled=True)
    query = query.reshape(blocks // QUAD, 2, 2, B, HD).transpose(0, 1, 3, 2, 4)
    query = query.reshape(blocks // QUAD, 2 * B, LANES)
    ids = rand_blocks.reshape(seq_count, group_blocks, R)
    ids = lax.all_to_all(ids, "seq", 0, 0, tiled=True).reshape(blocks, R)
    ids = jnp.pad(ids, ((0, 0), (0, LANES - R)))
    offset = seq_at % group_count * group_blocks
    ids = ids.at[:, LANES - 1].set(offset)
    places = [
        [((n * QUAD + b) // group_blocks, (n * QUAD + b) % group_blocks) for b in range(QUAD)]
        for n in range(blocks // QUAD)
    ]
    global_quads = -(-GBLOCKS // group_count // QUAD)
    plan = (tok_rows, blocks_dev, total_blocks, places, global_quads, True, False, False)
    out = attention([key_value, query, ids], plan, 1, seq_count, 56 * MIB)
    out = out.reshape(blocks // QUAD, 2, HD, 2, B).transpose(0, 3, 1, 4, 2)
    out = lax.all_to_all(out.reshape(seq_count, -1, HD), "seq", 0, 0, tiled=True)
    attn = out.reshape(head_count, tok_rows, HD).transpose(1, 0, 2)
    return lax.psum_scatter(
        jnp.dot(
            attn.reshape(tok_rows, head_count * HD),
            out_weight,
            preferred_element_type=jnp.float32,
        ).astype(jnp.bfloat16),
        "head",
        scatter_dimension=0,
        tiled=True,
    )


def solution(mesh):
    placed = (
        P(("groups", "seq"), None),
        P(None, None, "head"),
        P("head", None),
        P("head", ("groups", "seq"), None),
    )
    return jax.shard_map(
        shards,
        mesh=mesh,
        in_specs=placed,
        out_specs=P(("groups", "seq", "head"), None),
        check_vma=False,
    )
```
